256 devices in a mesh: theta: 128 (over x, y_hi, z, core), rad: 2 (over y_lo).
Axes of the slice: x: 4, y: 4 (y_hi: 2, y_lo: 2; y = y_hi * 2 + y_lo), z: 8, core: 2. Of those that a mesh axis runs over, the one named last changes fastest.
Arguments:
- q_level: float32 [5, 32, 1024, 256], P(None, 'rad', 'theta'), as said below
- q_prev: float32 [5, 32, 1024, 256], P(None, 'rad', 'theta'), as said below
- blade_row: int32 [256], replicated, may hold values from 0 to 2, as said below
Outputs:
- flow_state: float32 [5, 32, 1024, 256], P(None, 'rad', 'theta')
- spectra: float32 [256, 32, 256], P('theta', 'rad')
The draws below stay inside these ranges and needn't reach their ends.
Inputs may be any that keep to these rules, and one draw needn't show every extreme that they name: q_level holds conserved variables of a state whose density lies within 0.8 to 1.25, pressure within 0.55 to 0.9, axial velocity within 0.05 to 0.95, radial velocity within -0.3 to 0.3 and swirl velocity within -0.6 to 0.6. q_prev holds conserved variables of a state within the same bounds as q_level. `blade_row`: 0 marks a gap, 1 the rotor, 2 a stator; along the axial stations the rows come in contiguous runs: gap, stator, gap, rotor, gap, stator, gap.
All inputs are finite; a program needn't handle non-finite values.
Results may differ from the reference program's by a relative error of at most 0.0003.
Values sent between devices are 32-bit elements; how exact they have to be, the bound alone decides.
No kernel may reach another device: no remote copies, remote signals or barrier semaphores. Data moves between devices by JAX's collectives and lax.ppermute only.
A program may use at most 64 MiB of HBM per device.

```python
import math
import jax
import jax.numpy as jnp
from jax import lax

NA = 256
MODES = 64
NT = 1024
NR = 32


def build_state(key):
    keys = jax.random.split(key, 5)
    shape = (NR, NT, NA)
    density = jnp.exp(jax.random.uniform(keys[0], shape, jnp.float32, math.log(0.8), math.log(1.25)))
    axial_speed = jnp.clip(0.5 + 0.15 * jax.random.normal(keys[1], shape, jnp.float32), 0.05, 0.95)
    radial_speed = jnp.clip(0.1 * jax.random.normal(keys[2], shape, jnp.float32), -0.3, 0.3)
    swirl_speed = jnp.clip(0.25 * jax.random.normal(keys[3], shape, jnp.float32), -0.6, 0.6)
    pressure = jax.random.uniform(keys[4], shape, jnp.float32, 0.55, 0.9)
    energy = pressure / 0.4 + 0.5 * density * (axial_speed * axial_speed + radial_speed * radial_speed + swirl_speed * swirl_speed)
    return jnp.stack([density, density * axial_speed, density * radial_speed, density * swirl_speed, energy])


def draw_q_level(key, part):
    return build_state(jax.random.fold_in(key, 11))


def draw_q_prev(key, part):
    return build_state(jax.random.fold_in(key, 23))


def draw_blade_row(key, part):
    spacing = NA // 7
    jitter = jax.random.randint(key, (6,), 0, max(spacing // 2, 1), dtype=jnp.int32)
    cuts = jnp.arange(1, 7, dtype=jnp.int32) * spacing + jitter
    stations = jnp.arange(NA, dtype=jnp.int32)
    segment = jnp.sum((stations[:, None] >= cuts[None, :]).astype(jnp.int32), axis=1)
    kinds = jnp.array([0, 2, 0, 1, 0, 2, 0], dtype=jnp.int32)
    return kinds[segment]


def setup_inputs(seed: int = 0) -> dict:
    key_list = jax.random.split(jax.random.key(seed), 4)
    q_level = draw_q_level(jax.random.fold_in(key_list[3], 71), 0)
    q_prev = draw_q_prev(jax.random.fold_in(key_list[3], 71), 0)
    blade_row = draw_blade_row(jax.random.fold_in(key_list[3], 71), 0)
    return {"q_level": q_level, "q_prev": q_prev, "blade_row": blade_row}


GAMMA = 1.4
CFL = 0.5
DT_PHYS = 0.1
KAPPA = 2.0

def take_range(values, along, first_index, stop_index):
    return lax.slice_in_dim(values, first_index, stop_index, axis=along)

def primitive_of(flow):
    density = flow[0]
    axial_speed = flow[1] / density
    radial_speed = flow[2] / density
    swirl_speed = flow[3] / density
    kinetic = 0.5 * (flow[1] * axial_speed + flow[2] * radial_speed + flow[3] * swirl_speed)
    pressure = (GAMMA - 1.0) * (flow[4] - kinetic)
    sound_speed = jnp.sqrt(GAMMA * pressure / density)
    return jnp.stack([axial_speed, radial_speed, swirl_speed, pressure, sound_speed])

def face_flux(flow, primitive, component, along):
    normal = primitive[component - 1]
    flux_term = flow * normal[None]
    flux_term = flux_term.at[component].add(primitive[3])
    flux_term = flux_term.at[4].add(primitive[3] * normal)
    wave_speed = jnp.abs(normal) + primitive[4]
    length = flow.shape[along]
    left_flow = take_range(flow, along, 0, length - 1)
    right_flow = take_range(flow, along, 1, length)
    mean_flux = 0.5 * (take_range(flux_term, along, 0, length - 1) + take_range(flux_term, along, 1, length))
    fastest = jnp.maximum(take_range(wave_speed, along - 1, 0, length - 1), take_range(wave_speed, along - 1, 1, length))
    return mean_flux - 0.5 * fastest[None] * (right_flow - left_flow)

def geometry(total_rows, circle_cells, first_row, band_rows):
    mean_radius = circle_cells / (2.0 * math.pi)
    row_index = jnp.arange(band_rows, dtype=jnp.float32) + jnp.asarray(first_row).astype(jnp.float32)
    radius = mean_radius * (0.8 + 0.4 * (row_index + 0.5) / total_rows)
    inner_face = mean_radius * (0.8 + 0.4 * row_index / total_rows)
    outer_face = mean_radius * (0.8 + 0.4 * (row_index + 1.0) / total_rows)
    theta_step = 2.0 * math.pi / circle_cells
    spin_rate = 1.0 / (1.2 * mean_radius)
    return (radius, inner_face, outer_face, theta_step, spin_rate)

def pseudo_step(extended, source, radius, inner_face, outer_face, theta_step, spin_rate, rotor_frame, bladed):
    primitive = primitive_of(extended)
    center = extended[:, 1:-1, 1:-1, :]
    center_prim = primitive[:, 1:-1, 1:-1, :]
    axial_flow = jnp.concatenate([center[..., :1], center, center[..., -1:]], axis=3)
    axial_prim = jnp.concatenate([center_prim[..., :1], center_prim, center_prim[..., -1:]], axis=3)
    axial_faces = face_flux(axial_flow, axial_prim, 1, 3)
    radial_faces = face_flux(extended[:, :, 1:-1, :], primitive[:, :, 1:-1, :], 2, 1)
    circ_faces = face_flux(extended[:, 1:-1], primitive[:, 1:-1], 3, 2)
    radius_col = radius[:, None, None]
    spacing = radius_col * theta_step
    divergence = axial_faces[..., 1:] - axial_faces[..., :-1]
    divergence = divergence + (outer_face[:, None, None] * radial_faces[:, 1:] - inner_face[:, None, None] * radial_faces[:, :-1]) / radius_col
    divergence = divergence + (circ_faces[:, :, 1:] - circ_faces[:, :, :-1]) / spacing
    density = center[0]
    axial_speed = center_prim[0]
    radial_speed = center_prim[1]
    swirl_speed = center_prim[2]
    pressure = center_prim[3]
    sound_speed = center_prim[4]
    blade_force = -KAPPA * bladed * density * (swirl_speed - rotor_frame * spin_rate * radius_col)
    zeros_field = jnp.zeros_like(density)
    sources = jnp.stack([zeros_field, zeros_field, (density * swirl_speed * swirl_speed + pressure) / radius_col, blade_force - density * radial_speed * swirl_speed / radius_col, swirl_speed * blade_force])
    pseudo_dt = CFL / (jnp.abs(axial_speed) + jnp.abs(radial_speed) + jnp.abs(swirl_speed) / spacing + sound_speed * (2.0 + 1.0 / spacing))
    return (center + pseudo_dt[None] * (source - divergence + sources)) / (1.0 + 1.5 * pseudo_dt[None] / DT_PHYS)

def reflect_rows(rows):
    return rows * jnp.array([1.0, 1.0, -1.0, 1.0, 1.0], dtype=rows.dtype)[:, None, None, None]

def pad_grid(flow):
    wrapped_rows = jnp.concatenate([flow[:, :, -1:], flow, flow[:, :, :1]], axis=2)
    return jnp.concatenate([reflect_rows(wrapped_rows[:, :1]), wrapped_rows, reflect_rows(wrapped_rows[:, -1:])], axis=1)

def field_pair(flow):
    density = flow[0]
    kinetic = 0.5 * (flow[1] * flow[1] + flow[2] * flow[2] + flow[3] * flow[3]) / density
    pressure = (GAMMA - 1.0) * (flow[4] - kinetic)
    return jnp.stack([pressure, flow[1] / density])

def mode_basis(circle_cells):
    cells = jnp.arange(circle_cells, dtype=jnp.int32)
    orders = jnp.arange(1, MODES + 1, dtype=jnp.int32)
    phase = (cells[:, None] * orders[None, :] % circle_cells).astype(jnp.float32) * (2.0 * math.pi / circle_cells)
    return jnp.concatenate([jnp.cos(phase), -jnp.sin(phase)], axis=1) / math.sqrt(circle_cells)

def reference(q_level, q_prev, blade_row):
    source = (4.0 * q_level - q_prev) / (2.0 * DT_PHYS)
    radius, inner_face, outer_face, theta_step, spin_rate = geometry(NR, NT, 0, NR)
    rotor_frame = (blade_row == 1).astype(jnp.float32)
    bladed = (blade_row > 0).astype(jnp.float32)
    flow_state = q_level
    for sweep in range(2):
        flow_state = pseudo_step(pad_grid(flow_state), source, radius, inner_face, outer_face, theta_step, spin_rate, rotor_frame, bladed)
    fields = field_pair(flow_state)
    basis = mode_basis(NT)
    spectra = jnp.einsum('frsa,sc->arfc', fields, basis, precision=lax.Precision.HIGHEST)
    return (flow_state, spectra.reshape(NA, NR, 4 * MODES))
```

```python
import math

import jax
import jax.numpy as jnp
import numpy as np
from jax import lax
from jax.experimental import pallas as pl
from jax.experimental.pallas import tpu as pltpu
from jax.sharding import PartitionSpec as P

MODES = 64
GAMMA = 1.4
KAPPA = 2.0

BAND = 16
SECTOR = 8
AXIAL = 256
F32 = jnp.float32
ALL = range(5)


def primitives(q):
    inverse = 1.0 / q[0]
    ux, ur, ut = q[1] * inverse, q[2] * inverse, q[3] * inverse
    pressure = (GAMMA - 1.0) * (q[4] - 0.5 * (q[1] * ux + q[2] * ur + q[3] * ut))
    sound = jnp.sqrt(GAMMA * pressure * inverse)
    return ux, ur, ut, pressure, sound


def flux(q, prim, d):
    u, pressure = prim[d - 1], prim[3]
    f = [q[d], q[1] * u, q[2] * u, q[3] * u, (q[4] + pressure) * u]
    f[d] = f[d] + pressure
    return f, jnp.abs(u) + prim[4]


def face(left_q, left_flux, right_q, right_flux):
    (fl, sl), (fr, sr) = left_flux, right_flux
    fastest = jnp.maximum(sl, sr)
    return [(fl[v] + fr[v]) - fastest * (right_q[v] - left_q[v]) for v in ALL]


def roll(x, shift, axis):
    return pltpu.roll(x, shift % x.shape[axis], axis)


def axial_difference(q, prim, lane):
    f, speed = flux(q, prim, 1)
    axis = q[0].ndim - 1
    qn = [roll(x, -1, axis) for x in q]
    fn = [qn[1]] + [roll(f[v], -1, axis) for v in range(1, 5)]
    right = face(q, (f, speed), qn, (fn, roll(speed, -1, axis)))
    ends = [2.0 * x for x in f]
    right = [jnp.where(lane == AXIAL - 1, e, x) for e, x in zip(ends, right)]
    left = [jnp.where(lane == 0, e, roll(x, 1, axis)) for e, x in zip(ends, right)]
    return [a - b for a, b in zip(right, left)]


def advance(q, prim, half_source, axial, radial, swirl, inv_r, inv_h, spin_r, bladed, rotor):
    ux, ur, ut, pressure, sound = prim
    half_r = 0.5 * inv_r
    force = bladed * (q[0] * (ut - rotor * spin_r))
    gains = [
        None,
        None,
        half_r * (q[3] * ut + pressure),
        -force - half_r * (q[2] * ut),
        -ut * force,
    ]
    rate = jnp.abs(ux) + jnp.abs(ur) + jnp.abs(ut) * inv_h + sound * (2.0 + inv_h)
    weight = 1.0 / (rate + 7.5)
    out = []
    for v in ALL:
        total = half_source[v] - 0.25 * axial[v] - radial[v] - swirl[v]
        if gains[v] is not None:
            total = total + gains[v]
        out.append((rate * q[v] + total) * weight)
    return out


def geometry_table(rows, circle):
    mean = circle / (2.0 * math.pi)
    row = np.arange(-1, rows + 1, dtype=np.float64)
    radius = mean * (0.8 + 0.4 * (row + 0.5) / rows)
    inner = mean * (0.8 + 0.4 * row / rows)
    outer = mean * (0.8 + 0.4 * (row + 1.0) / rows)
    spacing = radius * (2.0 * math.pi / circle)
    spin = radius / (1.2 * mean)
    table = np.stack(
        [0.25 * outer / radius, 0.25 * inner / radius, 0.25 / spacing, 1.0 / radius, 1.0 / spacing, spin]
    )
    return table.astype(np.float32)


def pack_kernel(q_ref, qp_ref, rad_ref, other_ref, core_ref, odiag_ref, cdiag_ref):
    odd = lax.axis_index("theta") % 2 == 1
    band = lax.axis_index("rad")
    near = jnp.where(band == 0, BAND - 1, 0)
    far = jnp.where(band == 0, BAND - 2, 1)
    for v in ALL:
        rad_ref[v, 0] = q_ref[v, near]
        rad_ref[v, 1] = q_ref[v, far]
        rad_ref[v, 2] = qp_ref[v, near]
        first, second = q_ref[v, :, 0, :], q_ref[v, :, 1, :]
        last, before = q_ref[v, :, SECTOR - 1, :], q_ref[v, :, SECTOR - 2, :]
        pfirst, plast = qp_ref[v, :, 0, :], qp_ref[v, :, SECTOR - 1, :]
        for ref, flip in ((other_ref, odd), (core_ref, jnp.logical_not(odd))):
            ref[v, 0:16] = jnp.where(flip, last, first)
            ref[v, 16:32] = jnp.where(flip, before, second)
            ref[v, 32:48] = jnp.where(flip, plast, pfirst)
        edge = q_ref[v, near]
        head, tail = edge[0:1], edge[SECTOR - 1 : SECTOR]
        odiag_ref[v : v + 1] = jnp.where(odd, tail, head)
        cdiag_ref[v : v + 1] = jnp.where(odd, head, tail)
    odiag_ref[5:8] = jnp.zeros((3, AXIAL), F32)
    cdiag_ref[5:8] = jnp.zeros((3, AXIAL), F32)


def flow_kernel(
    total_rows,
    circle,
    table_ref,
    blade_ref,
    q_ref,
    qp_ref,
    rad_ref,
    other_ref,
    core_ref,
    odiag_ref,
    cdiag_ref,
    flow_ref,
    send_ref,
    p0,
    p1,
    hs,
    ce,
    h,
    h2,
    fields,
):
    odd = lax.axis_index("theta") % 2 == 1
    band = lax.axis_index("rad")
    first_row = band * BAND
    low = band == 0
    blade = blade_ref[...]
    bladed_row = (blade > 0).astype(F32)
    rotor_row = (blade == 1).astype(F32)
    bladed = jnp.broadcast_to(bladed_row, (SECTOR, AXIAL))
    rotor = jnp.broadcast_to(rotor_row, (SECTOR, AXIAL))
    lane = lax.broadcasted_iota(jnp.int32, (SECTOR, AXIAL), 1)
    sub = lax.broadcasted_iota(jnp.int32, (SECTOR, AXIAL), 0)
    mirror = (1.0, 1.0, -1.0, 1.0, 1.0)

    near_at = jnp.where(low, BAND + 2, 1)
    far_at = jnp.where(low, BAND + 3, 0)
    wall_at = jnp.where(low, 1, BAND + 2)
    wall_row = jnp.where(low, 0, BAND - 1)
    for v in ALL:
        p0[v, 2 : BAND + 2] = q_ref[v]
        hs[v, 1 : BAND + 1] = 10.0 * q_ref[v] - 2.5 * qp_ref[v]
        p0[v, near_at] = rad_ref[v, 0]
        p0[v, far_at] = rad_ref[v, 1]
        p0[v, wall_at] = mirror[v] * q_ref[v, wall_row]
        hs[v, near_at - 1] = 10.0 * rad_ref[v, 0] - 2.5 * rad_ref[v, 2]

    rows16 = lax.broadcasted_iota(jnp.int32, (BAND, AXIAL), 0) + first_row
    lane16 = lax.broadcasted_iota(jnp.int32, (BAND, AXIAL), 1)
    rowf = rows16.astype(F32)
    mean = circle / (2.0 * math.pi)
    radius = mean * (0.8 + 0.4 * (rowf + 0.5) / total_rows)
    inner = mean * (0.8 + 0.4 * rowf / total_rows)
    outer = mean * (0.8 + 0.4 * (rowf + 1.0) / total_rows)
    inv_r = 1.0 / radius
    inv_h = inv_r * mean
    spin_r = radius * (1.0 / (1.2 * mean))
    corner_at = jnp.where(low, BAND, -1) + 8
    bladed16 = jnp.broadcast_to(bladed_row, (BAND, AXIAL))
    rotor16 = jnp.broadcast_to(rotor_row, (BAND, AXIAL))
    columns = []
    for side in (0, 1):
        use_core = odd if side == 0 else jnp.logical_not(odd)
        edge = 0 if side == 0 else SECTOR - 1

        def pick(lo, hi):
            return [jnp.where(use_core, core_ref[v, lo:hi], other_ref[v, lo:hi]) for v in ALL]

        near, far, prev = pick(0, 16), pick(16, 32), pick(32, 48)
        corner = [jnp.where(use_core, cdiag_ref[v : v + 1], odiag_ref[v : v + 1]) for v in ALL]
        own = [q_ref[v, :, edge, :] for v in ALL]
        own_corner = [rad_ref[v, 0, edge : edge + 1, :] for v in ALL]

        def swirl_face(halo, own):
            a, b = flux(halo, primitives(halo), 3), flux(own, primitives(own), 3)
            return face(halo, a, own, b) if side == 0 else face(own, b, halo, a)

        near_prim = primitives(near)
        nf = flux(near, near_prim, 3)
        of = flux(own, primitives(own), 3)
        ff = flux(far, primitives(far), 3)
        if side == 0:
            inside, outside = face(near, nf, own, of), face(far, ff, near, nf)
            swirl = [a - b for a, b in zip(inside, outside)]
        else:
            inside, outside = face(own, of, near, nf), face(near, nf, far, ff)
            swirl = [a - b for a, b in zip(outside, inside)]
        corner_face = swirl_face(corner, own_corner)
        for v in ALL:
            h[v, side, 8:24] = inside[v]
            h[v, side, pl.ds(corner_at, 1)] = corner_face[v]
            ce[v, side, 8:24] = near[v]
            ce[v, side, 7:8] = jnp.where(low, mirror[v] * near[v][0:1], corner[v])
            ce[v, side, 24:25] = jnp.where(low, corner[v], mirror[v] * near[v][BAND - 1 : BAND])
        below = [ce[v, side, 7:23] for v in ALL]
        above = [ce[v, side, 9:25] for v in ALL]
        rf = flux(near, near_prim, 2)
        g_in = face(below, flux(below, primitives(below), 2), near, rf)
        g_out = face(near, rf, above, flux(above, primitives(above), 2))
        half_source = [10.0 * near[v] - 2.5 * prev[v] for v in ALL]
        radial = [(0.25 * inv_r) * (outer * g_out[v] - inner * g_in[v]) for v in ALL]
        columns.append(
            advance(
                near,
                near_prim,
                half_source,
                axial_difference(near, near_prim, lane16),
                radial,
                [(0.25 * inv_h) * x for x in swirl],
                inv_r,
                inv_h,
                spin_r,
                bladed16,
                rotor16,
            )
        )

    def row(j, q, prim, g_in, g_out, faces):
        f = flux(q, prim, 3)
        qn = [roll(x, -1, 0) for x in q]
        fn = [qn[3]] + [roll(f[0][v], -1, 0) for v in range(1, 5)]
        between = face(q, f, qn, (fn, roll(f[1], -1, 0)))
        swirl = []
        at = j + 8
        g = first_row + j + 1
        a_out, a_in, a_h = table_ref[0, g], table_ref[1, g], table_ref[2, g]
        for v in ALL:
            right = jnp.where(sub == SECTOR - 1, faces[v, 1, pl.ds(at, 1)], between[v])
            left = jnp.where(sub == 0, faces[v, 0, pl.ds(at, 1)], roll(between[v], 1, 0))
            swirl.append(a_h * (right - left))
        radial = [a_out * g_out[v] - a_in * g_in[v] for v in ALL]
        return advance(
            q,
            prim,
            [hs[v, j + 1] for v in ALL],
            axial_difference(q, prim, lane),
            radial,
            swirl,
            table_ref[3, g],
            table_ref[4, g],
            table_ref[5, g],
            bladed,
            rotor,
        )

    def sweep(source, offset, start, count, faces, store):
        def load(j):
            q = [source[v, j + offset] for v in ALL]
            return q, primitives(q)

        below, below_prim = load(start - 1)
        q, prim = load(start)
        g_in = face(below, flux(below, below_prim, 2), q, flux(q, prim, 2))

        def body(i, carry):
            q, prim, g_in = carry
            j = start + i
            above, above_prim = load(j + 1)
            g_out = face(q, flux(q, prim, 2), above, flux(above, above_prim, 2))
            store(j, row(j, q, prim, g_in, g_out, faces))
            return above, above_prim, g_out

        lax.fori_loop(0, count, body, (q, prim, g_in))

    def keep(j, q):
        for v in ALL:
            p1[v, j + 1] = q[v]

    sweep(p0, 2, jnp.where(low, 0, -1), BAND + 1, h, keep)
    for v in ALL:
        p1[v, wall_at - 1] = mirror[v] * p1[v, wall_row + 1]

    for side in (0, 1):
        edge = 0 if side == 0 else SECTOR - 1
        halo = columns[side]
        own = [p1[v, 1 : BAND + 1, edge, :] for v in ALL]
        a, b = flux(halo, primitives(halo), 3), flux(own, primitives(own), 3)
        faces = face(halo, a, own, b) if side == 0 else face(own, b, halo, a)
        for v in ALL:
            h2[v, side, 8:24] = faces[v]

    def finish(j, q):
        for v in ALL:
            flow_ref[v, j] = q[v]
        ux, _, _, pressure, _ = primitives(q)
        fields[0, j] = pressure
        fields[1, j] = ux

    sweep(p1, 1, 0, BAND, h2, finish)
    for f in (0, 1):
        turned = fields[f].reshape(BAND * SECTOR, AXIAL).T
        send_ref[pl.ds(f, AXIAL, stride=2), :] = turned


def mode_kernel(got_ref, basis_ref, out_ref, turned):
    sectors = got_ref.shape[0] // 4
    parts = []
    for e in (0, 1):
        for f in (0, 1):
            n = 2 * e + f
            turned[n] = got_ref[pl.ds(n, sectors, stride=4), :].T
            parts.append(
                jnp.concatenate([turned[n, pl.ds(m, BAND, stride=SECTOR), :] for m in range(SECTOR)], axis=1)
            )
    product = jnp.dot(
        jnp.concatenate(parts, axis=0), basis_ref[...], precision=lax.Precision.HIGHEST, preferred_element_type=F32
    )
    for e in (0, 1):
        for f in (0, 1):
            n = 2 * e + f
            out_ref[e, :, 2 * MODES * f : 2 * MODES * (f + 1)] = product[BAND * n : BAND * (n + 1)]


def mode_basis(sectors):
    circle = sectors * SECTOR
    cell = (np.arange(SECTOR)[:, None] + SECTOR * np.arange(sectors)[None, :]).reshape(-1)
    phase = (cell[:, None] * np.arange(1, MODES + 1)[None, :] % circle) * (2.0 * np.pi / circle)
    return (np.concatenate([np.cos(phase), -np.sin(phase)], axis=1) / np.sqrt(circle)).astype(np.float32)


def shaped(*shape):
    return jax.ShapeDtypeStruct(shape, F32)


def vmem():
    return pl.BlockSpec(memory_space=pltpu.VMEM)


def per_device(q_level, q_prev, blade_row):
    sectors = lax.axis_size("theta")
    bands = lax.axis_size("rad")
    circle = sectors * SECTOR
    core = [(t, t ^ 1) for t in range(sectors)]
    other = [(t, (((t + 1) ^ 1) - 1) % sectors) for t in range(sectors)]
    diagonal = lambda pairs: [(bands * a + b, bands * c + 1 - b) for a, c in pairs for b in range(bands)]

    rad_out, other_out, core_out, odiag_out, cdiag_out = pl.pallas_call(
        pack_kernel,
        out_shape=[
            shaped(5, 3, SECTOR, AXIAL),
            shaped(5, 48, AXIAL),
            shaped(5, 48, AXIAL),
            shaped(8, AXIAL),
            shaped(8, AXIAL),
        ],
        in_specs=[vmem()] * 2,
        out_specs=[vmem()] * 5,
    )(q_level, q_prev)
    other_in = lax.ppermute(other_out, "theta", other)
    odiag_in = lax.ppermute(odiag_out, ("theta", "rad"), diagonal(other))
    rad_in = lax.ppermute(rad_out, "rad", [(0, 1), (1, 0)])
    cdiag_in = lax.ppermute(cdiag_out, ("theta", "rad"), diagonal(core))
    core_in = lax.ppermute(core_out, "theta", core)

    def kernel(*refs):
        flow_kernel(bands * BAND, circle, *refs)

    flow_state, send = pl.pallas_call(
        kernel,
        out_shape=[shaped(5, BAND, SECTOR, AXIAL), shaped(2 * AXIAL, BAND * SECTOR)],
        in_specs=[pl.BlockSpec(memory_space=pltpu.SMEM)] + [vmem()] * 8,
        out_specs=[vmem()] * 2,
        scratch_shapes=[
            pltpu.VMEM((5, BAND + 4, SECTOR, AXIAL), F32),
            pltpu.VMEM((5, BAND + 2, SECTOR, AXIAL), F32),
            pltpu.VMEM((5, BAND + 2, SECTOR, AXIAL), F32),
            pltpu.VMEM((5, 2, 32, AXIAL), F32),
            pltpu.VMEM((5, 2, 32, AXIAL), F32),
            pltpu.VMEM((5, 2, 32, AXIAL), F32),
            pltpu.VMEM((2, BAND, SECTOR, AXIAL), F32),
        ],
    )(
        jnp.asarray(geometry_table(bands * BAND, circle)),
        blade_row.reshape(1, AXIAL),
        q_level,
        q_prev,
        rad_in,
        other_in,
        core_in,
        odiag_in,
        cdiag_in,
    )
    got = lax.all_to_all(send.reshape(sectors, 4, 128), "theta", split_axis=0, concat_axis=0, tiled=True)
    spectra = pl.pallas_call(
        mode_kernel,
        out_shape=shaped(2, BAND, 4 * MODES),
        in_specs=[vmem()] * 2,
        out_specs=vmem(),
        scratch_shapes=[pltpu.VMEM((4, BAND * SECTOR, sectors), F32)],
    )(got.reshape(4 * sectors, 128), jnp.asarray(mode_basis(sectors)))
    return flow_state, spectra


def solution(mesh):
    in_specs = (P(None, "rad", "theta", None), P(None, "rad", "theta", None), P())
    out_specs = (P(None, "rad", "theta", None), P("theta", "rad", None))
    return jax.shard_map(per_device, mesh=mesh, in_specs=in_specs, out_specs=out_specs, check_vma=False)
```

```python
import math

import jax
import jax.numpy as jnp
import numpy as np
from jax import lax
from jax.experimental import pallas as pl
from jax.experimental.pallas import tpu as pltpu
from jax.sharding import PartitionSpec as P

MODES = 64
GAMMA = 1.4
KAPPA = 2.0

BAND = 16
SECTOR = 8
AXIAL = 256
F32 = jnp.float32
ALL = range(5)


def primitives(q):
    inverse = 1.0 / q[0]
    ux, ur, ut = q[1] * inverse, q[2] * inverse, q[3] * inverse
    pressure = (GAMMA - 1.0) * (q[4] - 0.5 * (q[1] * ux + q[2] * ur + q[3] * ut))
    sound = jnp.sqrt(GAMMA * pressure * inverse)
    return ux, ur, ut, pressure, sound


def flux(q, prim, d):
    u, pressure = prim[d - 1], prim[3]
    f = [q[d], q[1] * u, q[2] * u, q[3] * u, (q[4] + pressure) * u]
    f[d] = f[d] + pressure
    return f, jnp.abs(u) + prim[4]


def face(left_q, left_flux, right_q, right_flux):
    (fl, sl), (fr, sr) = left_flux, right_flux
    fastest = jnp.maximum(sl, sr)
    return [(fl[v] + fr[v]) - fastest * (right_q[v] - left_q[v]) for v in ALL]


def roll(x, shift, axis):
    return pltpu.roll(x, shift % x.shape[axis], axis)


def axial_difference(q, prim, lane):
    f, speed = flux(q, prim, 1)
    axis = q[0].ndim - 1
    qn = [roll(x, -1, axis) for x in q]
    fn = [qn[1]] + [roll(f[v], -1, axis) for v in range(1, 5)]
    right = face(q, (f, speed), qn, (fn, roll(speed, -1, axis)))
    ends = [2.0 * x for x in f]
    right = [jnp.where(lane == AXIAL - 1, e, x) for e, x in zip(ends, right)]
    left = [jnp.where(lane == 0, e, roll(x, 1, axis)) for e, x in zip(ends, right)]
    return [a - b for a, b in zip(right, left)]


def advance(q, prim, half_source, axial, radial, swirl, inv_r, inv_h, spin_r, bladed, rotor):
    ux, ur, ut, pressure, sound = prim
    half_r = 0.5 * inv_r
    force = bladed * (q[0] * (ut - rotor * spin_r))
    gains = [
        None,
        None,
        half_r * (q[3] * ut + pressure),
        -force - half_r * (q[2] * ut),
        -ut * force,
    ]
    rate = jnp.abs(ux) + jnp.abs(ur) + jnp.abs(ut) * inv_h + sound * (2.0 + inv_h)
    weight = 1.0 / (rate + 7.5)
    out = []
    for v in ALL:
        total = half_source[v] - 0.25 * axial[v] - radial[v] - swirl[v]
        if gains[v] is not None:
            total = total + gains[v]
        out.append((rate * q[v] + total) * weight)
    return out


def geometry_table(rows, circle):
    mean = circle / (2.0 * math.pi)
    row = np.arange(-1, rows + 1, dtype=np.float64)
    radius = mean * (0.8 + 0.4 * (row + 0.5) / rows)
    inner = mean * (0.8 + 0.4 * row / rows)
    outer = mean * (0.8 + 0.4 * (row + 1.0) / rows)
    spacing = radius * (2.0 * math.pi / circle)
    spin = radius / (1.2 * mean)
    table = np.stack(
        [0.25 * outer / radius, 0.25 * inner / radius, 0.25 / spacing, 1.0 / radius, 1.0 / spacing, spin]
    )
    return table.astype(np.float32)


def edge_row(band, at_low, at_high):
    return jnp.where(band == 0, at_low, at_high)


def rad_kernel(q_ref, qp_ref, rad_ref):
    band = lax.axis_index("rad")
    near = edge_row(band, BAND - 1, 0)
    far = edge_row(band, BAND - 2, 1)
    for v in ALL:
        rad_ref[v, 0] = q_ref[v, near]
        rad_ref[v, 1] = q_ref[v, far]
        rad_ref[v, 2] = qp_ref[v, near]


def pack_kernel(q_ref, qp_ref, rad_ref, other_ref, core_ref):
    odd = lax.axis_index("theta") % 2 == 1
    last = SECTOR - 1
    for v in ALL:
        low = [q_ref[v, :, 0, :], q_ref[v, :, 1, :], qp_ref[v, :, 0, :]]
        high = [q_ref[v, :, last, :], q_ref[v, :, last - 1, :], qp_ref[v, :, last, :]]
        corner = rad_ref[v, 0]
        low.append(jnp.broadcast_to(corner[0:1], (8, AXIAL)))
        high.append(jnp.broadcast_to(corner[last : last + 1], (8, AXIAL)))
        for n, (a, b) in enumerate(zip(low, high)):
            rows = slice(BAND * n, BAND * n + a.shape[0])
            other_ref[v, rows] = jnp.where(odd, b, a)
            core_ref[v, rows] = jnp.where(odd, a, b)


MIRROR = (1.0, 1.0, -1.0, 1.0, 1.0)


def blades(blade_ref, rows):
    blade = blade_ref[...]
    bladed = jnp.broadcast_to((blade > 0).astype(F32), (rows, AXIAL))
    rotor = jnp.broadcast_to((blade == 1).astype(F32), (rows, AXIAL))
    return bladed, rotor


def row_step(g, table_ref, q, prim, half_source, g_in, g_out, ends, masks, blade):
    lane, sub = masks
    f, speed = flux(q, prim, 3)
    qn = [roll(x, -1, 0) for x in q]
    fn = [qn[3]] + [roll(f[v], -1, 0) for v in range(1, 5)]
    between = face(q, (f, speed), qn, (fn, roll(speed, -1, 0)))
    a_out, a_in, a_h = table_ref[0, g], table_ref[1, g], table_ref[2, g]
    swirl = []
    for v in ALL:
        end = 0.0 if ends is None else ends[v]
        right = jnp.where(sub == SECTOR - 1, end, between[v])
        left = jnp.where(sub == 0, end, roll(between[v], 1, 0))
        swirl.append(a_h * (right - left))
    radial = [a_out * g_out[v] - a_in * g_in[v] for v in ALL]
    return advance(
        q,
        prim,
        half_source,
        axial_difference(q, prim, lane),
        radial,
        swirl,
        table_ref[3, g],
        table_ref[4, g],
        table_ref[5, g],
        *blade,
    )


def sweep(load, step, store):
    below = load(-1)
    below_prim = primitives(below)
    q = load(0)
    prim = primitives(q)
    g_in = face(below, flux(below, below_prim, 2), q, flux(q, prim, 2))

    def body(j, carry):
        q, prim, g_in = carry
        above = load(j + 1)
        above_prim = primitives(above)
        g_out = face(q, flux(q, prim, 2), above, flux(above, above_prim, 2))
        store(j, step(j, q, prim, g_in, g_out))
        return above, above_prim, g_out

    lax.fori_loop(0, BAND, body, (q, prim, g_in), unroll=4)


def early_kernel(table_ref, blade_ref, q_ref, qp_ref, rad_ref, p1_ref, hs_ref, p0):
    band = lax.axis_index("rad")
    first_row = band * BAND
    low = band == 0
    masks = (
        lax.broadcasted_iota(jnp.int32, (SECTOR, AXIAL), 1),
        lax.broadcasted_iota(jnp.int32, (SECTOR, AXIAL), 0),
    )
    blade = blades(blade_ref, SECTOR)
    near_at = edge_row(band, BAND + 1, 0)
    wall_at = edge_row(band, 0, BAND + 1)
    wall_row = edge_row(band, 0, BAND - 1)
    edge = edge_row(band, BAND - 1, 0)
    for v in ALL:
        p0[v, 1 : BAND + 1] = q_ref[v]
        p0[v, near_at] = rad_ref[v, 0]
        p0[v, wall_at] = MIRROR[v] * q_ref[v, wall_row]
        hs_ref[v] = 10.0 * q_ref[v] - 2.5 * qp_ref[v]

    def store(j, q):
        for v in ALL:
            p1_ref[v, j + 1] = q[v]

    sweep(
        lambda j: [p0[v, j + 1] for v in ALL],
        lambda j, q, prim, g_in, g_out: row_step(
            first_row + j + 1, table_ref, q, prim, [hs_ref[v, j] for v in ALL], g_in, g_out, None, masks, blade
        ),
        store,
    )
    near = [rad_ref[v, 0] for v in ALL]
    far = [rad_ref[v, 1] for v in ALL]
    own = [q_ref[v, edge] for v in ALL]
    below = [jnp.where(low, own[v], far[v]) for v in ALL]
    above = [jnp.where(low, far[v], own[v]) for v in ALL]
    prim = primitives(near)
    f = flux(near, prim, 2)
    g_in = face(below, flux(below, primitives(below), 2), near, f)
    g_out = face(near, f, above, flux(above, primitives(above), 2))
    half_source = [10.0 * near[v] - 2.5 * rad_ref[v, 2] for v in ALL]
    stepped = row_step(first_row + near_at, table_ref, near, prim, half_source, g_in, g_out, None, masks, blade)
    for v in ALL:
        p1_ref[v, near_at] = stepped[v]
        p1_ref[v, wall_at] = jnp.zeros((SECTOR, AXIAL), F32)


def final_kernel(
    total_rows,
    circle,
    table_ref,
    blade_ref,
    q_ref,
    rad_ref,
    p1_ref,
    hs_ref,
    other_ref,
    core_ref,
    flow_ref,
    send_ref,
    p1,
    ends,
    ce,
    fields,
):
    odd = lax.axis_index("theta") % 2 == 1
    band = lax.axis_index("rad")
    first_row = band * BAND
    low = band == 0
    near_at = edge_row(band, BAND + 1, 0)
    wall_at = edge_row(band, 0, BAND + 1)
    wall_row = edge_row(band, 0, BAND - 1)
    masks = (
        lax.broadcasted_iota(jnp.int32, (SECTOR, AXIAL), 1),
        lax.broadcasted_iota(jnp.int32, (SECTOR, AXIAL), 0),
    )
    for v in ALL:
        p1[v] = p1_ref[v]

    rows = (lax.broadcasted_iota(jnp.int32, (BAND, AXIAL), 0) + first_row).astype(F32)
    lane = lax.broadcasted_iota(jnp.int32, (BAND, AXIAL), 1)
    mean = circle / (2.0 * math.pi)
    radius = mean * (0.8 + 0.4 * (rows + 0.5) / total_rows)
    inner = mean * (0.8 + 0.4 * rows / total_rows)
    outer = mean * (0.8 + 0.4 * (rows + 1.0) / total_rows)
    inv_r = 1.0 / radius
    inv_h = inv_r * mean
    spin_r = radius * (1.0 / (1.2 * mean))
    a_h = 0.25 * inv_h
    blade16 = blades(blade_ref, BAND)
    g_near = first_row + near_at

    def speed_weight(prim, inv_h):
        ux, ur, ut, _, sound = prim
        return 1.0 / (jnp.abs(ux) + jnp.abs(ur) + jnp.abs(ut) * inv_h + sound * (2.0 + inv_h) + 7.5)

    for side in (0, 1):
        use_core = odd if side == 0 else jnp.logical_not(odd)
        at = 0 if side == 0 else SECTOR - 1
        sign = 1.0 if side == 0 else -1.0

        def pick(lo, hi):
            return [jnp.where(use_core, core_ref[v, lo:hi], other_ref[v, lo:hi]) for v in ALL]

        def ordered(halo, halo_flux, own, own_flux):
            if side == 0:
                return face(halo, halo_flux, own, own_flux)
            return face(own, own_flux, halo, halo_flux)

        near, far, prev, corner = pick(0, 16), pick(16, 32), pick(32, 48), pick(48, 49)
        own = [q_ref[v, :, at, :] for v in ALL]
        own_prim, near_prim = primitives(own), primitives(near)
        near_flux = flux(near, near_prim, 3)
        inside = ordered(near, near_flux, own, flux(own, own_prim, 3))
        outside = ordered(far, flux(far, primitives(far), 3), near, near_flux)
        scale = (sign * a_h) * speed_weight(own_prim, inv_h)
        own_next = [p1_ref[v, 1 : BAND + 1, at, :] + scale * inside[v] for v in ALL]

        edge = [rad_ref[v, 0, at : at + 1, :] for v in ALL]
        edge_prim = primitives(edge)
        corner_face = ordered(corner, flux(corner, primitives(corner), 3), edge, flux(edge, edge_prim, 3))
        corner_scale = (sign * table_ref[2, g_near]) * speed_weight(edge_prim, table_ref[4, g_near])

        for v in ALL:
            p1[v, 1 : BAND + 1, at, :] = own_next[v]
            p1[v, near_at, at : at + 1, :] = p1_ref[v, near_at, at : at + 1, :] + corner_scale * corner_face[v]
            ce[v, side, 8:24] = near[v]
            ce[v, side, 7:8] = jnp.where(low, MIRROR[v] * near[v][0:1], corner[v])
            ce[v, side, 24:25] = jnp.where(low, corner[v], MIRROR[v] * near[v][BAND - 1 : BAND])
        below = [ce[v, side, 7:23] for v in ALL]
        above = [ce[v, side, 9:25] for v in ALL]
        f = flux(near, near_prim, 2)
        g_in = face(below, flux(below, primitives(below), 2), near, f)
        g_out = face(near, f, above, flux(above, primitives(above), 2))
        near_next = advance(
            near,
            near_prim,
            [10.0 * near[v] - 2.5 * prev[v] for v in ALL],
            axial_difference(near, near_prim, lane),
            [(0.25 * inv_r) * (outer * g_out[v] - inner * g_in[v]) for v in ALL],
            [(sign * a_h) * (inside[v] - outside[v]) for v in ALL],
            inv_r,
            inv_h,
            spin_r,
            *blade16,
        )
        faces = ordered(
            near_next, flux(near_next, primitives(near_next), 3), own_next, flux(own_next, primitives(own_next), 3)
        )
        for v in ALL:
            ends[v, :, at, :] = faces[v]

    for v in ALL:
        p1[v, wall_at] = MIRROR[v] * p1[v, wall_row + 1]

    def store(j, q):
        for v in ALL:
            flow_ref[v, j] = q[v]
        ux, _, _, pressure, _ = primitives(q)
        fields[0, j] = pressure
        fields[1, j] = ux

    blade = blades(blade_ref, SECTOR)
    sweep(
        lambda j: [p1[v, j + 1] for v in ALL],
        lambda j, q, prim, g_in, g_out: row_step(
            first_row + j + 1,
            table_ref,
            q,
            prim,
            [hs_ref[v, j] for v in ALL],
            g_in,
            g_out,
            [ends[v, j] for v in ALL],
            masks,
            blade,
        ),
        store,
    )
    for f in (0, 1):
        turned = fields[f].reshape(BAND * SECTOR, AXIAL).T
        send_ref[pl.ds(f, AXIAL, stride=2), :] = turned


def mode_kernel(got_ref, basis_ref, out_ref, turned):
    sectors = got_ref.shape[0] // 4
    parts = []
    for e in (0, 1):
        for f in (0, 1):
            n = 2 * e + f
            turned[n] = got_ref[pl.ds(n, sectors, stride=4), :].T
            parts.append(
                jnp.concatenate([turned[n, pl.ds(m, BAND, stride=SECTOR), :] for m in range(SECTOR)], axis=1)
            )
    product = jnp.dot(
        jnp.concatenate(parts, axis=0), basis_ref[...], precision=lax.Precision.HIGHEST, preferred_element_type=F32
    )
    for e in (0, 1):
        for f in (0, 1):
            n = 2 * e + f
            out_ref[e, :, 2 * MODES * f : 2 * MODES * (f + 1)] = product[BAND * n : BAND * (n + 1)]


def mode_basis(sectors):
    circle = sectors * SECTOR
    cell = (np.arange(SECTOR)[:, None] + SECTOR * np.arange(sectors)[None, :]).reshape(-1)
    phase = (cell[:, None] * np.arange(1, MODES + 1)[None, :] % circle) * (2.0 * np.pi / circle)
    return (np.concatenate([np.cos(phase), -np.sin(phase)], axis=1) / np.sqrt(circle)).astype(np.float32)


def shaped(*shape):
    return jax.ShapeDtypeStruct(shape, F32)


def vmem():
    return pl.BlockSpec(memory_space=pltpu.VMEM)


def limit(mib):
    return pltpu.CompilerParams(vmem_limit_bytes=mib << 20)


def per_device(q_level, q_prev, blade_row):
    sectors = lax.axis_size("theta")
    bands = lax.axis_size("rad")
    circle = sectors * SECTOR
    core = [(t, t ^ 1) for t in range(sectors)]
    other = [(t, (((t + 1) ^ 1) - 1) % sectors) for t in range(sectors)]
    table = jnp.asarray(geometry_table(bands * BAND, circle))
    blade = blade_row.reshape(1, AXIAL)
    smem = pl.BlockSpec(memory_space=pltpu.SMEM)

    rad_out = pl.pallas_call(
        rad_kernel,
        out_shape=shaped(5, 3, SECTOR, AXIAL),
        in_specs=[vmem()] * 2,
        out_specs=vmem(),
        compiler_params=limit(4),
    )(q_level, q_prev)
    rad_in = lax.ppermute(rad_out, "rad", [(0, 1), (1, 0)])
    other_out, core_out = pl.pallas_call(
        pack_kernel,
        out_shape=[shaped(5, 56, AXIAL)] * 2,
        in_specs=[vmem()] * 3,
        out_specs=[vmem()] * 2,
        compiler_params=limit(4),
    )(q_level, q_prev, rad_in)
    other_in = lax.ppermute(other_out, "theta", other)
    core_in = lax.ppermute(core_out, "theta", core)
    part, half_source = pl.pallas_call(
        early_kernel,
        out_shape=[shaped(5, BAND + 2, SECTOR, AXIAL), shaped(5, BAND, SECTOR, AXIAL)],
        in_specs=[smem] + [vmem()] * 4,
        out_specs=[vmem()] * 2,
        scratch_shapes=[pltpu.VMEM((5, BAND + 2, SECTOR, AXIAL), F32)],
        compiler_params=limit(8),
        cost_estimate=pl.CostEstimate(flops=10_000_000, bytes_accessed=3_500_000, transcendentals=100_000),
    )(table, blade, q_level, q_prev, rad_in)

    def kernel(*refs):
        final_kernel(bands * BAND, circle, *refs)

    flow_state, send = pl.pallas_call(
        kernel,
        out_shape=[shaped(5, BAND, SECTOR, AXIAL), shaped(2 * AXIAL, BAND * SECTOR)],
        in_specs=[smem] + [vmem()] * 7,
        out_specs=[vmem()] * 2,
        scratch_shapes=[
            pltpu.VMEM((5, BAND + 2, SECTOR, AXIAL), F32),
            pltpu.VMEM((5, BAND, SECTOR, AXIAL), F32),
            pltpu.VMEM((5, 2, 32, AXIAL), F32),
            pltpu.VMEM((2, BAND, SECTOR, AXIAL), F32),
        ],
        compiler_params=limit(8),
    )(table, blade, q_level, rad_in, part, half_source, other_in, core_in)
    got = lax.all_to_all(send.reshape(sectors, 4, 128), "theta", split_axis=0, concat_axis=0, tiled=True)
    spectra = pl.pallas_call(
        mode_kernel,
        out_shape=shaped(2, BAND, 4 * MODES),
        in_specs=[vmem()] * 2,
        out_specs=vmem(),
        scratch_shapes=[pltpu.VMEM((4, BAND * SECTOR, sectors), F32)],
        compiler_params=limit(4),
    )(got.reshape(4 * sectors, 128), jnp.asarray(mode_basis(sectors)))
    return flow_state, spectra


def solution(mesh):
    in_specs = (P(None, "rad", "theta", None), P(None, "rad", "theta", None), P())
    out_specs = (P(None, "rad", "theta", None), P("theta", "rad", None))
    return jax.shard_map(per_device, mesh=mesh, in_specs=in_specs, out_specs=out_specs, check_vma=False)
```

```python
import math

import jax
import jax.numpy as jnp
import numpy as np
from jax import lax
from jax.experimental import pallas as pl
from jax.experimental.pallas import tpu as pltpu
from jax.sharding import PartitionSpec as P

MODES = 64
GAMMA = 1.4
KAPPA = 2.0

BAND = 16
SECTOR = 8
AXIAL = 256
F32 = jnp.float32
ALL = range(5)


def primitives(q):
    inverse = 1.0 / q[0]
    ux, ur, ut = q[1] * inverse, q[2] * inverse, q[3] * inverse
    pressure = (GAMMA - 1.0) * (q[4] - 0.5 * (q[1] * ux + q[2] * ur + q[3] * ut))
    sound = jnp.sqrt(GAMMA * pressure * inverse)
    return ux, ur, ut, pressure, sound


def flux(q, prim, d):
    u, pressure = prim[d - 1], prim[3]
    f = [q[d], q[1] * u, q[2] * u, q[3] * u, (q[4] + pressure) * u]
    f[d] = f[d] + pressure
    return f, jnp.abs(u) + prim[4]


def face(left_q, left_flux, right_q, right_flux):
    (fl, sl), (fr, sr) = left_flux, right_flux
    fastest = jnp.maximum(sl, sr)
    return [(fl[v] + fr[v]) - fastest * (right_q[v] - left_q[v]) for v in ALL]


def roll(x, shift, axis):
    return pltpu.roll(x, shift % x.shape[axis], axis)


def axial_difference(q, prim, lane):
    f, speed = flux(q, prim, 1)
    axis = q[0].ndim - 1
    qn = [roll(x, -1, axis) for x in q]
    fn = [qn[1]] + [roll(f[v], -1, axis) for v in range(1, 5)]
    right = face(q, (f, speed), qn, (fn, roll(speed, -1, axis)))
    ends = [2.0 * x for x in f]
    right = [jnp.where(lane == AXIAL - 1, e, x) for e, x in zip(ends, right)]
    left = [jnp.where(lane == 0, e, roll(x, 1, axis)) for e, x in zip(ends, right)]
    return [a - b for a, b in zip(right, left)]


def advance(q, prim, half_source, axial, radial, swirl, inv_r, inv_h, spin_r, bladed, rotor):
    ux, ur, ut, pressure, sound = prim
    half_r = 0.5 * inv_r
    force = bladed * (q[0] * (ut - rotor * spin_r))
    gains = [
        None,
        None,
        half_r * (q[3] * ut + pressure),
        -force - half_r * (q[2] * ut),
        -ut * force,
    ]
    rate = jnp.abs(ux) + jnp.abs(ur) + jnp.abs(ut) * inv_h + sound * (2.0 + inv_h)
    weight = 1.0 / (rate + 7.5)
    out = []
    for v in ALL:
        total = half_source[v] - 0.25 * axial[v] - radial[v] - swirl[v]
        if gains[v] is not None:
            total = total + gains[v]
        out.append((rate * q[v] + total) * weight)
    return out


def geometry_table(rows, circle):
    mean = circle / (2.0 * math.pi)
    row = np.arange(-1, rows + 1, dtype=np.float64)
    radius = mean * (0.8 + 0.4 * (row + 0.5) / rows)
    inner = mean * (0.8 + 0.4 * row / rows)
    outer = mean * (0.8 + 0.4 * (row + 1.0) / rows)
    spacing = radius * (2.0 * math.pi / circle)
    spin = radius / (1.2 * mean)
    table = np.stack(
        [0.25 * outer / radius, 0.25 * inner / radius, 0.25 / spacing, 1.0 / radius, 1.0 / spacing, spin]
    )
    return table.astype(np.float32)


def edge_row(band, at_low, at_high):
    return jnp.where(band == 0, at_low, at_high)


def rad_kernel(q_ref, rad_ref, sem):
    near = edge_row(lax.axis_index("rad"), BAND - 1, 0)
    copy = pltpu.make_async_copy(q_ref.at[:, near], rad_ref, sem)
    copy.start()
    copy.wait()


MIRROR = (1.0, 1.0, -1.0, 1.0, 1.0)


def blades(blade_ref, rows):
    blade = blade_ref[...]
    bladed = jnp.broadcast_to((blade > 0).astype(F32), (rows, AXIAL))
    rotor = jnp.broadcast_to((blade == 1).astype(F32), (rows, AXIAL))
    return bladed, rotor


class Columns:
    def __init__(self, first_row, total_rows, circle):
        rows = (lax.broadcasted_iota(jnp.int32, (BAND, AXIAL), 0) + first_row).astype(F32)
        mean = circle / (2.0 * math.pi)
        radius = mean * (0.8 + 0.4 * (rows + 0.5) / total_rows)
        self.inner = mean * (0.8 + 0.4 * rows / total_rows)
        self.outer = mean * (0.8 + 0.4 * (rows + 1.0) / total_rows)
        self.inv_r = 1.0 / radius
        self.inv_h = self.inv_r * mean
        self.spin_r = radius * (1.0 / (1.2 * mean))
        self.a_h = 0.25 * self.inv_h


def load_kernel(q_ref, qp_ref, q_out_ref, qp_out_ref, sems):
    copies = [
        pltpu.make_async_copy(q_ref, q_out_ref, sems.at[0]),
        pltpu.make_async_copy(qp_ref, qp_out_ref, sems.at[1]),
    ]
    for copy in copies:
        copy.start()
    for copy in copies:
        copy.wait()


def pack_kernel(total_rows, circle, blade_ref, q_ref, qp_ref, rad_ref, other_ref, core_ref, ce):
    odd = lax.axis_index("theta") % 2 == 1
    band = lax.axis_index("rad")
    low = band == 0
    geo = Columns(band * BAND, total_rows, circle)
    blade = blades(blade_ref, BAND)
    lane = lax.broadcasted_iota(jnp.int32, (BAND, AXIAL), 1)
    sides = []
    for side in (0, 1):
        at, inner = (0, 1) if side == 0 else (SECTOR - 1, SECTOR - 2)
        edge = [q_ref[v, :, at, :] for v in ALL]
        second = [q_ref[v, :, inner, :] for v in ALL]
        half_source = [10.0 * edge[v] - 2.5 * qp_ref[v, :, at, :] for v in ALL]
        corner = [rad_ref[v, at : at + 1, :] for v in ALL]
        for v in ALL:
            ce[v, side, 8:24] = edge[v]
            ce[v, side, 7:8] = jnp.where(low, MIRROR[v] * edge[v][0:1], corner[v])
            ce[v, side, 24:25] = jnp.where(low, corner[v], MIRROR[v] * edge[v][BAND - 1 : BAND])
        below = [ce[v, side, 7:23] for v in ALL]
        above = [ce[v, side, 9:25] for v in ALL]
        prim = primitives(edge)
        f = flux(edge, prim, 2)
        g_in = face(below, flux(below, primitives(below), 2), edge, f)
        g_out = face(edge, f, above, flux(above, primitives(above), 2))
        f = flux(edge, prim, 3)
        second_flux = flux(second, primitives(second), 3)
        if side == 0:
            swirl = [geo.a_h * x for x in face(edge, f, second, second_flux)]
        else:
            swirl = [-geo.a_h * x for x in face(second, second_flux, edge, f)]
        part = advance(
            edge,
            prim,
            half_source,
            axial_difference(edge, prim, lane),
            [(0.25 * geo.inv_r) * (geo.outer * g_out[v] - geo.inner * g_in[v]) for v in ALL],
            swirl,
            geo.inv_r,
            geo.inv_h,
            geo.spin_r,
            *blade,
        )
        sides.append((edge, part, [jnp.broadcast_to(x, (8, AXIAL)) for x in corner]))
    for n, (a, b) in enumerate(zip(*sides)):
        for v in ALL:
            rows = slice(BAND * n, BAND * n + a[v].shape[0])
            other_ref[v, rows] = jnp.where(odd, b[v], a[v])
            core_ref[v, rows] = jnp.where(odd, a[v], b[v])


def row_step(g, table_ref, q, prim, half_source, g_in, g_out, ends, masks, blade):
    lane, sub = masks
    f, speed = flux(q, prim, 3)
    qn = [roll(x, -1, 0) for x in q]
    fn = [qn[3]] + [roll(f[v], -1, 0) for v in range(1, 5)]
    between = face(q, (f, speed), qn, (fn, roll(speed, -1, 0)))
    a_out, a_in, a_h = table_ref[0, g], table_ref[1, g], table_ref[2, g]
    swirl = []
    for v in ALL:
        end = 0.0 if ends is None else ends[v]
        right = jnp.where(sub == SECTOR - 1, end, between[v])
        left = jnp.where(sub == 0, end, roll(between[v], 1, 0))
        swirl.append(a_h * (right - left))
    radial = [a_out * g_out[v] - a_in * g_in[v] for v in ALL]
    return advance(
        q,
        prim,
        half_source,
        axial_difference(q, prim, lane),
        radial,
        swirl,
        table_ref[3, g],
        table_ref[4, g],
        table_ref[5, g],
        *blade,
    )


def sweep(load, step, store):
    below = load(-1)
    below_prim = primitives(below)
    q = load(0)
    prim = primitives(q)
    g_in = face(below, flux(below, below_prim, 2), q, flux(q, prim, 2))

    def body(j, carry):
        q, prim, g_in = carry
        above = load(j + 1)
        above_prim = primitives(above)
        g_out = face(q, flux(q, prim, 2), above, flux(above, above_prim, 2))
        store(j, step(j, q, prim, g_in, g_out))
        return above, above_prim, g_out

    lax.fori_loop(0, BAND, body, (q, prim, g_in), unroll=4)


def early_kernel(table_ref, blade_ref, q_ref, qp_ref, rad_ref, p1_ref, edge_ref, hs_ref, p0):
    band = lax.axis_index("rad")
    first_row = band * BAND
    masks = (
        lax.broadcasted_iota(jnp.int32, (SECTOR, AXIAL), 1),
        lax.broadcasted_iota(jnp.int32, (SECTOR, AXIAL), 0),
    )
    blade = blades(blade_ref, SECTOR)
    near_at = edge_row(band, BAND + 1, 0)
    wall_at = edge_row(band, 0, BAND + 1)
    wall_row = edge_row(band, 0, BAND - 1)
    for v in ALL:
        p0[v, 1 : BAND + 1] = q_ref[v]
        p0[v, near_at] = rad_ref[v]
        p0[v, wall_at] = MIRROR[v] * q_ref[v, wall_row]
        hs_ref[v] = 10.0 * q_ref[v] - 2.5 * qp_ref[v]

    def store(j, q):
        for v in ALL:
            p1_ref[v, j] = q[v]

    sweep(
        lambda j: [p0[v, j + 1] for v in ALL],
        lambda j, q, prim, g_in, g_out: row_step(
            first_row + j + 1, table_ref, q, prim, [hs_ref[v, j] for v in ALL], g_in, g_out, None, masks, blade
        ),
        store,
    )
    for v in ALL:
        edge_ref[v] = p1_ref[v, edge_row(band, BAND - 1, 0)]


def final_kernel(
    total_rows,
    circle,
    table_ref,
    blade_ref,
    q_ref,
    rad_ref,
    p1_ref,
    hs_ref,
    next_ref,
    other_ref,
    core_ref,
    flow_ref,
    send_ref,
    p1,
    ends,
    fields,
):
    odd = lax.axis_index("theta") % 2 == 1
    band = lax.axis_index("rad")
    first_row = band * BAND
    near_at = edge_row(band, BAND + 1, 0)
    wall_at = edge_row(band, 0, BAND + 1)
    wall_row = edge_row(band, 0, BAND - 1)
    masks = (
        lax.broadcasted_iota(jnp.int32, (SECTOR, AXIAL), 1),
        lax.broadcasted_iota(jnp.int32, (SECTOR, AXIAL), 0),
    )
    for v in ALL:
        p1[v, 1 : BAND + 1] = p1_ref[v]
        p1[v, near_at] = next_ref[v]

    geo = Columns(first_row, total_rows, circle)
    g_near = first_row + near_at

    def weight(prim, inv_h):
        ux, ur, ut, _, sound = prim
        return 1.0 / (jnp.abs(ux) + jnp.abs(ur) + jnp.abs(ut) * inv_h + sound * (2.0 + inv_h) + 7.5)

    for side in (0, 1):
        use_core = odd if side == 0 else jnp.logical_not(odd)
        at = 0 if side == 0 else SECTOR - 1
        sign = 1.0 if side == 0 else -1.0

        def pick(lo, hi):
            return [jnp.where(use_core, core_ref[v, lo:hi], other_ref[v, lo:hi]) for v in ALL]

        def ordered(halo, halo_prim, own, own_prim):
            a, b = flux(halo, halo_prim, 3), flux(own, own_prim, 3)
            return face(halo, a, own, b) if side == 0 else face(own, b, halo, a)

        near, near_part, corner = pick(0, 16), pick(16, 32), pick(32, 33)
        own = [q_ref[v, :, at, :] for v in ALL]
        own_prim, near_prim = primitives(own), primitives(near)
        shared = ordered(near, near_prim, own, own_prim)
        own_scale = (sign * geo.a_h) * weight(own_prim, geo.inv_h)
        near_scale = (-sign * geo.a_h) * weight(near_prim, geo.inv_h)
        own_next = [p1_ref[v, :, at, :] + own_scale * shared[v] for v in ALL]
        near_next = [near_part[v] + near_scale * shared[v] for v in ALL]

        edge = [rad_ref[v, at : at + 1, :] for v in ALL]
        edge_prim = primitives(edge)
        corner_face = ordered(corner, primitives(corner), edge, edge_prim)
        corner_scale = (sign * table_ref[2, g_near]) * weight(edge_prim, table_ref[4, g_near])

        faces = ordered(near_next, primitives(near_next), own_next, primitives(own_next))
        for v in ALL:
            p1[v, 1 : BAND + 1, at, :] = own_next[v]
            p1[v, near_at, at : at + 1, :] = next_ref[v, at : at + 1, :] + corner_scale * corner_face[v]
            ends[v, :, at, :] = faces[v]

    for v in ALL:
        p1[v, wall_at] = MIRROR[v] * p1[v, wall_row + 1]

    def store(j, q):
        for v in ALL:
            flow_ref[v, j] = q[v]
        ux, _, _, pressure, _ = primitives(q)
        fields[0, j] = pressure
        fields[1, j] = ux

    blade = blades(blade_ref, SECTOR)
    sweep(
        lambda j: [p1[v, j + 1] for v in ALL],
        lambda j, q, prim, g_in, g_out: row_step(
            first_row + j + 1,
            table_ref,
            q,
            prim,
            [hs_ref[v, j] for v in ALL],
            g_in,
            g_out,
            [ends[v, j] for v in ALL],
            masks,
            blade,
        ),
        store,
    )
    for f in (0, 1):
        turned = fields[f].reshape(BAND * SECTOR, AXIAL).T
        send_ref[pl.ds(f, AXIAL, stride=2), :] = turned


def mode_kernel(got_ref, basis_ref, flow_ref, out_ref, flow_out_ref, turned, sem):
    copy = pltpu.make_async_copy(flow_ref, flow_out_ref, sem)
    copy.start()
    sectors = got_ref.shape[0] // 4
    parts = []
    for e in (0, 1):
        for f in (0, 1):
            n = 2 * e + f
            turned[n] = got_ref[pl.ds(n, sectors, stride=4), :].T
            parts.append(
                jnp.concatenate([turned[n, pl.ds(m, BAND, stride=SECTOR), :] for m in range(SECTOR)], axis=1)
            )
    product = jnp.dot(
        jnp.concatenate(parts, axis=0), basis_ref[...], precision=lax.Precision.HIGHEST, preferred_element_type=F32
    )
    for e in (0, 1):
        for f in (0, 1):
            n = 2 * e + f
            out_ref[e, :, 2 * MODES * f : 2 * MODES * (f + 1)] = product[BAND * n : BAND * (n + 1)]
    copy.wait()


def mode_basis(sectors):
    circle = sectors * SECTOR
    cell = (np.arange(SECTOR)[:, None] + SECTOR * np.arange(sectors)[None, :]).reshape(-1)
    phase = (cell[:, None] * np.arange(1, MODES + 1)[None, :] % circle) * (2.0 * np.pi / circle)
    return (np.concatenate([np.cos(phase), -np.sin(phase)], axis=1) / np.sqrt(circle)).astype(np.float32)


def shaped(*shape):
    return jax.ShapeDtypeStruct(shape, F32)


def vmem():
    return pl.BlockSpec(memory_space=pltpu.VMEM)


def limit(mib):
    return pltpu.CompilerParams(vmem_limit_bytes=int(mib * 2**20))


def per_device(q_level, q_prev, blade_row):
    sectors = lax.axis_size("theta")
    bands = lax.axis_size("rad")
    circle = sectors * SECTOR
    core = [(t, t ^ 1) for t in range(sectors)]
    other = [(t, (((t + 1) ^ 1) - 1) % sectors) for t in range(sectors)]
    table = jnp.asarray(geometry_table(bands * BAND, circle))
    blade = blade_row.reshape(1, AXIAL)
    smem = pl.BlockSpec(memory_space=pltpu.SMEM)

    hbm = pl.BlockSpec(memory_space=pltpu.HBM)
    swap = [(0, 1), (1, 0)]

    def pack(*refs):
        pack_kernel(bands * BAND, circle, *refs)

    def final(*refs):
        final_kernel(bands * BAND, circle, *refs)

    rad_in = lax.ppermute(
        pl.pallas_call(
            rad_kernel,
            out_shape=shaped(5, SECTOR, AXIAL),
            in_specs=[hbm],
            out_specs=vmem(),
            scratch_shapes=[pltpu.SemaphoreType.DMA],
            compiler_params=limit(63.5),
        )(q_level),
        "rad",
        swap,
    )
    q_level, q_prev = pl.pallas_call(
        load_kernel,
        out_shape=[shaped(5, BAND, SECTOR, AXIAL)] * 2,
        in_specs=[hbm] * 2,
        out_specs=[vmem()] * 2,
        scratch_shapes=[pltpu.SemaphoreType.DMA((2,))],
        compiler_params=limit(2),
        cost_estimate=pl.CostEstimate(flops=0, bytes_accessed=3_000_000, transcendentals=0),
    )(q_level, q_prev)
    other_out, core_out = pl.pallas_call(
        pack,
        out_shape=[shaped(5, 40, AXIAL)] * 2,
        in_specs=[vmem()] * 4,
        out_specs=[vmem()] * 2,
        scratch_shapes=[pltpu.VMEM((5, 2, 32, AXIAL), F32)],
        compiler_params=limit(4),
    )(blade, q_level, q_prev, rad_in)
    core_in = lax.ppermute(core_out, "theta", core)
    other_in = lax.ppermute(other_out, "theta", other)
    part, edge, half_source = pl.pallas_call(
        early_kernel,
        out_shape=[shaped(5, BAND, SECTOR, AXIAL), shaped(5, SECTOR, AXIAL), shaped(5, BAND, SECTOR, AXIAL)],
        in_specs=[smem] + [vmem()] * 4,
        out_specs=[vmem()] * 3,
        scratch_shapes=[pltpu.VMEM((5, BAND + 2, SECTOR, AXIAL), F32)],
        compiler_params=limit(8),
        cost_estimate=pl.CostEstimate(flops=10_000_000, bytes_accessed=3_500_000, transcendentals=100_000),
    )(table, blade, q_level, q_prev, rad_in)
    next_in = lax.ppermute(edge, "rad", swap)
    flow_state, send = pl.pallas_call(
        final,
        out_shape=[shaped(5, BAND, SECTOR, AXIAL), shaped(2 * AXIAL, BAND * SECTOR)],
        in_specs=[smem] + [vmem()] * 8,
        out_specs=[vmem()] * 2,
        scratch_shapes=[
            pltpu.VMEM((5, BAND + 2, SECTOR, AXIAL), F32),
            pltpu.VMEM((5, BAND, SECTOR, AXIAL), F32),
            pltpu.VMEM((2, BAND, SECTOR, AXIAL), F32),
        ],
        compiler_params=limit(8),
    )(table, blade, q_level, rad_in, part, half_source, next_in, other_in, core_in)
    got = lax.all_to_all(send.reshape(sectors, 4, 128), "theta", split_axis=0, concat_axis=0, tiled=True)
    spectra, flow_state = pl.pallas_call(
        mode_kernel,
        out_shape=[shaped(2, BAND, 4 * MODES), shaped(5, BAND, SECTOR, AXIAL)],
        in_specs=[vmem()] * 3,
        out_specs=[vmem(), hbm],
        scratch_shapes=[pltpu.VMEM((4, BAND * SECTOR, sectors), F32), pltpu.SemaphoreType.DMA],
        compiler_params=limit(4),
    )(got.reshape(4 * sectors, 128), jnp.asarray(mode_basis(sectors)), flow_state)
    return flow_state, spectra


def solution(mesh):
    in_specs = (P(None, "rad", "theta", None), P(None, "rad", "theta", None), P())
    out_specs = (P(None, "rad", "theta", None), P("theta", "rad", None))
    return jax.shard_map(per_device, mesh=mesh, in_specs=in_specs, out_specs=out_specs, check_vma=False)
```

```python
import math

import jax
import jax.numpy as jnp
import numpy as np
from jax import lax
from jax.experimental import pallas as pl
from jax.experimental.pallas import tpu as pltpu
from jax.sharding import PartitionSpec as P

MODES = 64
GAMMA = 1.4
KAPPA = 2.0

BAND = 16
SECTOR = 8
AXIAL = 256
LOAD_VMEM = 55_000_000
F32 = jnp.float32
ALL = range(5)


def primitives(q):
    inverse = 1.0 / q[0]
    ux, ur, ut = q[1] * inverse, q[2] * inverse, q[3] * inverse
    pressure = (GAMMA - 1.0) * (q[4] - 0.5 * (q[1] * ux + q[2] * ur + q[3] * ut))
    sound = jnp.sqrt(GAMMA * pressure * inverse)
    return ux, ur, ut, pressure, sound


def flux(q, prim, d):
    u, pressure = prim[d - 1], prim[3]
    f = [q[d], q[1] * u, q[2] * u, q[3] * u, (q[4] + pressure) * u]
    f[d] = f[d] + pressure
    return f, jnp.abs(u) + prim[4]


def face(left_q, left_flux, right_q, right_flux):
    (fl, sl), (fr, sr) = left_flux, right_flux
    fastest = jnp.maximum(sl, sr)
    return [(fl[v] + fr[v]) - fastest * (right_q[v] - left_q[v]) for v in ALL]


def roll(x, shift, axis):
    return pltpu.roll(x, shift % x.shape[axis], axis)


def axial_difference(q, prim, lane):
    f, speed = flux(q, prim, 1)
    axis = q[0].ndim - 1
    qn = [roll(x, -1, axis) for x in q]
    fn = [qn[1]] + [roll(f[v], -1, axis) for v in range(1, 5)]
    right = face(q, (f, speed), qn, (fn, roll(speed, -1, axis)))
    ends = [2.0 * x for x in f]
    right = [jnp.where(lane == AXIAL - 1, e, x) for e, x in zip(ends, right)]
    left = [jnp.where(lane == 0, e, roll(x, 1, axis)) for e, x in zip(ends, right)]
    return [a - b for a, b in zip(right, left)]


def advance(q, prim, half_source, axial, radial, swirl, inv_r, inv_h, spin_r, bladed, rotor):
    ux, ur, ut, pressure, sound = prim
    half_r = 0.5 * inv_r
    force = bladed * (q[0] * (ut - rotor * spin_r))
    gains = [
        None,
        None,
        half_r * (q[3] * ut + pressure),
        -force - half_r * (q[2] * ut),
        -ut * force,
    ]
    rate = jnp.abs(ux) + jnp.abs(ur) + jnp.abs(ut) * inv_h + sound * (2.0 + inv_h)
    weight = 1.0 / (rate + 7.5)
    out = []
    for v in ALL:
        total = half_source[v] - 0.25 * axial[v] - radial[v] - swirl[v]
        if gains[v] is not None:
            total = total + gains[v]
        out.append((rate * q[v] + total) * weight)
    return out


def geometry_table(rows, circle):
    mean = circle / (2.0 * math.pi)
    row = np.arange(-1, rows + 1, dtype=np.float64)
    radius = mean * (0.8 + 0.4 * (row + 0.5) / rows)
    inner = mean * (0.8 + 0.4 * row / rows)
    outer = mean * (0.8 + 0.4 * (row + 1.0) / rows)
    spacing = radius * (2.0 * math.pi / circle)
    spin = radius / (1.2 * mean)
    table = np.stack(
        [0.25 * outer / radius, 0.25 * inner / radius, 0.25 / spacing, 1.0 / radius, 1.0 / spacing, spin]
    )
    return table.astype(np.float32)


def edge_row(band, at_low, at_high):
    return jnp.where(band == 0, at_low, at_high)


MIRROR = (1.0, 1.0, -1.0, 1.0, 1.0)


def blades(blade_ref, rows):
    blade = blade_ref[...]
    bladed = jnp.broadcast_to((blade > 0).astype(F32), (rows, AXIAL))
    rotor = jnp.broadcast_to((blade == 1).astype(F32), (rows, AXIAL))
    return bladed, rotor


class Columns:
    def __init__(self, first_row, total_rows, circle):
        rows = (lax.broadcasted_iota(jnp.int32, (BAND, AXIAL), 0) + first_row).astype(F32)
        mean = circle / (2.0 * math.pi)
        radius = mean * (0.8 + 0.4 * (rows + 0.5) / total_rows)
        self.inner = mean * (0.8 + 0.4 * rows / total_rows)
        self.outer = mean * (0.8 + 0.4 * (rows + 1.0) / total_rows)
        self.inv_r = 1.0 / radius
        self.inv_h = self.inv_r * mean
        self.spin_r = radius * (1.0 / (1.2 * mean))
        self.a_h = 0.25 * self.inv_h


def load_kernel(q_ref, qp_ref, near_ref, q_out_ref, qp_out_ref, sems):
    edge = edge_row(lax.axis_index("rad"), BAND - 1, 0)
    copies = [
        pltpu.make_async_copy(q_ref.at[:, edge], near_ref, sems.at[0]),
        pltpu.make_async_copy(q_ref, q_out_ref, sems.at[1]),
        pltpu.make_async_copy(qp_ref, qp_out_ref, sems.at[2]),
    ]
    for copy in copies:
        copy.start()
    for copy in copies:
        copy.wait()


def edge_kernel(total_rows, circle, blade_ref, q_ref, qp_ref, edges_ref, ce):
    band = lax.axis_index("rad")
    low = band == 0
    geo = Columns(band * BAND, total_rows, circle)
    blade = blades(blade_ref, BAND)
    lane = lax.broadcasted_iota(jnp.int32, (BAND, AXIAL), 1)
    row = lax.broadcasted_iota(jnp.int32, (BAND, AXIAL), 0)
    below_scale = jnp.where((row == 0) & jnp.logical_not(low), 0.0, 0.25 * geo.inv_r * geo.inner)
    above_scale = jnp.where((row == BAND - 1) & low, 0.0, 0.25 * geo.inv_r * geo.outer)
    for side in (0, 1):
        at, inner = (0, 1) if side == 0 else (SECTOR - 1, SECTOR - 2)
        edge = [q_ref[v, :, at, :] for v in ALL]
        second = [q_ref[v, :, inner, :] for v in ALL]
        half_source = [10.0 * edge[v] - 2.5 * qp_ref[v, :, at, :] for v in ALL]
        for v in ALL:
            ce[v, side, 8:24] = edge[v]
            ce[v, side, 7:8] = MIRROR[v] * edge[v][0:1]
            ce[v, side, 24:25] = MIRROR[v] * edge[v][BAND - 1 : BAND]
        below = [ce[v, side, 7:23] for v in ALL]
        above = [ce[v, side, 9:25] for v in ALL]
        prim = primitives(edge)
        f = flux(edge, prim, 2)
        g_in = face(below, flux(below, primitives(below), 2), edge, f)
        g_out = face(edge, f, above, flux(above, primitives(above), 2))
        f = flux(edge, prim, 3)
        second_flux = flux(second, primitives(second), 3)
        if side == 0:
            swirl = [geo.a_h * x for x in face(edge, f, second, second_flux)]
        else:
            swirl = [-geo.a_h * x for x in face(second, second_flux, edge, f)]
        part = advance(
            edge,
            prim,
            half_source,
            axial_difference(edge, prim, lane),
            [above_scale * g_out[v] - below_scale * g_in[v] for v in ALL],
            swirl,
            geo.inv_r,
            geo.inv_h,
            geo.spin_r,
            *blade,
        )
        for v in ALL:
            edges_ref[v, side, 0:16] = edge[v]
            edges_ref[v, side, 16:32] = part[v]


def step_weight(prim, inv_h):
    ux, ur, ut, _, sound = prim
    return 1.0 / (jnp.abs(ux) + jnp.abs(ur) + jnp.abs(ut) * inv_h + sound * (2.0 + inv_h) + 7.5)


def pack_kernel(table_ref, edges_ref, rad_ref, core_ref, other_ref):
    odd = lax.axis_index("theta") % 2 == 1
    band = lax.axis_index("rad")
    low = band == 0
    edge_at = edge_row(band, BAND - 1, 0)
    g = band * BAND + edge_at + 1
    scale = jnp.where(low, -table_ref[0, g], table_ref[1, g])
    sides = []
    for side in (0, 1):
        at = 0 if side == 0 else SECTOR - 1
        edge = [edges_ref[v, side, pl.ds(edge_at, 1), :] for v in ALL]
        corner = [rad_ref[v, at : at + 1, :] for v in ALL]
        prim = primitives(edge)
        a, b = flux(edge, prim, 2), flux(corner, primitives(corner), 2)
        below = [jnp.where(low, edge[v], corner[v]) for v in ALL]
        above = [jnp.where(low, corner[v], edge[v]) for v in ALL]
        pick = lambda x, y: ([jnp.where(low, p, r) for p, r in zip(x[0], y[0])], jnp.where(low, x[1], y[1]))
        g_face = face(below, pick(a, b), above, pick(b, a))
        weight = scale * step_weight(prim, table_ref[4, g])
        sides.append((corner, [weight * x for x in g_face]))
    for v in ALL:
        for ref, flip in ((core_ref, jnp.logical_not(odd)), (other_ref, odd)):
            ref[v, 0:32] = jnp.where(flip, edges_ref[v, 1], edges_ref[v, 0])
            at = 16 + edge_at
            ref[v, pl.ds(at, 1), :] = ref[v, pl.ds(at, 1), :] + jnp.where(flip, sides[1][1][v], sides[0][1][v])
            ref[v, 32:40] = jnp.broadcast_to(jnp.where(flip, sides[1][0][v], sides[0][0][v]), (8, AXIAL))


def row_step(g, table_ref, q, prim, half_source, g_in, g_out, ends, masks, blade):
    lane, sub = masks
    f, speed = flux(q, prim, 3)
    qn = [roll(x, -1, 0) for x in q]
    fn = [qn[3]] + [roll(f[v], -1, 0) for v in range(1, 5)]
    between = face(q, (f, speed), qn, (fn, roll(speed, -1, 0)))
    a_out, a_in, a_h = table_ref[0, g], table_ref[1, g], table_ref[2, g]
    swirl = []
    for v in ALL:
        end = 0.0 if ends is None else ends[v]
        right = jnp.where(sub == SECTOR - 1, end, between[v])
        left = jnp.where(sub == 0, end, roll(between[v], 1, 0))
        swirl.append(a_h * (right - left))
    radial = [a_out * g_out[v] - a_in * g_in[v] for v in ALL]
    return advance(
        q,
        prim,
        half_source,
        axial_difference(q, prim, lane),
        radial,
        swirl,
        table_ref[3, g],
        table_ref[4, g],
        table_ref[5, g],
        *blade,
    )


def sweep(load, step, store):
    below = load(-1)
    below_prim = primitives(below)
    q = load(0)
    prim = primitives(q)
    g_in = face(below, flux(below, below_prim, 2), q, flux(q, prim, 2))

    def body(j, carry):
        q, prim, g_in = carry
        above = load(j + 1)
        above_prim = primitives(above)
        g_out = face(q, flux(q, prim, 2), above, flux(above, above_prim, 2))
        store(j, step(j, q, prim, g_in, g_out))
        return above, above_prim, g_out

    lax.fori_loop(0, BAND, body, (q, prim, g_in), unroll=4)


def early_kernel(table_ref, blade_ref, q_ref, qp_ref, rad_ref, p1_ref, edge_ref, hs_ref, p0):
    band = lax.axis_index("rad")
    first_row = band * BAND
    masks = (
        lax.broadcasted_iota(jnp.int32, (SECTOR, AXIAL), 1),
        lax.broadcasted_iota(jnp.int32, (SECTOR, AXIAL), 0),
    )
    blade = blades(blade_ref, SECTOR)
    near_at = edge_row(band, BAND + 1, 0)
    wall_at = edge_row(band, 0, BAND + 1)
    wall_row = edge_row(band, 0, BAND - 1)
    for v in ALL:
        p0[v, 1 : BAND + 1] = q_ref[v]
        p0[v, near_at] = rad_ref[v]
        p0[v, wall_at] = MIRROR[v] * q_ref[v, wall_row]
        hs_ref[v] = 10.0 * q_ref[v] - 2.5 * qp_ref[v]

    def store(j, q):
        for v in ALL:
            p1_ref[v, j] = q[v]

    sweep(
        lambda j: [p0[v, j + 1] for v in ALL],
        lambda j, q, prim, g_in, g_out: row_step(
            first_row + j + 1, table_ref, q, prim, [hs_ref[v, j] for v in ALL], g_in, g_out, None, masks, blade
        ),
        store,
    )
    for v in ALL:
        edge_ref[v] = p1_ref[v, edge_row(band, BAND - 1, 0)]


def final_kernel(
    total_rows,
    circle,
    table_ref,
    blade_ref,
    q_ref,
    rad_ref,
    p1_ref,
    hs_ref,
    next_ref,
    other_ref,
    core_ref,
    flow_ref,
    send_ref,
    p1,
    ends,
    fields,
):
    odd = lax.axis_index("theta") % 2 == 1
    band = lax.axis_index("rad")
    first_row = band * BAND
    near_at = edge_row(band, BAND + 1, 0)
    wall_at = edge_row(band, 0, BAND + 1)
    wall_row = edge_row(band, 0, BAND - 1)
    masks = (
        lax.broadcasted_iota(jnp.int32, (SECTOR, AXIAL), 1),
        lax.broadcasted_iota(jnp.int32, (SECTOR, AXIAL), 0),
    )
    for v in ALL:
        p1[v, 1 : BAND + 1] = p1_ref[v]
        p1[v, near_at] = next_ref[v]

    geo = Columns(first_row, total_rows, circle)
    g_near = first_row + near_at

    for side in (0, 1):
        use_core = odd if side == 0 else jnp.logical_not(odd)
        at = 0 if side == 0 else SECTOR - 1
        sign = 1.0 if side == 0 else -1.0

        def pick(lo, hi):
            return [jnp.where(use_core, core_ref[v, lo:hi], other_ref[v, lo:hi]) for v in ALL]

        def ordered(halo, halo_prim, own, own_prim):
            a, b = flux(halo, halo_prim, 3), flux(own, own_prim, 3)
            return face(halo, a, own, b) if side == 0 else face(own, b, halo, a)

        near, near_part, corner = pick(0, 16), pick(16, 32), pick(32, 33)
        own = [q_ref[v, :, at, :] for v in ALL]
        own_prim, near_prim = primitives(own), primitives(near)
        shared = ordered(near, near_prim, own, own_prim)
        own_scale = (sign * geo.a_h) * step_weight(own_prim, geo.inv_h)
        near_scale = (-sign * geo.a_h) * step_weight(near_prim, geo.inv_h)
        own_next = [p1_ref[v, :, at, :] + own_scale * shared[v] for v in ALL]
        near_next = [near_part[v] + near_scale * shared[v] for v in ALL]

        edge = [rad_ref[v, at : at + 1, :] for v in ALL]
        edge_prim = primitives(edge)
        corner_face = ordered(corner, primitives(corner), edge, edge_prim)
        corner_scale = (sign * table_ref[2, g_near]) * step_weight(edge_prim, table_ref[4, g_near])

        faces = ordered(near_next, primitives(near_next), own_next, primitives(own_next))
        for v in ALL:
            p1[v, 1 : BAND + 1, at, :] = own_next[v]
            p1[v, near_at, at : at + 1, :] = next_ref[v, at : at + 1, :] + corner_scale * corner_face[v]
            ends[v, :, at, :] = faces[v]

    for v in ALL:
        p1[v, wall_at] = MIRROR[v] * p1[v, wall_row + 1]

    def store(j, q):
        for v in ALL:
            flow_ref[v, j] = q[v]
        ux, _, _, pressure, _ = primitives(q)
        fields[0, j] = pressure
        fields[1, j] = ux

    blade = blades(blade_ref, SECTOR)
    sweep(
        lambda j: [p1[v, j + 1] for v in ALL],
        lambda j, q, prim, g_in, g_out: row_step(
            first_row + j + 1,
            table_ref,
            q,
            prim,
            [hs_ref[v, j] for v in ALL],
            g_in,
            g_out,
            [ends[v, j] for v in ALL],
            masks,
            blade,
        ),
        store,
    )
    for f in (0, 1):
        turned = fields[f].reshape(BAND * SECTOR, AXIAL).T
        send_ref[pl.ds(f, AXIAL, stride=2), :] = turned


def mode_kernel(got_ref, basis_ref, flow_ref, out_ref, flow_out_ref, turned, sem):
    copy = pltpu.make_async_copy(flow_ref, flow_out_ref, sem)
    copy.start()
    sectors = got_ref.shape[0] // 4
    parts = []
    for e in (0, 1):
        for f in (0, 1):
            n = 2 * e + f
            turned[n] = got_ref[pl.ds(n, sectors, stride=4), :].T
            parts.append(
                jnp.concatenate([turned[n, pl.ds(m, BAND, stride=SECTOR), :] for m in range(SECTOR)], axis=1)
            )
    product = jnp.dot(
        jnp.concatenate(parts, axis=0), basis_ref[...], precision=lax.Precision.HIGHEST, preferred_element_type=F32
    )
    for e in (0, 1):
        for f in (0, 1):
            n = 2 * e + f
            out_ref[e, :, 2 * MODES * f : 2 * MODES * (f + 1)] = product[BAND * n : BAND * (n + 1)]
    copy.wait()


def mode_basis(sectors):
    circle = sectors * SECTOR
    cell = (np.arange(SECTOR)[:, None] + SECTOR * np.arange(sectors)[None, :]).reshape(-1)
    phase = (cell[:, None] * np.arange(1, MODES + 1)[None, :] % circle) * (2.0 * np.pi / circle)
    return (np.concatenate([np.cos(phase), -np.sin(phase)], axis=1) / np.sqrt(circle)).astype(np.float32)


def shaped(*shape):
    return jax.ShapeDtypeStruct(shape, F32)


def vmem():
    return pl.BlockSpec(memory_space=pltpu.VMEM)


def limit(mib):
    return pltpu.CompilerParams(vmem_limit_bytes=int(mib * 2**20))


def per_device(q_level, q_prev, blade_row):
    sectors = lax.axis_size("theta")
    bands = lax.axis_size("rad")
    circle = sectors * SECTOR
    core = [(t, t ^ 1) for t in range(sectors)]
    other = [(t, (((t + 1) ^ 1) - 1) % sectors) for t in range(sectors)]
    table = jnp.asarray(geometry_table(bands * BAND, circle))
    blade = blade_row.reshape(1, AXIAL)
    smem = pl.BlockSpec(memory_space=pltpu.SMEM)

    hbm = pl.BlockSpec(memory_space=pltpu.HBM)
    swap = [(0, 1), (1, 0)]

    def edges(*refs):
        edge_kernel(bands * BAND, circle, *refs)

    def final(*refs):
        final_kernel(bands * BAND, circle, *refs)

    near, q_level, q_prev = pl.pallas_call(
        load_kernel,
        out_shape=[
            shaped(5, SECTOR, AXIAL),
            shaped(5, BAND, SECTOR, AXIAL),
            shaped(5, BAND, SECTOR, AXIAL),
        ],
        in_specs=[hbm] * 2,
        out_specs=[vmem()] * 3,
        scratch_shapes=[pltpu.SemaphoreType.DMA((3,))],
        compiler_params=pltpu.CompilerParams(vmem_limit_bytes=LOAD_VMEM),
    )(q_level, q_prev)
    rad_in = lax.ppermute(near, "rad", swap)
    edge_columns = pl.pallas_call(
        edges,
        out_shape=shaped(5, 2, 32, AXIAL),
        in_specs=[vmem()] * 3,
        out_specs=vmem(),
        scratch_shapes=[pltpu.VMEM((5, 2, 32, AXIAL), F32)],
        compiler_params=limit(4),
        cost_estimate=pl.CostEstimate(flops=5_000_000, bytes_accessed=2_000_000, transcendentals=50_000),
    )(blade, q_level, q_prev)
    core_out, other_out = pl.pallas_call(
        pack_kernel,
        out_shape=[shaped(5, 40, AXIAL)] * 2,
        in_specs=[smem] + [vmem()] * 2,
        out_specs=[vmem()] * 2,
        compiler_params=limit(4),
    )(table, edge_columns, rad_in)
    core_in = lax.ppermute(core_out, "theta", core)
    other_in = lax.ppermute(other_out, "theta", other)
    part, edge, half_source = pl.pallas_call(
        early_kernel,
        out_shape=[shaped(5, BAND, SECTOR, AXIAL), shaped(5, SECTOR, AXIAL), shaped(5, BAND, SECTOR, AXIAL)],
        in_specs=[smem] + [vmem()] * 4,
        out_specs=[vmem()] * 3,
        scratch_shapes=[pltpu.VMEM((5, BAND + 2, SECTOR, AXIAL), F32)],
        compiler_params=limit(8),
        cost_estimate=pl.CostEstimate(flops=10_000_000, bytes_accessed=3_500_000, transcendentals=100_000),
    )(table, blade, q_level, q_prev, rad_in)
    next_in = lax.ppermute(edge, "rad", swap)
    flow_state, send = pl.pallas_call(
        final,
        out_shape=[shaped(5, BAND, SECTOR, AXIAL), shaped(2 * AXIAL, BAND * SECTOR)],
        in_specs=[smem] + [vmem()] * 8,
        out_specs=[vmem()] * 2,
        scratch_shapes=[
            pltpu.VMEM((5, BAND + 2, SECTOR, AXIAL), F32),
            pltpu.VMEM((5, BAND, SECTOR, AXIAL), F32),
            pltpu.VMEM((2, BAND, SECTOR, AXIAL), F32),
        ],
        compiler_params=limit(8),
    )(table, blade, q_level, rad_in, part, half_source, next_in, other_in, core_in)
    got = lax.all_to_all(send.reshape(sectors, 4, 128), "theta", split_axis=0, concat_axis=0, tiled=True)
    spectra, flow_state = pl.pallas_call(
        mode_kernel,
        out_shape=[shaped(2, BAND, 4 * MODES), shaped(5, BAND, SECTOR, AXIAL)],
        in_specs=[vmem()] * 3,
        out_specs=[vmem(), hbm],
        scratch_shapes=[pltpu.VMEM((4, BAND * SECTOR, sectors), F32), pltpu.SemaphoreType.DMA],
        compiler_params=limit(4),
    )(got.reshape(4 * sectors, 128), jnp.asarray(mode_basis(sectors)), flow_state)
    return flow_state, spectra


def solution(mesh):
    in_specs = (P(None, "rad", "theta", None), P(None, "rad", "theta", None), P())
    out_specs = (P(None, "rad", "theta", None), P("theta", "rad", None))
    return jax.shard_map(per_device, mesh=mesh, in_specs=in_specs, out_specs=out_specs, check_vma=False)
```

```python
import math

import jax
import jax.numpy as jnp
import numpy as np
from jax import lax
from jax.experimental import pallas as pl
from jax.experimental.pallas import tpu as pltpu
from jax.sharding import PartitionSpec as P

MODES = 64
GAMMA = 1.4
KAPPA = 2.0

BAND = 16
SECTOR = 8
AXIAL = 256
RAD_VMEM = 56_200_000
LOAD_VMEM = 55_000_000
F32 = jnp.float32
ALL = range(5)


def primitives(q):
    inverse = 1.0 / q[0]
    ux, ur, ut = q[1] * inverse, q[2] * inverse, q[3] * inverse
    pressure = (GAMMA - 1.0) * (q[4] - 0.5 * (q[1] * ux + q[2] * ur + q[3] * ut))
    sound = jnp.sqrt(GAMMA * pressure * inverse)
    return ux, ur, ut, pressure, sound


def flux(q, prim, d):
    u, pressure = prim[d - 1], prim[3]
    f = [q[d], q[1] * u, q[2] * u, q[3] * u, (q[4] + pressure) * u]
    f[d] = f[d] + pressure
    return f, jnp.abs(u) + prim[4]


def face(left_q, left_flux, right_q, right_flux):
    (fl, sl), (fr, sr) = left_flux, right_flux
    fastest = jnp.maximum(sl, sr)
    return [(fl[v] + fr[v]) - fastest * (right_q[v] - left_q[v]) for v in ALL]


def roll(x, shift, axis):
    return pltpu.roll(x, shift % x.shape[axis], axis)


def axial_difference(q, prim, lane):
    f, speed = flux(q, prim, 1)
    axis = q[0].ndim - 1
    qn = [roll(x, -1, axis) for x in q]
    fn = [qn[1]] + [roll(f[v], -1, axis) for v in range(1, 5)]
    right = face(q, (f, speed), qn, (fn, roll(speed, -1, axis)))
    ends = [2.0 * x for x in f]
    right = [jnp.where(lane == AXIAL - 1, e, x) for e, x in zip(ends, right)]
    left = [jnp.where(lane == 0, e, roll(x, 1, axis)) for e, x in zip(ends, right)]
    return [a - b for a, b in zip(right, left)]


def advance(q, prim, half_source, axial, radial, swirl, inv_r, inv_h, spin_r, bladed, rotor):
    ux, ur, ut, pressure, sound = prim
    half_r = 0.5 * inv_r
    force = bladed * (q[0] * (ut - rotor * spin_r))
    gains = [
        None,
        None,
        half_r * (q[3] * ut + pressure),
        -force - half_r * (q[2] * ut),
        -ut * force,
    ]
    rate = jnp.abs(ux) + jnp.abs(ur) + jnp.abs(ut) * inv_h + sound * (2.0 + inv_h)
    weight = 1.0 / (rate + 7.5)
    out = []
    for v in ALL:
        total = half_source[v] - 0.25 * axial[v] - radial[v] - swirl[v]
        if gains[v] is not None:
            total = total + gains[v]
        out.append((rate * q[v] + total) * weight)
    return out


def geometry_table(rows, circle):
    mean = circle / (2.0 * math.pi)
    row = np.arange(-1, rows + 1, dtype=np.float64)
    radius = mean * (0.8 + 0.4 * (row + 0.5) / rows)
    inner = mean * (0.8 + 0.4 * row / rows)
    outer = mean * (0.8 + 0.4 * (row + 1.0) / rows)
    spacing = radius * (2.0 * math.pi / circle)
    spin = radius / (1.2 * mean)
    table = np.stack(
        [0.25 * outer / radius, 0.25 * inner / radius, 0.25 / spacing, 1.0 / radius, 1.0 / spacing, spin]
    )
    return table.astype(np.float32)


def edge_row(band, at_low, at_high):
    return jnp.where(band == 0, at_low, at_high)


MIRROR = (1.0, 1.0, -1.0, 1.0, 1.0)


def blades(blade_ref, rows):
    blade = blade_ref[...]
    bladed = jnp.broadcast_to((blade > 0).astype(F32), (rows, AXIAL))
    rotor = jnp.broadcast_to((blade == 1).astype(F32), (rows, AXIAL))
    return bladed, rotor


class Columns:
    def __init__(self, first_row, total_rows, circle):
        rows = (lax.broadcasted_iota(jnp.int32, (BAND, AXIAL), 0) + first_row).astype(F32)
        mean = circle / (2.0 * math.pi)
        radius = mean * (0.8 + 0.4 * (rows + 0.5) / total_rows)
        self.inner = mean * (0.8 + 0.4 * rows / total_rows)
        self.outer = mean * (0.8 + 0.4 * (rows + 1.0) / total_rows)
        self.inv_r = 1.0 / radius
        self.inv_h = self.inv_r * mean
        self.spin_r = radius * (1.0 / (1.2 * mean))
        self.a_h = 0.25 * self.inv_h


def rad_kernel(q_ref, near_ref, sem):
    copy = pltpu.make_async_copy(q_ref.at[:, edge_row(lax.axis_index("rad"), BAND - 1, 0)], near_ref, sem)
    copy.start()
    copy.wait()


def load_kernel(q_ref, qp_ref, q_out_ref, qp_out_ref, sems):
    copies = [
        pltpu.make_async_copy(q_ref, q_out_ref, sems.at[0]),
        pltpu.make_async_copy(qp_ref, qp_out_ref, sems.at[1]),
    ]
    for copy in copies:
        copy.start()
    for copy in copies:
        copy.wait()


def edge_kernel(total_rows, circle, blade_ref, q_ref, qp_ref, edges_ref, ce, taken):
    band = lax.axis_index("rad")
    low = band == 0
    geo = Columns(band * BAND, total_rows, circle)
    blade = blades(blade_ref, BAND)
    lane = lax.broadcasted_iota(jnp.int32, (BAND, AXIAL), 1)
    row = lax.broadcasted_iota(jnp.int32, (BAND, AXIAL), 0)
    below_scale = jnp.where((row == 0) & jnp.logical_not(low), 0.0, 0.25 * geo.inv_r * geo.inner)
    above_scale = jnp.where((row == BAND - 1) & low, 0.0, 0.25 * geo.inv_r * geo.outer)
    for side in (0, 1):
        at, inner = (0, 1) if side == 0 else (SECTOR - 1, SECTOR - 2)
        for v in ALL:
            ce[v, side, 8:24] = q_ref[v, :, at, :]
            taken[v, side, 0] = q_ref[v, :, inner, :]
            taken[v, side, 1] = qp_ref[v, :, at, :]
    for side in (0, 1):
        edge = [ce[v, side, 8:24] for v in ALL]
        second = [taken[v, side, 0] for v in ALL]
        half_source = [10.0 * edge[v] - 2.5 * taken[v, side, 1] for v in ALL]
        for v in ALL:
            ce[v, side, 7:8] = MIRROR[v] * edge[v][0:1]
            ce[v, side, 24:25] = MIRROR[v] * edge[v][BAND - 1 : BAND]
        below = [ce[v, side, 7:23] for v in ALL]
        above = [ce[v, side, 9:25] for v in ALL]
        prim = primitives(edge)
        f = flux(edge, prim, 2)
        g_in = face(below, flux(below, primitives(below), 2), edge, f)
        g_out = face(edge, f, above, flux(above, primitives(above), 2))
        f = flux(edge, prim, 3)
        second_flux = flux(second, primitives(second), 3)
        if side == 0:
            swirl = [geo.a_h * x for x in face(edge, f, second, second_flux)]
        else:
            swirl = [-geo.a_h * x for x in face(second, second_flux, edge, f)]
        part = advance(
            edge,
            prim,
            half_source,
            axial_difference(edge, prim, lane),
            [above_scale * g_out[v] - below_scale * g_in[v] for v in ALL],
            swirl,
            geo.inv_r,
            geo.inv_h,
            geo.spin_r,
            *blade,
        )
        for v in ALL:
            edges_ref[v, side, 0:16] = edge[v]
            edges_ref[v, side, 16:32] = part[v]


def step_weight(prim, inv_h):
    ux, ur, ut, _, sound = prim
    return 1.0 / (jnp.abs(ux) + jnp.abs(ur) + jnp.abs(ut) * inv_h + sound * (2.0 + inv_h) + 7.5)


def pack_kernel(table_ref, edges_ref, rad_ref, own_ref, core_ref, other_ref):
    odd = lax.axis_index("theta") % 2 == 1
    band = lax.axis_index("rad")
    low = band == 0
    edge_at = edge_row(band, BAND - 1, 0)
    g = band * BAND + edge_at + 1
    scale = jnp.where(low, -table_ref[0, g], table_ref[1, g])
    sides = []
    for side in (0, 1):
        at = 0 if side == 0 else SECTOR - 1
        edge = [edges_ref[v, side, pl.ds(edge_at, 1), :] for v in ALL]
        corner = [rad_ref[v, at : at + 1, :] for v in ALL]
        prim = primitives(edge)
        a, b = flux(edge, prim, 2), flux(corner, primitives(corner), 2)
        below = [jnp.where(low, edge[v], corner[v]) for v in ALL]
        above = [jnp.where(low, corner[v], edge[v]) for v in ALL]
        pick = lambda x, y: ([jnp.where(low, p, r) for p, r in zip(x[0], y[0])], jnp.where(low, x[1], y[1]))
        g_face = face(below, pick(a, b), above, pick(b, a))
        weight = scale * step_weight(prim, table_ref[4, g])
        sides.append((corner, [weight * x for x in g_face]))
    for v in ALL:
        for side in (0, 1):
            own_ref[v, side] = edges_ref[v, side, 16:32]
            own_ref[v, side, pl.ds(edge_at, 1), :] = edges_ref[v, side, pl.ds(16 + edge_at, 1), :] + sides[side][1][v]
        for ref, flip in ((core_ref, jnp.logical_not(odd)), (other_ref, odd)):
            at = 32 * v
            ref[at : at + 16] = jnp.where(flip, edges_ref[v, 1, 0:16], edges_ref[v, 0, 0:16])
            ref[at + 16 : at + 32] = jnp.where(flip, own_ref[v, 1], own_ref[v, 0])
            ref[160 + v : 161 + v] = jnp.where(flip, sides[1][0][v], sides[0][0][v])


def row_step(g, table_ref, q, prim, half_source, g_in, g_out, ends, masks, blade):
    lane, sub = masks
    f, speed = flux(q, prim, 3)
    qn = [roll(x, -1, 0) for x in q]
    fn = [qn[3]] + [roll(f[v], -1, 0) for v in range(1, 5)]
    between = face(q, (f, speed), qn, (fn, roll(speed, -1, 0)))
    a_out, a_in, a_h = table_ref[0, g], table_ref[1, g], table_ref[2, g]
    swirl = []
    for v in ALL:
        end = 0.0 if ends is None else ends[v]
        right = jnp.where(sub == SECTOR - 1, end, between[v])
        left = jnp.where(sub == 0, end, roll(between[v], 1, 0))
        swirl.append(a_h * (right - left))
    radial = [a_out * g_out[v] - a_in * g_in[v] for v in ALL]
    return advance(
        q,
        prim,
        half_source,
        axial_difference(q, prim, lane),
        radial,
        swirl,
        table_ref[3, g],
        table_ref[4, g],
        table_ref[5, g],
        *blade,
    )


def sweep(load, step, store):
    below = load(-1)
    below_prim = primitives(below)
    q = load(0)
    prim = primitives(q)
    g_in = face(below, flux(below, below_prim, 2), q, flux(q, prim, 2))

    def body(j, carry):
        q, prim, g_in = carry
        above = load(j + 1)
        above_prim = primitives(above)
        g_out = face(q, flux(q, prim, 2), above, flux(above, above_prim, 2))
        store(j, step(j, q, prim, g_in, g_out))
        return above, above_prim, g_out

    lax.fori_loop(0, BAND, body, (q, prim, g_in), unroll=4)


def early_kernel(table_ref, blade_ref, q_ref, qp_ref, rad_ref, p1_ref, edge_ref, hs_ref, p0):
    band = lax.axis_index("rad")
    first_row = band * BAND
    masks = (
        lax.broadcasted_iota(jnp.int32, (SECTOR, AXIAL), 1),
        lax.broadcasted_iota(jnp.int32, (SECTOR, AXIAL), 0),
    )
    blade = blades(blade_ref, SECTOR)
    near_at = edge_row(band, BAND + 1, 0)
    wall_at = edge_row(band, 0, BAND + 1)
    wall_row = edge_row(band, 0, BAND - 1)
    for v in ALL:
        p0[v, 1 : BAND + 1] = q_ref[v]
        p0[v, near_at] = rad_ref[v]
        p0[v, wall_at] = MIRROR[v] * q_ref[v, wall_row]
        hs_ref[v] = 10.0 * q_ref[v] - 2.5 * qp_ref[v]

    def store(j, q):
        for v in ALL:
            p1_ref[v, j] = q[v]

    sweep(
        lambda j: [p0[v, j + 1] for v in ALL],
        lambda j, q, prim, g_in, g_out: row_step(
            first_row + j + 1, table_ref, q, prim, [hs_ref[v, j] for v in ALL], g_in, g_out, None, masks, blade
        ),
        store,
    )
    for v in ALL:
        edge_ref[v] = p1_ref[v, edge_row(band, BAND - 1, 0)]


def final_kernel(
    total_rows,
    circle,
    table_ref,
    blade_ref,
    edges_ref,
    own_ref,
    rad_ref,
    p1_ref,
    hs_ref,
    next_ref,
    other_ref,
    core_ref,
    flow_ref,
    send_ref,
    p1,
    ends,
    fields,
):
    odd = lax.axis_index("theta") % 2 == 1
    band = lax.axis_index("rad")
    first_row = band * BAND
    near_at = edge_row(band, BAND + 1, 0)
    wall_at = edge_row(band, 0, BAND + 1)
    wall_row = edge_row(band, 0, BAND - 1)
    masks = (
        lax.broadcasted_iota(jnp.int32, (SECTOR, AXIAL), 1),
        lax.broadcasted_iota(jnp.int32, (SECTOR, AXIAL), 0),
    )
    for v in ALL:
        p1[v, 1 : BAND + 1] = p1_ref[v]
        p1[v, near_at] = next_ref[v]

    geo = Columns(first_row, total_rows, circle)
    g_near = first_row + near_at

    for side in (0, 1):
        use_core = odd if side == 0 else jnp.logical_not(odd)
        at = 0 if side == 0 else SECTOR - 1
        sign = 1.0 if side == 0 else -1.0

        def pick(first, step, count):
            spans = [slice(first + step * v, first + step * v + count) for v in ALL]
            return [jnp.where(use_core, core_ref[span], other_ref[span]) for span in spans]

        def ordered(halo, halo_prim, own, own_prim):
            a, b = flux(halo, halo_prim, 3), flux(own, own_prim, 3)
            return face(halo, a, own, b) if side == 0 else face(own, b, halo, a)

        near, near_part, corner = pick(0, 32, 16), pick(16, 32, 16), pick(160, 1, 1)
        own = [edges_ref[v, side, 0:16] for v in ALL]
        own_prim, near_prim = primitives(own), primitives(near)
        shared = ordered(near, near_prim, own, own_prim)
        own_scale = (sign * geo.a_h) * step_weight(own_prim, geo.inv_h)
        near_scale = (-sign * geo.a_h) * step_weight(near_prim, geo.inv_h)
        own_next = [own_ref[v, side] + own_scale * shared[v] for v in ALL]
        near_next = [near_part[v] + near_scale * shared[v] for v in ALL]

        edge = [rad_ref[v, at : at + 1, :] for v in ALL]
        edge_prim = primitives(edge)
        corner_face = ordered(corner, primitives(corner), edge, edge_prim)
        corner_scale = (sign * table_ref[2, g_near]) * step_weight(edge_prim, table_ref[4, g_near])

        faces = ordered(near_next, primitives(near_next), own_next, primitives(own_next))
        for v in ALL:
            p1[v, 1 : BAND + 1, at, :] = own_next[v]
            p1[v, near_at, at : at + 1, :] = next_ref[v, at : at + 1, :] + corner_scale * corner_face[v]
            ends[v, :, at, :] = faces[v]

    for v in ALL:
        p1[v, wall_at] = MIRROR[v] * p1[v, wall_row + 1]

    def store(j, q):
        for v in ALL:
            flow_ref[v, j] = q[v]
        ux, _, _, pressure, _ = primitives(q)
        fields[0, j] = pressure
        fields[1, j] = ux

    blade = blades(blade_ref, SECTOR)
    sweep(
        lambda j: [p1[v, j + 1] for v in ALL],
        lambda j, q, prim, g_in, g_out: row_step(
            first_row + j + 1,
            table_ref,
            q,
            prim,
            [hs_ref[v, j] for v in ALL],
            g_in,
            g_out,
            [ends[v, j] for v in ALL],
            masks,
            blade,
        ),
        store,
    )
    for f in (0, 1):
        turned = fields[f].reshape(BAND * SECTOR, AXIAL).T
        send_ref[pl.ds(f, AXIAL, stride=2), :] = turned


def mode_kernel(got_ref, basis_ref, flow_ref, out_ref, flow_out_ref, turned, sem):
    copy = pltpu.make_async_copy(flow_ref, flow_out_ref, sem)
    copy.start()
    sectors = got_ref.shape[0] // 4
    parts = []
    for e in (0, 1):
        for f in (0, 1):
            n = 2 * e + f
            turned[n] = got_ref[pl.ds(n, sectors, stride=4), :].T
            parts.append(
                jnp.concatenate([turned[n, pl.ds(m, BAND, stride=SECTOR), :] for m in range(SECTOR)], axis=1)
            )
    product = jnp.dot(
        jnp.concatenate(parts, axis=0), basis_ref[...], precision=lax.Precision.HIGHEST, preferred_element_type=F32
    )
    for e in (0, 1):
        for f in (0, 1):
            n = 2 * e + f
            out_ref[e, :, 2 * MODES * f : 2 * MODES * (f + 1)] = product[BAND * n : BAND * (n + 1)]
    copy.wait()


def mode_basis(sectors):
    circle = sectors * SECTOR
    cell = (np.arange(SECTOR)[:, None] + SECTOR * np.arange(sectors)[None, :]).reshape(-1)
    phase = (cell[:, None] * np.arange(1, MODES + 1)[None, :] % circle) * (2.0 * np.pi / circle)
    return (np.concatenate([np.cos(phase), -np.sin(phase)], axis=1) / np.sqrt(circle)).astype(np.float32)


def shaped(*shape):
    return jax.ShapeDtypeStruct(shape, F32)


def vmem():
    return pl.BlockSpec(memory_space=pltpu.VMEM)


def limit(mib):
    return pltpu.CompilerParams(vmem_limit_bytes=int(mib * 2**20))


def per_device(q_level, q_prev, blade_row):
    sectors = lax.axis_size("theta")
    bands = lax.axis_size("rad")
    circle = sectors * SECTOR
    core = [(t, t ^ 1) for t in range(sectors)]
    other = [(t, (((t + 1) ^ 1) - 1) % sectors) for t in range(sectors)]
    table = jnp.asarray(geometry_table(bands * BAND, circle))
    blade = blade_row.reshape(1, AXIAL)
    smem = pl.BlockSpec(memory_space=pltpu.SMEM)

    hbm = pl.BlockSpec(memory_space=pltpu.HBM)
    swap = [(0, 1), (1, 0)]

    def edges(*refs):
        edge_kernel(bands * BAND, circle, *refs)

    def final(*refs):
        final_kernel(bands * BAND, circle, *refs)

    near = pl.pallas_call(
        rad_kernel,
        out_shape=shaped(5, SECTOR, AXIAL),
        in_specs=[hbm],
        out_specs=vmem(),
        scratch_shapes=[pltpu.SemaphoreType.DMA],
        compiler_params=pltpu.CompilerParams(vmem_limit_bytes=RAD_VMEM),
    )(q_level)
    rad_in = lax.ppermute(near, "rad", swap)
    q_level, q_prev = pl.pallas_call(
        load_kernel,
        out_shape=[shaped(5, BAND, SECTOR, AXIAL)] * 2,
        in_specs=[hbm] * 2,
        out_specs=[vmem()] * 2,
        scratch_shapes=[pltpu.SemaphoreType.DMA((2,))],
        compiler_params=pltpu.CompilerParams(vmem_limit_bytes=LOAD_VMEM),
        cost_estimate=pl.CostEstimate(flops=0, bytes_accessed=3_000_000, transcendentals=0),
    )(q_level, q_prev)
    edge_columns = pl.pallas_call(
        edges,
        out_shape=shaped(5, 2, 32, AXIAL),
        in_specs=[vmem()] * 3,
        out_specs=vmem(),
        scratch_shapes=[pltpu.VMEM((5, 2, 32, AXIAL), F32), pltpu.VMEM((5, 2, 2, BAND, AXIAL), F32)],
        compiler_params=limit(4),
        cost_estimate=pl.CostEstimate(flops=5_000_000, bytes_accessed=2_000_000, transcendentals=50_000),
    )(blade, q_level, q_prev)
    own_columns, core_out, other_out = pl.pallas_call(
        pack_kernel,
        out_shape=[shaped(5, 2, BAND, AXIAL)] + [shaped(168, AXIAL)] * 2,
        in_specs=[smem] + [vmem()] * 2,
        out_specs=[vmem()] * 3,
        compiler_params=limit(4),
    )(table, edge_columns, rad_in)
    core_in = lax.ppermute(core_out, "theta", core)
    other_in = lax.ppermute(other_out, "theta", other)
    part, edge, half_source = pl.pallas_call(
        early_kernel,
        out_shape=[shaped(5, BAND, SECTOR, AXIAL), shaped(5, SECTOR, AXIAL), shaped(5, BAND, SECTOR, AXIAL)],
        in_specs=[smem] + [vmem()] * 4,
        out_specs=[vmem()] * 3,
        scratch_shapes=[pltpu.VMEM((5, BAND + 2, SECTOR, AXIAL), F32)],
        compiler_params=limit(8),
        cost_estimate=pl.CostEstimate(flops=10_000_000, bytes_accessed=3_500_000, transcendentals=100_000),
    )(table, blade, q_level, q_prev, rad_in)
    next_in = lax.ppermute(edge, "rad", swap)
    flow_state, send = pl.pallas_call(
        final,
        out_shape=[shaped(5, BAND, SECTOR, AXIAL), shaped(2 * AXIAL, BAND * SECTOR)],
        in_specs=[smem] + [vmem()] * 9,
        out_specs=[vmem()] * 2,
        scratch_shapes=[
            pltpu.VMEM((5, BAND + 2, SECTOR, AXIAL), F32),
            pltpu.VMEM((5, BAND, SECTOR, AXIAL), F32),
            pltpu.VMEM((2, BAND, SECTOR, AXIAL), F32),
        ],
        compiler_params=limit(8),
    )(table, blade, edge_columns, own_columns, rad_in, part, half_source, next_in, other_in, core_in)
    got = lax.all_to_all(send.reshape(sectors, 4, 128), "theta", split_axis=0, concat_axis=0, tiled=True)
    spectra, flow_state = pl.pallas_call(
        mode_kernel,
        out_shape=[shaped(2, BAND, 4 * MODES), shaped(5, BAND, SECTOR, AXIAL)],
        in_specs=[vmem()] * 3,
        out_specs=[vmem(), hbm],
        scratch_shapes=[pltpu.VMEM((4, BAND * SECTOR, sectors), F32), pltpu.SemaphoreType.DMA],
        compiler_params=limit(4),
    )(got.reshape(4 * sectors, 128), jnp.asarray(mode_basis(sectors)), flow_state)
    return flow_state, spectra


def solution(mesh):
    in_specs = (P(None, "rad", "theta", None), P(None, "rad", "theta", None), P())
    out_specs = (P(None, "rad", "theta", None), P("theta", "rad", None))
    return jax.shard_map(per_device, mesh=mesh, in_specs=in_specs, out_specs=out_specs, check_vma=False)
```

```python
import math

import jax
import jax.numpy as jnp
import numpy as np
from jax import lax
from jax.experimental import pallas as pl
from jax.experimental.pallas import tpu as pltpu
from jax.sharding import PartitionSpec as P

MODES = 64
GAMMA = 1.4
KAPPA = 2.0

BAND = 16
SECTOR = 8
AXIAL = 256
RAD_VMEM = 56_200_000
LOAD_VMEM = 55_000_000
F32 = jnp.float32
ALL = range(5)


def primitives(q):
    inverse = 1.0 / q[0]
    ux, ur, ut = q[1] * inverse, q[2] * inverse, q[3] * inverse
    pressure = (GAMMA - 1.0) * (q[4] - 0.5 * (q[1] * ux + q[2] * ur + q[3] * ut))
    sound = jnp.sqrt(GAMMA * pressure * inverse)
    return ux, ur, ut, pressure, sound


def flux(q, prim, d):
    u, pressure = prim[d - 1], prim[3]
    f = [q[d], q[1] * u, q[2] * u, q[3] * u, (q[4] + pressure) * u]
    f[d] = f[d] + pressure
    return f, jnp.abs(u) + prim[4]


def face(left_q, left_flux, right_q, right_flux):
    (fl, sl), (fr, sr) = left_flux, right_flux
    fastest = jnp.maximum(sl, sr)
    return [(fl[v] + fr[v]) - fastest * (right_q[v] - left_q[v]) for v in ALL]


HALF = AXIAL // 2


def axial_neighbour(x, lane, step, end):
    low, high = x[:, :HALF], x[:, HALF:]
    turned_low, turned_high = pltpu.roll(low, -step % HALF, 1), pltpu.roll(high, -step % HALF, 1)
    if step == 1:
        seam = lane == HALF - 1
        parts = [jnp.where(seam, turned_high, turned_low), jnp.where(seam, end, turned_high)]
    else:
        seam = lane == 0
        parts = [jnp.where(seam, end, turned_low), jnp.where(seam, turned_low, turned_high)]
    return jnp.concatenate(parts, axis=1)


def axial_difference(q, prim, lane):
    f, speed = flux(q, prim, 1)

    def following(x):
        return axial_neighbour(x, lane, 1, x[:, HALF:])

    qn = [following(x) for x in q]
    fn = [qn[1]] + [following(f[v]) for v in range(1, 5)]
    right = face(q, (f, speed), qn, (fn, following(speed)))
    return [x - axial_neighbour(x, lane, -1, 2.0 * f[v][:, :HALF]) for v, x in enumerate(right)]


def step_weight(prim, inv_h):
    ux, ur, ut, _, sound = prim
    rate = 4.0 * (jnp.abs(ux) + jnp.abs(ur)) + jnp.abs(ut) * (4.0 * inv_h) + sound * (8.0 + 4.0 * inv_h)
    return rate, 1.0 / (rate + 30.0)


def advance(q, prim, source, axial, radial, swirl, inv_r, inv_h, spin_r, blade):
    ux, ur, ut, pressure, sound = prim
    twice_r = 2.0 * inv_r
    rate, weight = step_weight(prim, inv_h)
    bladed, rotor = blade
    force = bladed * (q[3] - (rotor * spin_r) * q[0])
    gains = [None, None, twice_r * (q[3] * ut + pressure), -twice_r * (q[2] * ut) - force, -ut * force]
    out = []
    for v in ALL:
        total = source[v] - axial[v] - radial[v] - swirl[v]
        if gains[v] is not None:
            total = total + gains[v]
        out.append((rate * q[v] + total) * weight)
    return out


def geometry_table(rows, circle):
    mean = circle / (2.0 * math.pi)
    row = np.arange(rows, dtype=np.float64)
    radius = mean * (0.8 + 0.4 * (row + 0.5) / rows)
    inner = mean * (0.8 + 0.4 * row / rows)
    outer = mean * (0.8 + 0.4 * (row + 1.0) / rows)
    spacing = radius * (2.0 * math.pi / circle)
    return np.stack([outer / radius, inner / radius, 1.0 / spacing, 1.0 / radius, radius / (1.2 * mean)])


def coefficients(low, table, j):
    last = table.shape[1] - 1
    at = [min(max(j + first, 0), last) for first in (0, BAND)]
    return [jnp.where(low, np.float32(row[at[0]]), np.float32(row[at[1]])) for row in table]


def edge_row(band, at_low, at_high):
    return jnp.where(band == 0, at_low, at_high)


MIRROR = (1.0, 1.0, -1.0, 1.0, 1.0)


def blades(blade_ref, rows):
    blade = blade_ref[...]
    bladed = jnp.broadcast_to(4.0 * (blade > 0).astype(F32), (rows, AXIAL))
    rotor = jnp.broadcast_to((blade == 1).astype(F32), (rows, AXIAL))
    return bladed, rotor


def rad_kernel(q_ref, near_ref, sem):
    copy = pltpu.make_async_copy(q_ref.at[:, edge_row(lax.axis_index("rad"), BAND - 1, 0)], near_ref, sem)
    copy.start()
    copy.wait()


def load_kernel(q_ref, qp_ref, q_out_ref, qp_out_ref, sems):
    copies = [
        pltpu.make_async_copy(q_ref, q_out_ref, sems.at[0]),
        pltpu.make_async_copy(qp_ref, qp_out_ref, sems.at[1]),
    ]
    for copy in copies:
        copy.start()
    for copy in copies:
        copy.wait()


class Columns:
    def __init__(self, first_row, total_rows, circle):
        rows = (lax.broadcasted_iota(jnp.int32, (BAND, AXIAL), 0) + first_row).astype(F32)
        mean = circle / (2.0 * math.pi)
        radius = mean * (0.8 + 0.4 * (rows + 0.5) / total_rows)
        self.inner = mean * (0.8 + 0.4 * rows / total_rows)
        self.outer = mean * (0.8 + 0.4 * (rows + 1.0) / total_rows)
        self.inv_r = 1.0 / radius
        self.inv_h = self.inv_r * mean
        self.spin_r = radius * (1.0 / (1.2 * mean))
        self.a_h = 0.25 * self.inv_h


def edge_kernel(total_rows, circle, blade_ref, q_ref, qp_ref, edges_ref, ce, taken):
    band = lax.axis_index("rad")
    low = band == 0
    geo = Columns(band * BAND, total_rows, circle)
    blade = blades(blade_ref, BAND)
    lane = lax.broadcasted_iota(jnp.int32, (BAND, HALF), 1)
    row = lax.broadcasted_iota(jnp.int32, (BAND, AXIAL), 0)
    below_scale = jnp.where((row == 0) & jnp.logical_not(low), 0.0, geo.inv_r * geo.inner)
    above_scale = jnp.where((row == BAND - 1) & low, 0.0, geo.inv_r * geo.outer)
    for side in (0, 1):
        at, inner = (0, 1) if side == 0 else (SECTOR - 1, SECTOR - 2)
        for v in ALL:
            ce[v, side, 8:24] = q_ref[v, :, at, :]
            taken[v, side, 0] = q_ref[v, :, inner, :]
            taken[v, side, 1] = qp_ref[v, :, at, :]
    for side in (0, 1):
        edge = [ce[v, side, 8:24] for v in ALL]
        second = [taken[v, side, 0] for v in ALL]
        source = [40.0 * edge[v] - 10.0 * taken[v, side, 1] for v in ALL]
        for v in ALL:
            ce[v, side, 7:8] = MIRROR[v] * edge[v][0:1]
            ce[v, side, 24:25] = MIRROR[v] * edge[v][BAND - 1 : BAND]
        below = [ce[v, side, 7:23] for v in ALL]
        above = [ce[v, side, 9:25] for v in ALL]
        prim = primitives(edge)
        f = flux(edge, prim, 2)
        g_in = face(below, flux(below, primitives(below), 2), edge, f)
        g_out = face(edge, f, above, flux(above, primitives(above), 2))
        f = flux(edge, prim, 3)
        second_flux = flux(second, primitives(second), 3)
        if side == 0:
            swirl = [geo.inv_h * x for x in face(edge, f, second, second_flux)]
        else:
            swirl = [-geo.inv_h * x for x in face(second, second_flux, edge, f)]
        part = advance(
            edge,
            prim,
            source,
            axial_difference(edge, prim, lane),
            [above_scale * g_out[v] - below_scale * g_in[v] for v in ALL],
            swirl,
            geo.inv_r,
            geo.inv_h,
            geo.spin_r,
            blade,
        )
        for v in ALL:
            edges_ref[v, side, 0:16] = edge[v]
            edges_ref[v, side, 16:32] = part[v]


def pack_kernel(table, q_ref, edges_ref, rad_ref, own_ref, core_ref, other_ref):
    odd = lax.axis_index("theta") % 2 == 1
    band = lax.axis_index("rad")
    low = band == 0
    edge_at = edge_row(band, BAND - 1, 0)
    below_coefs, above_coefs = coefficients(low, table, 0), coefficients(low, table, BAND - 1)
    edge = [q_ref[v, edge_at] for v in ALL]
    near = [rad_ref[v] for v in ALL]
    edge_prim, near_prim = primitives(edge), primitives(near)
    (fe, se), (fn, sn) = flux(edge, edge_prim, 2), flux(near, near_prim, 2)
    fastest = jnp.where(low, np.float32(1.0), np.float32(-1.0)) * jnp.maximum(se, sn)
    _, weight = step_weight(edge_prim, jnp.where(low, above_coefs[2], below_coefs[2]))
    scale = jnp.where(low, -above_coefs[0], below_coefs[1]) * weight
    change = [scale * ((fe[v] + fn[v]) - fastest * (near[v] - edge[v])) for v in ALL]
    here = lax.broadcasted_iota(jnp.int32, (BAND, AXIAL), 0) == edge_at
    for v in ALL:
        for side in (0, 1):
            at = 0 if side == 0 else SECTOR - 1
            own_ref[v, side] = edges_ref[v, side, 16:32] + jnp.where(here, change[v][at : at + 1], 0.0)
        for ref, flip in ((core_ref, jnp.logical_not(odd)), (other_ref, odd)):
            at = 32 * v
            ref[at : at + 16] = jnp.where(flip, edges_ref[v, 1, 0:16], edges_ref[v, 0, 0:16])
            ref[at + 16 : at + 32] = jnp.where(flip, own_ref[v, 1], own_ref[v, 0])
            ref[160 + v : 161 + v] = jnp.where(flip, near[v][SECTOR - 1 : SECTOR], near[v][0:1])


def masks():
    return (
        lax.broadcasted_iota(jnp.int32, (SECTOR, HALF), 1),
        lax.broadcasted_iota(jnp.int32, (SECTOR, AXIAL), 0),
    )


def row_step(coefs, q, prim, source, g_in, g_out, ends, masks, blade):
    lane, sub = masks
    a_out, a_in, inv_h, inv_r, spin_r = coefs
    f, speed = flux(q, prim, 3)
    ahead = lambda x: pltpu.roll(x, SECTOR - 1, 0)
    qn = [ahead(x) for x in q]
    fn = [qn[3]] + [ahead(f[v]) for v in range(1, 5)]
    between = face(q, (f, speed), qn, (fn, ahead(speed)))
    swirl = []
    for v in ALL:
        end = 0.0 if ends is None else ends[v]
        right = jnp.where(sub == SECTOR - 1, end, between[v])
        left = jnp.where(sub == 0, end, pltpu.roll(between[v], 1, 0))
        swirl.append(inv_h * (right - left))
    radial = [a_out * g_out[v] - a_in * g_in[v] for v in ALL]
    return advance(q, prim, source, axial_difference(q, prim, lane), radial, swirl, inv_r, inv_h, spin_r, blade)


def sweep(load, step, store):
    below, q = load(-1), load(0)
    prim = primitives(q)
    g_in = face(below, flux(below, primitives(below), 2), q, flux(q, prim, 2))
    for j in range(BAND):
        above = load(j + 1)
        above_prim = primitives(above)
        g_out = face(q, flux(q, prim, 2), above, flux(above, above_prim, 2))
        store(j, step(j, q, prim, g_in, g_out))
        q, prim, g_in = above, above_prim, g_out


def early_kernel(table, blade_ref, q_ref, qp_ref, rad_ref, p1_ref, edge_ref, source_ref):
    band = lax.axis_index("rad")
    low = band == 0
    mask = masks()
    blade = blades(blade_ref, SECTOR)

    def load(j):
        if j < 0:
            return [jnp.where(low, MIRROR[v] * q_ref[v, 0], rad_ref[v]) for v in ALL]
        if j == BAND:
            return [jnp.where(low, rad_ref[v], MIRROR[v] * q_ref[v, BAND - 1]) for v in ALL]
        return [q_ref[v, j] for v in ALL]

    def step(j, q, prim, g_in, g_out):
        source = [40.0 * q[v] - 10.0 * qp_ref[v, j] for v in ALL]
        for v in ALL:
            source_ref[v, j] = source[v]
        return row_step(coefficients(low, table, j), q, prim, source, g_in, g_out, None, mask, blade)

    def store(j, q):
        for v in ALL:
            p1_ref[v, j] = q[v]

    sweep(load, step, store)
    for v in ALL:
        edge_ref[v] = p1_ref[v, edge_row(band, BAND - 1, 0)]


def final_kernel(
    total_rows,
    circle,
    table,
    blade_ref,
    edges_ref,
    own_ref,
    rad_ref,
    p1_ref,
    source_ref,
    next_ref,
    other_ref,
    core_ref,
    flow_ref,
    send_ref,
    p1,
    nearby,
    ends,
    fields,
):
    odd = lax.axis_index("theta") % 2 == 1
    band = lax.axis_index("rad")
    low = band == 0
    mask = masks()
    blade = blades(blade_ref, SECTOR)
    for v in ALL:
        p1[v] = p1_ref[v]
        nearby[v] = next_ref[v]

    geo = Columns(band * BAND, total_rows, circle)
    near_inv_h = jnp.where(low, coefficients(low, table, BAND)[2], coefficients(low, table, -1)[2])

    for side in (0, 1):
        use_core = odd if side == 0 else jnp.logical_not(odd)
        at = 0 if side == 0 else SECTOR - 1
        sign = 1.0 if side == 0 else -1.0

        def pick(first, step, count):
            spans = [slice(first + step * v, first + step * v + count) for v in ALL]
            return [jnp.where(use_core, core_ref[span], other_ref[span]) for span in spans]

        def ordered(halo, halo_prim, own, own_prim):
            a, b = flux(halo, halo_prim, 3), flux(own, own_prim, 3)
            return face(halo, a, own, b) if side == 0 else face(own, b, halo, a)

        near, near_part, corner = pick(0, 32, 16), pick(16, 32, 16), pick(160, 1, 1)
        own = [edges_ref[v, side, 0:16] for v in ALL]
        own_prim, near_prim = primitives(own), primitives(near)
        shared = ordered(near, near_prim, own, own_prim)
        own_scale = (sign * geo.inv_h) * step_weight(own_prim, geo.inv_h)[1]
        near_scale = (-sign * geo.inv_h) * step_weight(near_prim, geo.inv_h)[1]
        own_next = [own_ref[v, side] + own_scale * shared[v] for v in ALL]
        near_next = [near_part[v] + near_scale * shared[v] for v in ALL]

        edge = [rad_ref[v, at : at + 1, :] for v in ALL]
        edge_prim = primitives(edge)
        corner_face = ordered(corner, primitives(corner), edge, edge_prim)
        corner_scale = (sign * near_inv_h) * step_weight(edge_prim, near_inv_h)[1]

        faces = ordered(near_next, primitives(near_next), own_next, primitives(own_next))
        for v in ALL:
            p1[v, :, at, :] = own_next[v]
            nearby[v, at : at + 1, :] = next_ref[v, at : at + 1, :] + corner_scale * corner_face[v]
            ends[v, :, at, :] = faces[v]

    def load(j):
        if j < 0:
            return [jnp.where(low, MIRROR[v] * p1[v, 0], nearby[v]) for v in ALL]
        if j == BAND:
            return [jnp.where(low, nearby[v], MIRROR[v] * p1[v, BAND - 1]) for v in ALL]
        return [p1[v, j] for v in ALL]

    def step(j, q, prim, g_in, g_out):
        source, end = [source_ref[v, j] for v in ALL], [ends[v, j] for v in ALL]
        return row_step(coefficients(low, table, j), q, prim, source, g_in, g_out, end, mask, blade)

    def store(j, q):
        for v in ALL:
            flow_ref[v, j] = q[v]
        ux, _, _, pressure, _ = primitives(q)
        fields[0, j] = pressure
        fields[1, j] = ux

    sweep(load, step, store)
    for f in (0, 1):
        turned = fields[f].reshape(BAND * SECTOR, AXIAL).T
        send_ref[pl.ds(f, AXIAL, stride=2), :] = turned


def mode_kernel(got_ref, basis_ref, flow_ref, out_ref, flow_out_ref, turned, sem):
    copy = pltpu.make_async_copy(flow_ref, flow_out_ref, sem)
    copy.start()
    sectors = got_ref.shape[0] // 4
    parts = []
    for e in (0, 1):
        for f in (0, 1):
            n = 2 * e + f
            turned[n] = got_ref[pl.ds(n, sectors, stride=4), :].T
            parts.append(
                jnp.concatenate([turned[n, pl.ds(m, BAND, stride=SECTOR), :] for m in range(SECTOR)], axis=1)
            )
    product = jnp.dot(
        jnp.concatenate(parts, axis=0), basis_ref[...], precision=lax.Precision.HIGHEST, preferred_element_type=F32
    )
    for e in (0, 1):
        for f in (0, 1):
            n = 2 * e + f
            out_ref[e, :, 2 * MODES * f : 2 * MODES * (f + 1)] = product[BAND * n : BAND * (n + 1)]
    copy.wait()


def mode_basis(sectors):
    circle = sectors * SECTOR
    cell = (np.arange(SECTOR)[:, None] + SECTOR * np.arange(sectors)[None, :]).reshape(-1)
    phase = (cell[:, None] * np.arange(1, MODES + 1)[None, :] % circle) * (2.0 * np.pi / circle)
    return (np.concatenate([np.cos(phase), -np.sin(phase)], axis=1) / np.sqrt(circle)).astype(np.float32)


def shaped(*shape):
    return jax.ShapeDtypeStruct(shape, F32)


def vmem():
    return pl.BlockSpec(memory_space=pltpu.VMEM)


def limit(mib):
    return pltpu.CompilerParams(vmem_limit_bytes=int(mib * 2**20))


def per_device(q_level, q_prev, blade_row):
    sectors = lax.axis_size("theta")
    bands = lax.axis_size("rad")
    circle = sectors * SECTOR
    core = [(t, t ^ 1) for t in range(sectors)]
    other = [(t, (((t + 1) ^ 1) - 1) % sectors) for t in range(sectors)]
    table = geometry_table(bands * BAND, circle)
    blade = blade_row.reshape(1, AXIAL)

    hbm = pl.BlockSpec(memory_space=pltpu.HBM)
    swap = [(0, 1), (1, 0)]

    def edges(*refs):
        edge_kernel(bands * BAND, circle, *refs)

    def pack(*refs):
        pack_kernel(table, *refs)

    def early(*refs):
        early_kernel(table, *refs)

    def final(*refs):
        final_kernel(bands * BAND, circle, table, *refs)

    near = pl.pallas_call(
        rad_kernel,
        out_shape=shaped(5, SECTOR, AXIAL),
        in_specs=[hbm],
        out_specs=vmem(),
        scratch_shapes=[pltpu.SemaphoreType.DMA],
        compiler_params=pltpu.CompilerParams(vmem_limit_bytes=RAD_VMEM),
    )(q_level)
    rad_in = lax.ppermute(near, "rad", swap)
    q_level, q_prev = pl.pallas_call(
        load_kernel,
        out_shape=[shaped(5, BAND, SECTOR, AXIAL)] * 2,
        in_specs=[hbm] * 2,
        out_specs=[vmem()] * 2,
        scratch_shapes=[pltpu.SemaphoreType.DMA((2,))],
        compiler_params=pltpu.CompilerParams(vmem_limit_bytes=LOAD_VMEM),
        cost_estimate=pl.CostEstimate(flops=0, bytes_accessed=3_000_000, transcendentals=0),
    )(q_level, q_prev)
    edge_columns = pl.pallas_call(
        edges,
        out_shape=shaped(5, 2, 32, AXIAL),
        in_specs=[vmem()] * 3,
        out_specs=vmem(),
        scratch_shapes=[pltpu.VMEM((5, 2, 32, AXIAL), F32), pltpu.VMEM((5, 2, 2, BAND, AXIAL), F32)],
        compiler_params=limit(4),
        cost_estimate=pl.CostEstimate(flops=5_000_000, bytes_accessed=2_000_000, transcendentals=50_000),
    )(blade, q_level, q_prev)
    own_columns, core_out, other_out = pl.pallas_call(
        pack,
        out_shape=[shaped(5, 2, BAND, AXIAL)] + [shaped(168, AXIAL)] * 2,
        in_specs=[vmem()] * 3,
        out_specs=[vmem()] * 3,
        compiler_params=limit(4),
    )(q_level, edge_columns, rad_in)
    core_in = lax.ppermute(core_out, "theta", core)
    other_in = lax.ppermute(other_out, "theta", other)
    part, edge, source = pl.pallas_call(
        early,
        out_shape=[shaped(5, BAND, SECTOR, AXIAL), shaped(5, SECTOR, AXIAL), shaped(5, BAND, SECTOR, AXIAL)],
        in_specs=[vmem()] * 4,
        out_specs=[vmem()] * 3,
        compiler_params=limit(8),
        cost_estimate=pl.CostEstimate(flops=10_000_000, bytes_accessed=3_500_000, transcendentals=100_000),
    )(blade, q_level, q_prev, rad_in)
    next_in = lax.ppermute(edge, "rad", swap)
    flow_state, send = pl.pallas_call(
        final,
        out_shape=[shaped(5, BAND, SECTOR, AXIAL), shaped(2 * AXIAL, BAND * SECTOR)],
        in_specs=[vmem()] * 9,
        out_specs=[vmem()] * 2,
        scratch_shapes=[
            pltpu.VMEM((5, BAND, SECTOR, AXIAL), F32),
            pltpu.VMEM((5, SECTOR, AXIAL), F32),
            pltpu.VMEM((5, BAND, SECTOR, AXIAL), F32),
            pltpu.VMEM((2, BAND, SECTOR, AXIAL), F32),
        ],
        compiler_params=limit(8),
    )(blade, edge_columns, own_columns, rad_in, part, source, next_in, other_in, core_in)
    got = lax.all_to_all(send.reshape(sectors, 4, 128), "theta", split_axis=0, concat_axis=0, tiled=True)
    spectra, flow_state = pl.pallas_call(
        mode_kernel,
        out_shape=[shaped(2, BAND, 4 * MODES), shaped(5, BAND, SECTOR, AXIAL)],
        in_specs=[vmem()] * 3,
        out_specs=[vmem(), hbm],
        scratch_shapes=[pltpu.VMEM((4, BAND * SECTOR, sectors), F32), pltpu.SemaphoreType.DMA],
        compiler_params=limit(4),
    )(got.reshape(4 * sectors, 128), jnp.asarray(mode_basis(sectors)), flow_state)
    return flow_state, spectra


def solution(mesh):
    in_specs = (P(None, "rad", "theta", None), P(None, "rad", "theta", None), P())
    out_specs = (P(None, "rad", "theta", None), P("theta", "rad", None))
    return jax.shard_map(per_device, mesh=mesh, in_specs=in_specs, out_specs=out_specs, check_vma=False)
```

```python
import math

import jax
import jax.numpy as jnp
import numpy as np
from jax import lax
from jax.experimental import pallas as pl
from jax.experimental.pallas import tpu as pltpu
from jax.sharding import PartitionSpec as P

MODES = 64
GAMMA = 1.4
KAPPA = 2.0

BAND = 16
SECTOR = 8
AXIAL = 256
RAD_VMEM = 56_200_000
LOAD_VMEM = 55_000_000
F32 = jnp.float32
ALL = range(5)


def primitives(q):
    inverse = 1.0 / q[0]
    ux, ur, ut = q[1] * inverse, q[2] * inverse, q[3] * inverse
    pressure = (GAMMA - 1.0) * (q[4] - 0.5 * (q[1] * ux + q[2] * ur + q[3] * ut))
    sound = jnp.sqrt(GAMMA * pressure * inverse)
    return ux, ur, ut, pressure, sound


def flux(q, prim, d):
    u, pressure = prim[d - 1], prim[3]
    f = [q[d], q[1] * u, q[2] * u, q[3] * u, (q[4] + pressure) * u]
    f[d] = f[d] + pressure
    return f, jnp.abs(u) + prim[4]


def face(left_q, left_flux, right_q, right_flux):
    (fl, sl), (fr, sr) = left_flux, right_flux
    fastest = jnp.maximum(sl, sr)
    return [(fl[v] + fr[v]) - fastest * (right_q[v] - left_q[v]) for v in ALL]


HALF = AXIAL // 2


def axial_neighbour(x, lane, step, end):
    low, high = x[:, :HALF], x[:, HALF:]
    turned_low, turned_high = pltpu.roll(low, -step % HALF, 1), pltpu.roll(high, -step % HALF, 1)
    if step == 1:
        seam = lane == HALF - 1
        parts = [jnp.where(seam, turned_high, turned_low), jnp.where(seam, end, turned_high)]
    else:
        seam = lane == 0
        parts = [jnp.where(seam, end, turned_low), jnp.where(seam, turned_low, turned_high)]
    return jnp.concatenate(parts, axis=1)


def axial_difference(q, prim, lane):
    f, speed = flux(q, prim, 1)

    def following(x):
        return axial_neighbour(x, lane, 1, x[:, HALF:])

    qn = [following(x) for x in q]
    fn = [qn[1]] + [following(f[v]) for v in range(1, 5)]
    right = face(q, (f, speed), qn, (fn, following(speed)))
    return [x - axial_neighbour(x, lane, -1, 2.0 * f[v][:, :HALF]) for v, x in enumerate(right)]


def step_weight(prim, inv_h):
    ux, ur, ut, _, sound = prim
    rate = 4.0 * (jnp.abs(ux) + jnp.abs(ur)) + jnp.abs(ut) * (4.0 * inv_h) + sound * (8.0 + 4.0 * inv_h)
    return rate, 1.0 / (rate + 30.0)


def advance(q, prim, source, axial, radial, swirl, inv_r, inv_h, spin_r, blade):
    ux, ur, ut, pressure, sound = prim
    twice_r = 2.0 * inv_r
    rate, weight = step_weight(prim, inv_h)
    bladed, rotor = blade
    force = bladed * (q[3] - (rotor * spin_r) * q[0])
    gains = [None, None, twice_r * (q[3] * ut + pressure), -twice_r * (q[2] * ut) - force, -ut * force]
    out = []
    for v in ALL:
        total = source[v] - axial[v] - radial[v] - swirl[v]
        if gains[v] is not None:
            total = total + gains[v]
        out.append((rate * q[v] + total) * weight)
    return out


def geometry_table(rows, circle):
    mean = circle / (2.0 * math.pi)
    row = np.arange(rows, dtype=np.float64)
    radius = mean * (0.8 + 0.4 * (row + 0.5) / rows)
    inner = mean * (0.8 + 0.4 * row / rows)
    outer = mean * (0.8 + 0.4 * (row + 1.0) / rows)
    spacing = radius * (2.0 * math.pi / circle)
    return np.stack([outer / radius, inner / radius, 1.0 / spacing, 1.0 / radius, radius / (1.2 * mean)])


def coefficients(low, table, j):
    last = table.shape[1] - 1
    at = [min(max(j + first, 0), last) for first in (0, BAND)]
    return [jnp.where(low, np.float32(row[at[0]]), np.float32(row[at[1]])) for row in table]


def edge_row(band, at_low, at_high):
    return jnp.where(band == 0, at_low, at_high)


MIRROR = (1.0, 1.0, -1.0, 1.0, 1.0)


def blades(blade_ref, rows):
    blade = blade_ref[...]
    bladed = jnp.broadcast_to(4.0 * (blade > 0).astype(F32), (rows, AXIAL))
    rotor = jnp.broadcast_to((blade == 1).astype(F32), (rows, AXIAL))
    return bladed, rotor


def rad_kernel(q_ref, near_ref, sem):
    copy = pltpu.make_async_copy(q_ref.at[:, edge_row(lax.axis_index("rad"), BAND - 1, 0)], near_ref, sem)
    copy.start()
    copy.wait()


def load_kernel(q_ref, qp_ref, q_out_ref, qp_out_ref, sems):
    copies = [
        pltpu.make_async_copy(q_ref, q_out_ref, sems.at[0]),
        pltpu.make_async_copy(qp_ref, qp_out_ref, sems.at[1]),
    ]
    for copy in copies:
        copy.start()
    for copy in copies:
        copy.wait()


class Columns:
    def __init__(self, first_row, total_rows, circle):
        rows = (lax.broadcasted_iota(jnp.int32, (BAND, AXIAL), 0) + first_row).astype(F32)
        mean = circle / (2.0 * math.pi)
        radius = mean * (0.8 + 0.4 * (rows + 0.5) / total_rows)
        self.inner = mean * (0.8 + 0.4 * rows / total_rows)
        self.outer = mean * (0.8 + 0.4 * (rows + 1.0) / total_rows)
        self.inv_r = 1.0 / radius
        self.inv_h = self.inv_r * mean
        self.spin_r = radius * (1.0 / (1.2 * mean))
        self.a_h = 0.25 * self.inv_h


def edge_kernel(total_rows, circle, blade_ref, q_ref, qp_ref, edges_ref, ce, taken):
    band = lax.axis_index("rad")
    low = band == 0
    geo = Columns(band * BAND, total_rows, circle)
    blade = blades(blade_ref, BAND)
    lane = lax.broadcasted_iota(jnp.int32, (BAND, HALF), 1)
    row = lax.broadcasted_iota(jnp.int32, (BAND, AXIAL), 0)
    below_scale = jnp.where((row == 0) & jnp.logical_not(low), 0.0, geo.inv_r * geo.inner)
    above_scale = jnp.where((row == BAND - 1) & low, 0.0, geo.inv_r * geo.outer)
    for side in (0, 1):
        at, inner = (0, 1) if side == 0 else (SECTOR - 1, SECTOR - 2)
        for v in ALL:
            ce[v, side, 8:24] = q_ref[v, :, at, :]
            taken[v, side, 0] = q_ref[v, :, inner, :]
            taken[v, side, 1] = qp_ref[v, :, at, :]
    for side in (0, 1):
        edge = [ce[v, side, 8:24] for v in ALL]
        second = [taken[v, side, 0] for v in ALL]
        source = [40.0 * edge[v] - 10.0 * taken[v, side, 1] for v in ALL]
        for v in ALL:
            ce[v, side, 7:8] = MIRROR[v] * edge[v][0:1]
            ce[v, side, 24:25] = MIRROR[v] * edge[v][BAND - 1 : BAND]
        below = [ce[v, side, 7:23] for v in ALL]
        above = [ce[v, side, 9:25] for v in ALL]
        prim = primitives(edge)
        f = flux(edge, prim, 2)
        g_in = face(below, flux(below, primitives(below), 2), edge, f)
        g_out = face(edge, f, above, flux(above, primitives(above), 2))
        f = flux(edge, prim, 3)
        second_flux = flux(second, primitives(second), 3)
        if side == 0:
            swirl = [geo.inv_h * x for x in face(edge, f, second, second_flux)]
        else:
            swirl = [-geo.inv_h * x for x in face(second, second_flux, edge, f)]
        part = advance(
            edge,
            prim,
            source,
            axial_difference(edge, prim, lane),
            [above_scale * g_out[v] - below_scale * g_in[v] for v in ALL],
            swirl,
            geo.inv_r,
            geo.inv_h,
            geo.spin_r,
            blade,
        )
        for v in ALL:
            edges_ref[v, side, 0:16] = edge[v]
            edges_ref[v, side, 16:32] = part[v]


def pack_kernel(table, q_ref, edges_ref, rad_ref, own_ref, core_ref, other_ref):
    odd = lax.axis_index("theta") % 2 == 1
    band = lax.axis_index("rad")
    low = band == 0
    edge_at = edge_row(band, BAND - 1, 0)
    below_coefs, above_coefs = coefficients(low, table, 0), coefficients(low, table, BAND - 1)
    edge = [q_ref[v, edge_at] for v in ALL]
    near = [rad_ref[v] for v in ALL]
    edge_prim, near_prim = primitives(edge), primitives(near)
    (fe, se), (fn, sn) = flux(edge, edge_prim, 2), flux(near, near_prim, 2)
    fastest = jnp.where(low, np.float32(1.0), np.float32(-1.0)) * jnp.maximum(se, sn)
    _, weight = step_weight(edge_prim, jnp.where(low, above_coefs[2], below_coefs[2]))
    scale = jnp.where(low, -above_coefs[0], below_coefs[1]) * weight
    change = [scale * ((fe[v] + fn[v]) - fastest * (near[v] - edge[v])) for v in ALL]
    here = lax.broadcasted_iota(jnp.int32, (BAND, AXIAL), 0) == edge_at
    for v in ALL:
        for side in (0, 1):
            at = 0 if side == 0 else SECTOR - 1
            own_ref[v, side] = edges_ref[v, side, 16:32] + jnp.where(here, change[v][at : at + 1], 0.0)
        for ref, flip in ((core_ref, jnp.logical_not(odd)), (other_ref, odd)):
            at = 32 * v
            ref[at : at + 16] = jnp.where(flip, edges_ref[v, 1, 0:16], edges_ref[v, 0, 0:16])
            ref[at + 16 : at + 32] = jnp.where(flip, own_ref[v, 1], own_ref[v, 0])
            ref[160 + v : 161 + v] = jnp.where(flip, near[v][SECTOR - 1 : SECTOR], near[v][0:1])


def masks():
    return (
        lax.broadcasted_iota(jnp.int32, (SECTOR, HALF), 1),
        lax.broadcasted_iota(jnp.int32, (SECTOR, AXIAL), 0),
    )


def row_step(coefs, q, prim, source, g_in, g_out, ends, masks, blade):
    lane, sub = masks
    a_out, a_in, inv_h, inv_r, spin_r = coefs
    f, speed = flux(q, prim, 3)
    ahead = lambda x: pltpu.roll(x, SECTOR - 1, 0)
    qn = [ahead(x) for x in q]
    fn = [qn[3]] + [ahead(f[v]) for v in range(1, 5)]
    between = face(q, (f, speed), qn, (fn, ahead(speed)))
    swirl = []
    for v in ALL:
        end = 0.0 if ends is None else ends[v]
        right = jnp.where(sub == SECTOR - 1, end, between[v])
        left = jnp.where(sub == 0, end, pltpu.roll(between[v], 1, 0))
        swirl.append(inv_h * (right - left))
    radial = [a_out * g_out[v] - a_in * g_in[v] for v in ALL]
    return advance(q, prim, source, axial_difference(q, prim, lane), radial, swirl, inv_r, inv_h, spin_r, blade)


def sweep(load, step, store):
    below, q = load(-1), load(0)
    prim = primitives(q)
    g_in = face(below, flux(below, primitives(below), 2), q, flux(q, prim, 2))
    for j in range(BAND):
        above = load(j + 1)
        above_prim = primitives(above)
        g_out = face(q, flux(q, prim, 2), above, flux(above, above_prim, 2))
        store(j, step(j, q, prim, g_in, g_out))
        q, prim, g_in = above, above_prim, g_out


def early_kernel(table, blade_ref, q_ref, qp_ref, rad_ref, p1_ref, edge_ref, source_ref):
    band = lax.axis_index("rad")
    low = band == 0
    mask = masks()
    blade = blades(blade_ref, SECTOR)

    def load(j):
        if j < 0:
            return [jnp.where(low, MIRROR[v] * q_ref[v, 0], rad_ref[v]) for v in ALL]
        if j == BAND:
            return [jnp.where(low, rad_ref[v], MIRROR[v] * q_ref[v, BAND - 1]) for v in ALL]
        return [q_ref[v, j] for v in ALL]

    def step(j, q, prim, g_in, g_out):
        source = [40.0 * q[v] - 10.0 * qp_ref[v, j] for v in ALL]
        for v in ALL:
            source_ref[v, j] = source[v]
        return row_step(coefficients(low, table, j), q, prim, source, g_in, g_out, None, mask, blade)

    def store(j, q):
        for v in ALL:
            p1_ref[v, j] = q[v]

    sweep(load, step, store)
    for v in ALL:
        edge_ref[v] = p1_ref[v, edge_row(band, BAND - 1, 0)]


def final_kernel(
    total_rows,
    circle,
    table,
    blade_ref,
    edges_ref,
    own_ref,
    rad_ref,
    p1_ref,
    source_ref,
    next_ref,
    other_ref,
    core_ref,
    flow_ref,
    send_ref,
    p1,
    nearby,
    ends,
    fields,
):
    odd = lax.axis_index("theta") % 2 == 1
    band = lax.axis_index("rad")
    low = band == 0
    mask = masks()
    blade = blades(blade_ref, SECTOR)
    for v in ALL:
        p1[v] = p1_ref[v]
        nearby[v] = next_ref[v]

    geo = Columns(band * BAND, total_rows, circle)
    near_inv_h = jnp.where(low, coefficients(low, table, BAND)[2], coefficients(low, table, -1)[2])

    for side in (0, 1):
        use_core = odd if side == 0 else jnp.logical_not(odd)
        at = 0 if side == 0 else SECTOR - 1
        sign = 1.0 if side == 0 else -1.0

        def pick(first, step, count):
            spans = [slice(first + step * v, first + step * v + count) for v in ALL]
            return [jnp.where(use_core, core_ref[span], other_ref[span]) for span in spans]

        def ordered(halo, halo_prim, own, own_prim):
            a, b = flux(halo, halo_prim, 3), flux(own, own_prim, 3)
            return face(halo, a, own, b) if side == 0 else face(own, b, halo, a)

        near, near_part, corner = pick(0, 32, 16), pick(16, 32, 16), pick(160, 1, 1)
        own = [edges_ref[v, side, 0:16] for v in ALL]
        own_prim, near_prim = primitives(own), primitives(near)
        shared = ordered(near, near_prim, own, own_prim)
        own_scale = (sign * geo.inv_h) * step_weight(own_prim, geo.inv_h)[1]
        near_scale = (-sign * geo.inv_h) * step_weight(near_prim, geo.inv_h)[1]
        own_next = [own_ref[v, side] + own_scale * shared[v] for v in ALL]
        near_next = [near_part[v] + near_scale * shared[v] for v in ALL]

        edge = [rad_ref[v, at : at + 1, :] for v in ALL]
        edge_prim = primitives(edge)
        corner_face = ordered(corner, primitives(corner), edge, edge_prim)
        corner_scale = (sign * near_inv_h) * step_weight(edge_prim, near_inv_h)[1]

        faces = ordered(near_next, primitives(near_next), own_next, primitives(own_next))
        for v in ALL:
            p1[v, :, at, :] = own_next[v]
            nearby[v, at : at + 1, :] = next_ref[v, at : at + 1, :] + corner_scale * corner_face[v]
            ends[v, :, at, :] = faces[v]

    def load(j):
        if j < 0:
            return [jnp.where(low, MIRROR[v] * p1[v, 0], nearby[v]) for v in ALL]
        if j == BAND:
            return [jnp.where(low, nearby[v], MIRROR[v] * p1[v, BAND - 1]) for v in ALL]
        return [p1[v, j] for v in ALL]

    def step(j, q, prim, g_in, g_out):
        source, end = [source_ref[v, j] for v in ALL], [ends[v, j] for v in ALL]
        return row_step(coefficients(low, table, j), q, prim, source, g_in, g_out, end, mask, blade)

    def store(j, q):
        for v in ALL:
            flow_ref[v, j] = q[v]
        ux, _, _, pressure, _ = primitives(q)
        fields[0, j] = pressure
        fields[1, j] = ux

    sweep(load, step, store)
    for f in (0, 1):
        turned = fields[f].reshape(BAND * SECTOR, AXIAL).T
        send_ref[pl.ds(f, AXIAL, stride=2), :] = turned


def mode_kernel(got_ref, basis_ref, flow_ref, keep_ref, give_ref, flow_out_ref, turned, sem):
    copy = pltpu.make_async_copy(flow_ref, flow_out_ref, sem)
    copy.start()
    chips = got_ref.shape[0] // 8
    core = lax.axis_index("theta") % 2
    left = lax.broadcasted_iota(jnp.int32, (BAND, 2 * chips), 1) < chips
    parts = []
    for n in range(8):
        cells = got_ref[pl.ds(n, chips, stride=8), :]
        turned[n] = jnp.concatenate([cells, cells], axis=0).T
        rows = [turned[n, pl.ds(m, BAND, stride=SECTOR), :] for m in range(SECTOR)]
        parts.append(
            jnp.concatenate([jnp.where(left, rows[m], rows[m + 1]) for m in range(0, SECTOR, 2)], axis=1)
        )
    product = jnp.dot(
        jnp.concatenate(parts, axis=0), basis_ref[core], precision=lax.Precision.HIGHEST, preferred_element_type=F32
    )
    half = 4 * BAND
    keep_ref[...] = jnp.where(core == 0, product[:half], product[half:])
    give_ref[...] = jnp.where(core == 0, product[half:], product[:half])
    copy.wait()


def sum_kernel(keep_ref, got_ref, out_ref):
    total = keep_ref[...] + got_ref[...]
    for e in (0, 1):
        for f in (0, 1):
            n = 2 * e + f
            out_ref[e, :, 2 * MODES * f : 2 * MODES * (f + 1)] = total[BAND * n : BAND * (n + 1)]


def mode_basis(sectors):
    circle = sectors * SECTOR
    sector = 2 * np.arange(sectors // 2)[None, None, :] + np.arange(2)[:, None, None]
    cell = (np.arange(SECTOR)[None, :, None] + SECTOR * sector).reshape(2, -1)
    phase = (cell[:, :, None] * np.arange(1, MODES + 1) % circle) * (2.0 * np.pi / circle)
    return (np.concatenate([np.cos(phase), -np.sin(phase)], axis=2) / np.sqrt(circle)).astype(np.float32)


def shaped(*shape):
    return jax.ShapeDtypeStruct(shape, F32)


def vmem():
    return pl.BlockSpec(memory_space=pltpu.VMEM)


def limit(mib):
    return pltpu.CompilerParams(vmem_limit_bytes=int(mib * 2**20))


def per_device(q_level, q_prev, blade_row):
    sectors = lax.axis_size("theta")
    bands = lax.axis_size("rad")
    circle = sectors * SECTOR
    core = [(t, t ^ 1) for t in range(sectors)]
    other = [(t, (((t + 1) ^ 1) - 1) % sectors) for t in range(sectors)]
    table = geometry_table(bands * BAND, circle)
    blade = blade_row.reshape(1, AXIAL)

    hbm = pl.BlockSpec(memory_space=pltpu.HBM)
    swap = [(0, 1), (1, 0)]

    def edges(*refs):
        edge_kernel(bands * BAND, circle, *refs)

    def pack(*refs):
        pack_kernel(table, *refs)

    def early(*refs):
        early_kernel(table, *refs)

    def final(*refs):
        final_kernel(bands * BAND, circle, table, *refs)

    near = pl.pallas_call(
        rad_kernel,
        out_shape=shaped(5, SECTOR, AXIAL),
        in_specs=[hbm],
        out_specs=vmem(),
        scratch_shapes=[pltpu.SemaphoreType.DMA],
        compiler_params=pltpu.CompilerParams(vmem_limit_bytes=RAD_VMEM),
    )(q_level)
    rad_in = lax.ppermute(near, "rad", swap)
    q_level, q_prev = pl.pallas_call(
        load_kernel,
        out_shape=[shaped(5, BAND, SECTOR, AXIAL)] * 2,
        in_specs=[hbm] * 2,
        out_specs=[vmem()] * 2,
        scratch_shapes=[pltpu.SemaphoreType.DMA((2,))],
        compiler_params=pltpu.CompilerParams(vmem_limit_bytes=LOAD_VMEM),
        cost_estimate=pl.CostEstimate(flops=0, bytes_accessed=3_000_000, transcendentals=0),
    )(q_level, q_prev)
    edge_columns = pl.pallas_call(
        edges,
        out_shape=shaped(5, 2, 32, AXIAL),
        in_specs=[vmem()] * 3,
        out_specs=vmem(),
        scratch_shapes=[pltpu.VMEM((5, 2, 32, AXIAL), F32), pltpu.VMEM((5, 2, 2, BAND, AXIAL), F32)],
        compiler_params=limit(4),
        cost_estimate=pl.CostEstimate(flops=5_000_000, bytes_accessed=2_000_000, transcendentals=50_000),
    )(blade, q_level, q_prev)
    own_columns, core_out, other_out = pl.pallas_call(
        pack,
        out_shape=[shaped(5, 2, BAND, AXIAL)] + [shaped(168, AXIAL)] * 2,
        in_specs=[vmem()] * 3,
        out_specs=[vmem()] * 3,
        compiler_params=limit(4),
    )(q_level, edge_columns, rad_in)
    core_in = lax.ppermute(core_out, "theta", core)
    other_in = lax.ppermute(other_out, "theta", other)
    part, edge, source = pl.pallas_call(
        early,
        out_shape=[shaped(5, BAND, SECTOR, AXIAL), shaped(5, SECTOR, AXIAL), shaped(5, BAND, SECTOR, AXIAL)],
        in_specs=[vmem()] * 4,
        out_specs=[vmem()] * 3,
        compiler_params=limit(8),
        cost_estimate=pl.CostEstimate(flops=10_000_000, bytes_accessed=3_500_000, transcendentals=100_000),
    )(blade, q_level, q_prev, rad_in)
    next_in = lax.ppermute(edge, "rad", swap)
    flow_state, send = pl.pallas_call(
        final,
        out_shape=[shaped(5, BAND, SECTOR, AXIAL), shaped(2 * AXIAL, BAND * SECTOR)],
        in_specs=[vmem()] * 9,
        out_specs=[vmem()] * 2,
        scratch_shapes=[
            pltpu.VMEM((5, BAND, SECTOR, AXIAL), F32),
            pltpu.VMEM((5, SECTOR, AXIAL), F32),
            pltpu.VMEM((5, BAND, SECTOR, AXIAL), F32),
            pltpu.VMEM((2, BAND, SECTOR, AXIAL), F32),
        ],
        compiler_params=limit(8),
    )(blade, edge_columns, own_columns, rad_in, part, source, next_in, other_in, core_in)
    chips = sectors // 2
    got = lax.all_to_all(
        send.reshape(chips, 8, 128),
        "theta",
        split_axis=0,
        concat_axis=0,
        tiled=True,
        axis_index_groups=[[2 * chip + c for chip in range(chips)] for c in (0, 1)],
    )
    keep, give, flow_state = pl.pallas_call(
        mode_kernel,
        out_shape=[shaped(4 * BAND, 2 * MODES)] * 2 + [shaped(5, BAND, SECTOR, AXIAL)],
        in_specs=[vmem()] * 3,
        out_specs=[vmem(), vmem(), hbm],
        scratch_shapes=[pltpu.VMEM((8, BAND * SECTOR, 2 * chips), F32), pltpu.SemaphoreType.DMA],
        compiler_params=limit(4),
    )(got.reshape(8 * chips, 128), jnp.asarray(mode_basis(sectors)), flow_state)
    spectra = pl.pallas_call(
        sum_kernel,
        out_shape=shaped(2, BAND, 4 * MODES),
        in_specs=[vmem()] * 2,
        out_specs=vmem(),
        compiler_params=limit(2),
    )(keep, lax.ppermute(give, "theta", core))
    return flow_state, spectra


def solution(mesh):
    in_specs = (P(None, "rad", "theta", None), P(None, "rad", "theta", None), P())
    out_specs = (P(None, "rad", "theta", None), P("theta", "rad", None))
    return jax.shard_map(per_device, mesh=mesh, in_specs=in_specs, out_specs=out_specs, check_vma=False)
```

```python
import math

import jax
import jax.numpy as jnp
import numpy as np
from jax import lax
from jax.experimental import pallas as pl
from jax.experimental.pallas import tpu as pltpu
from jax.sharding import PartitionSpec as P

MODES = 64
GAMMA = 1.4
KAPPA = 2.0

BAND = 16
SECTOR = 8
AXIAL = 256
RAD_VMEM = 56_200_000
LOAD_VMEM = 55_000_000
F32 = jnp.float32
ALL = range(5)


def primitives(q):
    inverse = 1.0 / q[0]
    ux, ur, ut = q[1] * inverse, q[2] * inverse, q[3] * inverse
    pressure = (GAMMA - 1.0) * (q[4] - 0.5 * (q[1] * ux + q[2] * ur + q[3] * ut))
    sound = jnp.sqrt(GAMMA * pressure * inverse)
    return ux, ur, ut, pressure, sound


def flux(q, prim, d):
    u, pressure = prim[d - 1], prim[3]
    f = [q[d], q[1] * u, q[2] * u, q[3] * u, (q[4] + pressure) * u]
    f[d] = f[d] + pressure
    return f, jnp.abs(u) + prim[4]


def face(left_q, left_flux, right_q, right_flux):
    (fl, sl), (fr, sr) = left_flux, right_flux
    fastest = jnp.maximum(sl, sr)
    return [(fl[v] + fr[v]) - fastest * (right_q[v] - left_q[v]) for v in ALL]


HALF = AXIAL // 2


def axial_neighbour(x, lane, step, end):
    low, high = x[:, :HALF], x[:, HALF:]
    turned_low, turned_high = pltpu.roll(low, -step % HALF, 1), pltpu.roll(high, -step % HALF, 1)
    if step == 1:
        seam = lane == HALF - 1
        parts = [jnp.where(seam, turned_high, turned_low), jnp.where(seam, end, turned_high)]
    else:
        seam = lane == 0
        parts = [jnp.where(seam, end, turned_low), jnp.where(seam, turned_low, turned_high)]
    return jnp.concatenate(parts, axis=1)


def axial_difference(q, prim, lane):
    f, speed = flux(q, prim, 1)

    def following(x):
        return axial_neighbour(x, lane, 1, x[:, HALF:])

    qn = [following(x) for x in q]
    fn = [qn[1]] + [following(f[v]) for v in range(1, 5)]
    right = face(q, (f, speed), qn, (fn, following(speed)))
    return [x - axial_neighbour(x, lane, -1, 2.0 * f[v][:, :HALF]) for v, x in enumerate(right)]


def step_weight(prim, inv_h):
    ux, ur, ut, _, sound = prim
    rate = 4.0 * (jnp.abs(ux) + jnp.abs(ur)) + jnp.abs(ut) * (4.0 * inv_h) + sound * (8.0 + 4.0 * inv_h)
    return rate, 1.0 / (rate + 30.0)


def advance(q, prim, source, axial, radial, swirl, inv_r, inv_h, spin_r, blade):
    ux, ur, ut, pressure, sound = prim
    twice_r = 2.0 * inv_r
    rate, weight = step_weight(prim, inv_h)
    bladed, rotor = blade
    force = bladed * (q[3] - (rotor * spin_r) * q[0])
    gains = [None, None, twice_r * (q[3] * ut + pressure), -twice_r * (q[2] * ut) - force, -ut * force]
    out = []
    for v in ALL:
        total = source[v] - axial[v] - radial[v] - swirl[v]
        if gains[v] is not None:
            total = total + gains[v]
        out.append((rate * q[v] + total) * weight)
    return out


def geometry_table(rows, circle):
    mean = circle / (2.0 * math.pi)
    row = np.arange(rows, dtype=np.float64)
    radius = mean * (0.8 + 0.4 * (row + 0.5) / rows)
    inner = mean * (0.8 + 0.4 * row / rows)
    outer = mean * (0.8 + 0.4 * (row + 1.0) / rows)
    spacing = radius * (2.0 * math.pi / circle)
    return np.stack([outer / radius, inner / radius, 1.0 / spacing, 1.0 / radius, radius / (1.2 * mean)])


def coefficients(low, table, j):
    last = table.shape[1] - 1
    at = [min(max(j + first, 0), last) for first in (0, BAND)]
    return [jnp.where(low, np.float32(row[at[0]]), np.float32(row[at[1]])) for row in table]


def edge_row(band, at_low, at_high):
    return jnp.where(band == 0, at_low, at_high)


MIRROR = (1.0, 1.0, -1.0, 1.0, 1.0)


def blades(blade_ref, rows):
    blade = blade_ref[...]
    bladed = jnp.broadcast_to(4.0 * (blade > 0).astype(F32), (rows, AXIAL))
    rotor = jnp.broadcast_to((blade == 1).astype(F32), (rows, AXIAL))
    return bladed, rotor


def rad_kernel(q_ref, near_ref, sem):
    copy = pltpu.make_async_copy(q_ref.at[:, edge_row(lax.axis_index("rad"), BAND - 1, 0)], near_ref, sem)
    copy.start()
    copy.wait()


def load_kernel(q_ref, qp_ref, q_out_ref, qp_out_ref, sems):
    copies = [
        pltpu.make_async_copy(q_ref, q_out_ref, sems.at[0]),
        pltpu.make_async_copy(qp_ref, qp_out_ref, sems.at[1]),
    ]
    for copy in copies:
        copy.start()
    for copy in copies:
        copy.wait()


class Columns:
    def __init__(self, first_row, total_rows, circle):
        rows = (lax.broadcasted_iota(jnp.int32, (BAND, AXIAL), 0) + first_row).astype(F32)
        mean = circle / (2.0 * math.pi)
        radius = mean * (0.8 + 0.4 * (rows + 0.5) / total_rows)
        self.inner = mean * (0.8 + 0.4 * rows / total_rows)
        self.outer = mean * (0.8 + 0.4 * (rows + 1.0) / total_rows)
        self.inv_r = 1.0 / radius
        self.inv_h = self.inv_r * mean
        self.spin_r = radius * (1.0 / (1.2 * mean))
        self.a_h = 0.25 * self.inv_h


def edge_kernel(total_rows, circle, blade_ref, q_ref, qp_ref, edges_ref, ce, taken):
    band = lax.axis_index("rad")
    low = band == 0
    geo = Columns(band * BAND, total_rows, circle)
    blade = blades(blade_ref, BAND)
    lane = lax.broadcasted_iota(jnp.int32, (BAND, HALF), 1)
    row = lax.broadcasted_iota(jnp.int32, (BAND, AXIAL), 0)
    below_scale = jnp.where((row == 0) & jnp.logical_not(low), 0.0, geo.inv_r * geo.inner)
    above_scale = jnp.where((row == BAND - 1) & low, 0.0, geo.inv_r * geo.outer)
    for side in (0, 1):
        at, inner = (0, 1) if side == 0 else (SECTOR - 1, SECTOR - 2)
        for v in ALL:
            ce[v, side, 8:24] = q_ref[v, :, at, :]
            taken[v, side, 0] = q_ref[v, :, inner, :]
            taken[v, side, 1] = qp_ref[v, :, at, :]
    for side in (0, 1):
        edge = [ce[v, side, 8:24] for v in ALL]
        second = [taken[v, side, 0] for v in ALL]
        source = [40.0 * edge[v] - 10.0 * taken[v, side, 1] for v in ALL]
        for v in ALL:
            ce[v, side, 7:8] = MIRROR[v] * edge[v][0:1]
            ce[v, side, 24:25] = MIRROR[v] * edge[v][BAND - 1 : BAND]
        below = [ce[v, side, 7:23] for v in ALL]
        above = [ce[v, side, 9:25] for v in ALL]
        prim = primitives(edge)
        f = flux(edge, prim, 2)
        g_in = face(below, flux(below, primitives(below), 2), edge, f)
        g_out = face(edge, f, above, flux(above, primitives(above), 2))
        f = flux(edge, prim, 3)
        second_flux = flux(second, primitives(second), 3)
        if side == 0:
            swirl = [geo.inv_h * x for x in face(edge, f, second, second_flux)]
        else:
            swirl = [-geo.inv_h * x for x in face(second, second_flux, edge, f)]
        part = advance(
            edge,
            prim,
            source,
            axial_difference(edge, prim, lane),
            [above_scale * g_out[v] - below_scale * g_in[v] for v in ALL],
            swirl,
            geo.inv_r,
            geo.inv_h,
            geo.spin_r,
            blade,
        )
        for v in ALL:
            edges_ref[v, side, 0:16] = edge[v]
            edges_ref[v, side, 16:32] = part[v]


def pack_kernel(table, q_ref, edges_ref, rad_ref, own_ref, core_ref, other_ref):
    odd = lax.axis_index("theta") % 2 == 1
    band = lax.axis_index("rad")
    low = band == 0
    edge_at = edge_row(band, BAND - 1, 0)
    below_coefs, above_coefs = coefficients(low, table, 0), coefficients(low, table, BAND - 1)
    edge = [q_ref[v, edge_at] for v in ALL]
    near = [rad_ref[v] for v in ALL]
    edge_prim, near_prim = primitives(edge), primitives(near)
    (fe, se), (fn, sn) = flux(edge, edge_prim, 2), flux(near, near_prim, 2)
    fastest = jnp.where(low, np.float32(1.0), np.float32(-1.0)) * jnp.maximum(se, sn)
    _, weight = step_weight(edge_prim, jnp.where(low, above_coefs[2], below_coefs[2]))
    scale = jnp.where(low, -above_coefs[0], below_coefs[1]) * weight
    change = [scale * ((fe[v] + fn[v]) - fastest * (near[v] - edge[v])) for v in ALL]
    here = lax.broadcasted_iota(jnp.int32, (BAND, AXIAL), 0) == edge_at
    for v in ALL:
        for side in (0, 1):
            at = 0 if side == 0 else SECTOR - 1
            own_ref[v, side] = edges_ref[v, side, 16:32] + jnp.where(here, change[v][at : at + 1], 0.0)
        for ref, flip in ((core_ref, jnp.logical_not(odd)), (other_ref, odd)):
            at = 32 * v
            ref[at : at + 16] = jnp.where(flip, edges_ref[v, 1, 0:16], edges_ref[v, 0, 0:16])
            ref[at + 16 : at + 32] = jnp.where(flip, own_ref[v, 1], own_ref[v, 0])
            ref[160 + v : 161 + v] = jnp.where(flip, near[v][SECTOR - 1 : SECTOR], near[v][0:1])


def masks():
    return (
        lax.broadcasted_iota(jnp.int32, (SECTOR, HALF), 1),
        lax.broadcasted_iota(jnp.int32, (SECTOR, AXIAL), 0),
    )


def row_step(coefs, q, prim, source, g_in, g_out, ends, masks, blade):
    lane, sub = masks
    a_out, a_in, inv_h, inv_r, spin_r = coefs
    f, speed = flux(q, prim, 3)
    ahead = lambda x: pltpu.roll(x, SECTOR - 1, 0)
    qn = [ahead(x) for x in q]
    fn = [qn[3]] + [ahead(f[v]) for v in range(1, 5)]
    between = face(q, (f, speed), qn, (fn, ahead(speed)))
    swirl = []
    for v in ALL:
        end = 0.0 if ends is None else ends[v]
        right = jnp.where(sub == SECTOR - 1, end, between[v])
        left = jnp.where(sub == 0, end, pltpu.roll(between[v], 1, 0))
        swirl.append(inv_h * (right - left))
    radial = [a_out * g_out[v] - a_in * g_in[v] for v in ALL]
    return advance(q, prim, source, axial_difference(q, prim, lane), radial, swirl, inv_r, inv_h, spin_r, blade)


def sweep(load, step, store):
    below, q = load(-1), load(0)
    prim = primitives(q)
    g_in = face(below, flux(below, primitives(below), 2), q, flux(q, prim, 2))
    for j in range(BAND):
        above = load(j + 1)
        above_prim = primitives(above)
        g_out = face(q, flux(q, prim, 2), above, flux(above, above_prim, 2))
        store(j, step(j, q, prim, g_in, g_out))
        q, prim, g_in = above, above_prim, g_out


def next_kernel(table, blade_ref, q_ref, qp_ref, rad_ref, next_ref):
    band = lax.axis_index("rad")
    low = band == 0
    edge_at = edge_row(band, BAND - 1, 0)
    edge = [q_ref[v, edge_at] for v in ALL]
    inner = [q_ref[v, edge_row(band, BAND - 2, 1)] for v in ALL]
    near = [rad_ref[v] for v in ALL]
    prim = primitives(edge)
    f = flux(edge, prim, 2)
    below = [jnp.where(low, inner[v], near[v]) for v in ALL]
    above = [jnp.where(low, near[v], inner[v]) for v in ALL]
    g_in = face(below, flux(below, primitives(below), 2), edge, f)
    g_out = face(edge, f, above, flux(above, primitives(above), 2))
    source = [40.0 * edge[v] - 10.0 * qp_ref[v, edge_at] for v in ALL]
    coefs = [jnp.where(low, a, b) for a, b in zip(coefficients(low, table, BAND - 1), coefficients(low, table, 0))]
    stepped = row_step(coefs, edge, prim, source, g_in, g_out, None, masks(), blades(blade_ref, SECTOR))
    for v in ALL:
        next_ref[v] = stepped[v]


def early_kernel(table, blade_ref, q_ref, qp_ref, rad_ref, p1_ref, source_ref):
    low = lax.axis_index("rad") == 0
    mask = masks()
    blade = blades(blade_ref, SECTOR)

    def load(j):
        if j < 0:
            return [jnp.where(low, MIRROR[v] * q_ref[v, 0], rad_ref[v]) for v in ALL]
        if j == BAND:
            return [jnp.where(low, rad_ref[v], MIRROR[v] * q_ref[v, BAND - 1]) for v in ALL]
        return [q_ref[v, j] for v in ALL]

    def step(j, q, prim, g_in, g_out):
        source = [40.0 * q[v] - 10.0 * qp_ref[v, j] for v in ALL]
        for v in ALL:
            source_ref[v, j] = source[v]
        return row_step(coefficients(low, table, j), q, prim, source, g_in, g_out, None, mask, blade)

    def store(j, q):
        for v in ALL:
            p1_ref[v, j] = q[v]

    sweep(load, step, store)


def final_kernel(
    total_rows,
    circle,
    table,
    blade_ref,
    edges_ref,
    own_ref,
    rad_ref,
    p1_ref,
    source_ref,
    next_ref,
    other_ref,
    core_ref,
    flow_ref,
    send_ref,
    p1,
    nearby,
    ends,
    fields,
):
    odd = lax.axis_index("theta") % 2 == 1
    band = lax.axis_index("rad")
    low = band == 0
    mask = masks()
    blade = blades(blade_ref, SECTOR)
    for v in ALL:
        p1[v] = p1_ref[v]
        nearby[v] = next_ref[v]

    geo = Columns(band * BAND, total_rows, circle)
    near_inv_h = jnp.where(low, coefficients(low, table, BAND)[2], coefficients(low, table, -1)[2])

    for side in (0, 1):
        use_core = odd if side == 0 else jnp.logical_not(odd)
        at = 0 if side == 0 else SECTOR - 1
        sign = 1.0 if side == 0 else -1.0

        def pick(first, step, count):
            spans = [slice(first + step * v, first + step * v + count) for v in ALL]
            return [jnp.where(use_core, core_ref[span], other_ref[span]) for span in spans]

        def ordered(halo, halo_prim, own, own_prim):
            a, b = flux(halo, halo_prim, 3), flux(own, own_prim, 3)
            return face(halo, a, own, b) if side == 0 else face(own, b, halo, a)

        near, near_part, corner = pick(0, 32, 16), pick(16, 32, 16), pick(160, 1, 1)
        own = [edges_ref[v, side, 0:16] for v in ALL]
        own_prim, near_prim = primitives(own), primitives(near)
        shared = ordered(near, near_prim, own, own_prim)
        own_scale = (sign * geo.inv_h) * step_weight(own_prim, geo.inv_h)[1]
        near_scale = (-sign * geo.inv_h) * step_weight(near_prim, geo.inv_h)[1]
        own_next = [own_ref[v, side] + own_scale * shared[v] for v in ALL]
        near_next = [near_part[v] + near_scale * shared[v] for v in ALL]

        edge = [rad_ref[v, at : at + 1, :] for v in ALL]
        edge_prim = primitives(edge)
        corner_face = ordered(corner, primitives(corner), edge, edge_prim)
        corner_scale = (sign * near_inv_h) * step_weight(edge_prim, near_inv_h)[1]

        faces = ordered(near_next, primitives(near_next), own_next, primitives(own_next))
        for v in ALL:
            p1[v, :, at, :] = own_next[v]
            nearby[v, at : at + 1, :] = next_ref[v, at : at + 1, :] + corner_scale * corner_face[v]
            ends[v, :, at, :] = faces[v]

    def load(j):
        if j < 0:
            return [jnp.where(low, MIRROR[v] * p1[v, 0], nearby[v]) for v in ALL]
        if j == BAND:
            return [jnp.where(low, nearby[v], MIRROR[v] * p1[v, BAND - 1]) for v in ALL]
        return [p1[v, j] for v in ALL]

    def step(j, q, prim, g_in, g_out):
        source, end = [source_ref[v, j] for v in ALL], [ends[v, j] for v in ALL]
        return row_step(coefficients(low, table, j), q, prim, source, g_in, g_out, end, mask, blade)

    def store(j, q):
        for v in ALL:
            flow_ref[v, j] = q[v]
        ux, _, _, pressure, _ = primitives(q)
        fields[0, j] = pressure
        fields[1, j] = ux

    sweep(load, step, store)
    for f in (0, 1):
        turned = fields[f].reshape(BAND * SECTOR, AXIAL).T
        send_ref[pl.ds(f, AXIAL, stride=2), :] = turned


def mode_kernel(got_ref, basis_ref, flow_ref, keep_ref, give_ref, flow_out_ref, turned, sem):
    copy = pltpu.make_async_copy(flow_ref, flow_out_ref, sem)
    copy.start()
    chips = got_ref.shape[0] // 8
    core = lax.axis_index("theta") % 2
    left = lax.broadcasted_iota(jnp.int32, (BAND, 2 * chips), 1) < chips
    parts = []
    for n in range(8):
        cells = got_ref[pl.ds(n, chips, stride=8), :]
        turned[n] = jnp.concatenate([cells, cells], axis=0).T
        rows = [turned[n, pl.ds(m, BAND, stride=SECTOR), :] for m in range(SECTOR)]
        parts.append(
            jnp.concatenate([jnp.where(left, rows[m], rows[m + 1]) for m in range(0, SECTOR, 2)], axis=1)
        )
    product = jnp.dot(
        jnp.concatenate(parts, axis=0), basis_ref[core], precision=lax.Precision.HIGHEST, preferred_element_type=F32
    )
    half = 4 * BAND
    keep_ref[...] = jnp.where(core == 0, product[:half], product[half:])
    give_ref[...] = jnp.where(core == 0, product[half:], product[:half])
    copy.wait()


def sum_kernel(keep_ref, got_ref, out_ref):
    total = keep_ref[...] + got_ref[...]
    for e in (0, 1):
        for f in (0, 1):
            n = 2 * e + f
            out_ref[e, :, 2 * MODES * f : 2 * MODES * (f + 1)] = total[BAND * n : BAND * (n + 1)]


def mode_basis(sectors):
    circle = sectors * SECTOR
    sector = 2 * np.arange(sectors // 2)[None, None, :] + np.arange(2)[:, None, None]
    cell = (np.arange(SECTOR)[None, :, None] + SECTOR * sector).reshape(2, -1)
    phase = (cell[:, :, None] * np.arange(1, MODES + 1) % circle) * (2.0 * np.pi / circle)
    return (np.concatenate([np.cos(phase), -np.sin(phase)], axis=2) / np.sqrt(circle)).astype(np.float32)


def shaped(*shape):
    return jax.ShapeDtypeStruct(shape, F32)


def vmem():
    return pl.BlockSpec(memory_space=pltpu.VMEM)


def limit(mib):
    return pltpu.CompilerParams(vmem_limit_bytes=int(mib * 2**20))


def per_device(q_level, q_prev, blade_row):
    sectors = lax.axis_size("theta")
    bands = lax.axis_size("rad")
    circle = sectors * SECTOR
    core = [(t, t ^ 1) for t in range(sectors)]
    other = [(t, (((t + 1) ^ 1) - 1) % sectors) for t in range(sectors)]
    table = geometry_table(bands * BAND, circle)
    blade = blade_row.reshape(1, AXIAL)

    hbm = pl.BlockSpec(memory_space=pltpu.HBM)
    swap = [(0, 1), (1, 0)]

    def edges(*refs):
        edge_kernel(bands * BAND, circle, *refs)

    def pack(*refs):
        pack_kernel(table, *refs)

    def neighbour(*refs):
        next_kernel(table, *refs)

    def early(*refs):
        early_kernel(table, *refs)

    def final(*refs):
        final_kernel(bands * BAND, circle, table, *refs)

    near = pl.pallas_call(
        rad_kernel,
        out_shape=shaped(5, SECTOR, AXIAL),
        in_specs=[hbm],
        out_specs=vmem(),
        scratch_shapes=[pltpu.SemaphoreType.DMA],
        compiler_params=pltpu.CompilerParams(vmem_limit_bytes=RAD_VMEM),
    )(q_level)
    rad_in = lax.ppermute(near, "rad", swap)
    q_level, q_prev = pl.pallas_call(
        load_kernel,
        out_shape=[shaped(5, BAND, SECTOR, AXIAL)] * 2,
        in_specs=[hbm] * 2,
        out_specs=[vmem()] * 2,
        scratch_shapes=[pltpu.SemaphoreType.DMA((2,))],
        compiler_params=pltpu.CompilerParams(vmem_limit_bytes=LOAD_VMEM),
        cost_estimate=pl.CostEstimate(flops=0, bytes_accessed=3_000_000, transcendentals=0),
    )(q_level, q_prev)
    edge_columns = pl.pallas_call(
        edges,
        out_shape=shaped(5, 2, 32, AXIAL),
        in_specs=[vmem()] * 3,
        out_specs=vmem(),
        scratch_shapes=[pltpu.VMEM((5, 2, 32, AXIAL), F32), pltpu.VMEM((5, 2, 2, BAND, AXIAL), F32)],
        compiler_params=limit(4),
        cost_estimate=pl.CostEstimate(flops=5_000_000, bytes_accessed=2_000_000, transcendentals=50_000),
    )(blade, q_level, q_prev)
    own_columns, core_out, other_out = pl.pallas_call(
        pack,
        out_shape=[shaped(5, 2, BAND, AXIAL)] + [shaped(168, AXIAL)] * 2,
        in_specs=[vmem()] * 3,
        out_specs=[vmem()] * 3,
        compiler_params=limit(4),
    )(q_level, edge_columns, rad_in)
    core_in = lax.ppermute(core_out, "theta", core)
    other_in = lax.ppermute(other_out, "theta", other)
    next_out = pl.pallas_call(
        neighbour,
        out_shape=shaped(5, SECTOR, AXIAL),
        in_specs=[vmem()] * 4,
        out_specs=vmem(),
        compiler_params=limit(4),
    )(blade, q_level, q_prev, rad_in)
    next_in = lax.ppermute(next_out, "rad", swap)
    part, source = pl.pallas_call(
        early,
        out_shape=[shaped(5, BAND, SECTOR, AXIAL)] * 2,
        in_specs=[vmem()] * 4,
        out_specs=[vmem()] * 2,
        compiler_params=limit(8),
        cost_estimate=pl.CostEstimate(flops=10_000_000, bytes_accessed=3_500_000, transcendentals=100_000),
    )(blade, q_level, q_prev, rad_in)
    flow_state, send = pl.pallas_call(
        final,
        out_shape=[shaped(5, BAND, SECTOR, AXIAL), shaped(2 * AXIAL, BAND * SECTOR)],
        in_specs=[vmem()] * 9,
        out_specs=[vmem()] * 2,
        scratch_shapes=[
            pltpu.VMEM((5, BAND, SECTOR, AXIAL), F32),
            pltpu.VMEM((5, SECTOR, AXIAL), F32),
            pltpu.VMEM((5, BAND, SECTOR, AXIAL), F32),
            pltpu.VMEM((2, BAND, SECTOR, AXIAL), F32),
        ],
        compiler_params=limit(8),
    )(blade, edge_columns, own_columns, rad_in, part, source, next_in, other_in, core_in)
    chips = sectors // 2
    got = lax.all_to_all(
        send.reshape(chips, 8, 128),
        "theta",
        split_axis=0,
        concat_axis=0,
        tiled=True,
        axis_index_groups=[[2 * chip + c for chip in range(chips)] for c in (0, 1)],
    )
    keep, give, flow_state = pl.pallas_call(
        mode_kernel,
        out_shape=[shaped(4 * BAND, 2 * MODES)] * 2 + [shaped(5, BAND, SECTOR, AXIAL)],
        in_specs=[vmem()] * 3,
        out_specs=[vmem(), vmem(), hbm],
        scratch_shapes=[pltpu.VMEM((8, BAND * SECTOR, 2 * chips), F32), pltpu.SemaphoreType.DMA],
        compiler_params=limit(4),
    )(got.reshape(8 * chips, 128), jnp.asarray(mode_basis(sectors)), flow_state)
    spectra = pl.pallas_call(
        sum_kernel,
        out_shape=shaped(2, BAND, 4 * MODES),
        in_specs=[vmem()] * 2,
        out_specs=vmem(),
        compiler_params=limit(2),
    )(keep, lax.ppermute(give, "theta", core))
    return flow_state, spectra


def solution(mesh):
    in_specs = (P(None, "rad", "theta", None), P(None, "rad", "theta", None), P())
    out_specs = (P(None, "rad", "theta", None), P("theta", "rad", None))
    return jax.shard_map(per_device, mesh=mesh, in_specs=in_specs, out_specs=out_specs, check_vma=False)
```

```python
import math

import jax
import jax.numpy as jnp
import numpy as np
from jax import lax
from jax.experimental import pallas as pl
from jax.experimental.pallas import tpu as pltpu
from jax.sharding import PartitionSpec as P

MODES = 64
GAMMA = 1.4
KAPPA = 2.0

BAND = 16
SECTOR = 8
AXIAL = 256
LOAD_VMEM = 55_000_000
F32 = jnp.float32
ALL = range(5)


def primitives(q):
    inverse = 1.0 / q[0]
    ux, ur, ut = q[1] * inverse, q[2] * inverse, q[3] * inverse
    pressure = (GAMMA - 1.0) * (q[4] - 0.5 * (q[1] * ux + q[2] * ur + q[3] * ut))
    sound = jnp.sqrt(GAMMA * pressure * inverse)
    return ux, ur, ut, pressure, sound


def flux(q, prim, d):
    u, pressure = prim[d - 1], prim[3]
    f = [q[d], q[1] * u, q[2] * u, q[3] * u, (q[4] + pressure) * u]
    f[d] = f[d] + pressure
    return f, jnp.abs(u) + prim[4]


def face(left_q, left_flux, right_q, right_flux):
    (fl, sl), (fr, sr) = left_flux, right_flux
    fastest = jnp.maximum(sl, sr)
    return [(fl[v] + fr[v]) - fastest * (right_q[v] - left_q[v]) for v in ALL]


HALF = AXIAL // 2


def axial_neighbour(x, lane, step, end):
    low, high = x[:, :HALF], x[:, HALF:]
    turned_low, turned_high = pltpu.roll(low, -step % HALF, 1), pltpu.roll(high, -step % HALF, 1)
    if step == 1:
        seam = lane == HALF - 1
        parts = [jnp.where(seam, turned_high, turned_low), jnp.where(seam, end, turned_high)]
    else:
        seam = lane == 0
        parts = [jnp.where(seam, end, turned_low), jnp.where(seam, turned_low, turned_high)]
    return jnp.concatenate(parts, axis=1)


def axial_difference(q, prim, lane):
    f, speed = flux(q, prim, 1)

    def following(x):
        return axial_neighbour(x, lane, 1, x[:, HALF:])

    qn = [following(x) for x in q]
    fn = [qn[1]] + [following(f[v]) for v in range(1, 5)]
    right = face(q, (f, speed), qn, (fn, following(speed)))
    return [x - axial_neighbour(x, lane, -1, 2.0 * f[v][:, :HALF]) for v, x in enumerate(right)]


def step_weight(prim, inv_h):
    ux, ur, ut, _, sound = prim
    rate = 4.0 * (jnp.abs(ux) + jnp.abs(ur)) + jnp.abs(ut) * (4.0 * inv_h) + sound * (8.0 + 4.0 * inv_h)
    return rate, 1.0 / (rate + 30.0)


def advance(q, prim, source, axial, radial, swirl, inv_r, inv_h, spin_r, blade):
    ux, ur, ut, pressure, sound = prim
    twice_r = 2.0 * inv_r
    rate, weight = step_weight(prim, inv_h)
    bladed, rotor = blade
    force = bladed * (q[3] - (rotor * spin_r) * q[0])
    gains = [None, None, twice_r * (q[3] * ut + pressure), -twice_r * (q[2] * ut) - force, -ut * force]
    out = []
    for v in ALL:
        total = source[v] - axial[v] - radial[v] - swirl[v]
        if gains[v] is not None:
            total = total + gains[v]
        out.append((rate * q[v] + total) * weight)
    return out


def geometry_table(rows, circle):
    mean = circle / (2.0 * math.pi)
    row = np.arange(rows, dtype=np.float64)
    radius = mean * (0.8 + 0.4 * (row + 0.5) / rows)
    inner = mean * (0.8 + 0.4 * row / rows)
    outer = mean * (0.8 + 0.4 * (row + 1.0) / rows)
    spacing = radius * (2.0 * math.pi / circle)
    return np.stack([outer / radius, inner / radius, 1.0 / spacing, 1.0 / radius, radius / (1.2 * mean)])


def coefficients(low, table, j):
    last = table.shape[1] - 1
    at = [min(max(j + first, 0), last) for first in (0, BAND)]
    return [jnp.where(low, np.float32(row[at[0]]), np.float32(row[at[1]])) for row in table]


def edge_row(band, at_low, at_high):
    return jnp.where(band == 0, at_low, at_high)


MIRROR = (1.0, 1.0, -1.0, 1.0, 1.0)


def blades(blade_ref, rows):
    blade = blade_ref[...]
    bladed = jnp.broadcast_to(4.0 * (blade > 0).astype(F32), (rows, AXIAL))
    rotor = jnp.broadcast_to((blade == 1).astype(F32), (rows, AXIAL))
    return bladed, rotor


def load_kernel(q_ref, qp_ref, near_ref, q_out_ref, qp_out_ref, sems):
    copies = [
        pltpu.make_async_copy(q_ref.at[:, edge_row(lax.axis_index("rad"), BAND - 1, 0)], near_ref, sems.at[0]),
        pltpu.make_async_copy(q_ref, q_out_ref, sems.at[1]),
        pltpu.make_async_copy(qp_ref, qp_out_ref, sems.at[2]),
    ]
    for copy in copies:
        copy.start()
    for copy in copies:
        copy.wait()


class Columns:
    def __init__(self, first_row, total_rows, circle):
        rows = (lax.broadcasted_iota(jnp.int32, (BAND, AXIAL), 0) + first_row).astype(F32)
        mean = circle / (2.0 * math.pi)
        radius = mean * (0.8 + 0.4 * (rows + 0.5) / total_rows)
        self.inner = mean * (0.8 + 0.4 * rows / total_rows)
        self.outer = mean * (0.8 + 0.4 * (rows + 1.0) / total_rows)
        self.inv_r = 1.0 / radius
        self.inv_h = self.inv_r * mean
        self.spin_r = radius * (1.0 / (1.2 * mean))
        self.a_h = 0.25 * self.inv_h


def edge_kernel(total_rows, circle, blade_ref, q_ref, qp_ref, edges_ref, ce, taken):
    band = lax.axis_index("rad")
    low = band == 0
    geo = Columns(band * BAND, total_rows, circle)
    blade = blades(blade_ref, BAND)
    lane = lax.broadcasted_iota(jnp.int32, (BAND, HALF), 1)
    row = lax.broadcasted_iota(jnp.int32, (BAND, AXIAL), 0)
    below_scale = jnp.where((row == 0) & jnp.logical_not(low), 0.0, geo.inv_r * geo.inner)
    above_scale = jnp.where((row == BAND - 1) & low, 0.0, geo.inv_r * geo.outer)
    for side in (0, 1):
        at, inner = (0, 1) if side == 0 else (SECTOR - 1, SECTOR - 2)
        for v in ALL:
            ce[v, side, 8:24] = q_ref[v, :, at, :]
            taken[v, side, 0] = q_ref[v, :, inner, :]
            taken[v, side, 1] = qp_ref[v, :, at, :]
    for side in (0, 1):
        edge = [ce[v, side, 8:24] for v in ALL]
        second = [taken[v, side, 0] for v in ALL]
        source = [40.0 * edge[v] - 10.0 * taken[v, side, 1] for v in ALL]
        for v in ALL:
            ce[v, side, 7:8] = MIRROR[v] * edge[v][0:1]
            ce[v, side, 24:25] = MIRROR[v] * edge[v][BAND - 1 : BAND]
        below = [ce[v, side, 7:23] for v in ALL]
        above = [ce[v, side, 9:25] for v in ALL]
        prim = primitives(edge)
        f = flux(edge, prim, 2)
        g_in = face(below, flux(below, primitives(below), 2), edge, f)
        g_out = face(edge, f, above, flux(above, primitives(above), 2))
        f = flux(edge, prim, 3)
        second_flux = flux(second, primitives(second), 3)
        if side == 0:
            swirl = [geo.inv_h * x for x in face(edge, f, second, second_flux)]
        else:
            swirl = [-geo.inv_h * x for x in face(second, second_flux, edge, f)]
        part = advance(
            edge,
            prim,
            source,
            axial_difference(edge, prim, lane),
            [above_scale * g_out[v] - below_scale * g_in[v] for v in ALL],
            swirl,
            geo.inv_r,
            geo.inv_h,
            geo.spin_r,
            blade,
        )
        for v in ALL:
            edges_ref[v, side, 0:16] = edge[v]
            edges_ref[v, side, 16:32] = part[v]


def pack_kernel(table, q_ref, edges_ref, rad_ref, own_ref, core_ref, other_ref):
    odd = lax.axis_index("theta") % 2 == 1
    band = lax.axis_index("rad")
    low = band == 0
    edge_at = edge_row(band, BAND - 1, 0)
    below_coefs, above_coefs = coefficients(low, table, 0), coefficients(low, table, BAND - 1)
    edge = [q_ref[v, edge_at] for v in ALL]
    near = [rad_ref[v] for v in ALL]
    edge_prim, near_prim = primitives(edge), primitives(near)
    (fe, se), (fn, sn) = flux(edge, edge_prim, 2), flux(near, near_prim, 2)
    fastest = jnp.where(low, np.float32(1.0), np.float32(-1.0)) * jnp.maximum(se, sn)
    _, weight = step_weight(edge_prim, jnp.where(low, above_coefs[2], below_coefs[2]))
    scale = jnp.where(low, -above_coefs[0], below_coefs[1]) * weight
    change = [scale * ((fe[v] + fn[v]) - fastest * (near[v] - edge[v])) for v in ALL]
    here = lax.broadcasted_iota(jnp.int32, (BAND, AXIAL), 0) == edge_at
    for v in ALL:
        for side in (0, 1):
            at = 0 if side == 0 else SECTOR - 1
            own_ref[v, side] = edges_ref[v, side, 16:32] + jnp.where(here, change[v][at : at + 1], 0.0)
        for ref, flip in ((core_ref, jnp.logical_not(odd)), (other_ref, odd)):
            at = 32 * v
            ref[at : at + 16] = jnp.where(flip, edges_ref[v, 1, 0:16], edges_ref[v, 0, 0:16])
            ref[at + 16 : at + 32] = jnp.where(flip, own_ref[v, 1], own_ref[v, 0])
            ref[160 + v : 161 + v] = jnp.where(flip, near[v][SECTOR - 1 : SECTOR], near[v][0:1])


def masks():
    return (
        lax.broadcasted_iota(jnp.int32, (SECTOR, HALF), 1),
        lax.broadcasted_iota(jnp.int32, (SECTOR, AXIAL), 0),
    )


def row_step(coefs, q, prim, source, g_in, g_out, ends, masks, blade):
    lane, sub = masks
    a_out, a_in, inv_h, inv_r, spin_r = coefs
    f, speed = flux(q, prim, 3)
    ahead = lambda x: pltpu.roll(x, SECTOR - 1, 0)
    qn = [ahead(x) for x in q]
    fn = [qn[3]] + [ahead(f[v]) for v in range(1, 5)]
    between = face(q, (f, speed), qn, (fn, ahead(speed)))
    swirl = []
    for v in ALL:
        end = 0.0 if ends is None else ends[v]
        right = jnp.where(sub == SECTOR - 1, end, between[v])
        left = jnp.where(sub == 0, end, pltpu.roll(between[v], 1, 0))
        swirl.append(inv_h * (right - left))
    radial = [a_out * g_out[v] - a_in * g_in[v] for v in ALL]
    return advance(q, prim, source, axial_difference(q, prim, lane), radial, swirl, inv_r, inv_h, spin_r, blade)


def sweep(load, step, store):
    below, q = load(-1), load(0)
    prim = primitives(q)
    g_in = face(below, flux(below, primitives(below), 2), q, flux(q, prim, 2))
    for j in range(BAND):
        above = load(j + 1)
        above_prim = primitives(above)
        g_out = face(q, flux(q, prim, 2), above, flux(above, above_prim, 2))
        store(j, step(j, q, prim, g_in, g_out))
        q, prim, g_in = above, above_prim, g_out


def next_kernel(table, blade_ref, q_ref, qp_ref, rad_ref, next_ref):
    band = lax.axis_index("rad")
    low = band == 0
    edge_at = edge_row(band, BAND - 1, 0)
    edge = [q_ref[v, edge_at] for v in ALL]
    inner = [q_ref[v, edge_row(band, BAND - 2, 1)] for v in ALL]
    near = [rad_ref[v] for v in ALL]
    prim = primitives(edge)
    f = flux(edge, prim, 2)
    below = [jnp.where(low, inner[v], near[v]) for v in ALL]
    above = [jnp.where(low, near[v], inner[v]) for v in ALL]
    g_in = face(below, flux(below, primitives(below), 2), edge, f)
    g_out = face(edge, f, above, flux(above, primitives(above), 2))
    source = [40.0 * edge[v] - 10.0 * qp_ref[v, edge_at] for v in ALL]
    coefs = [jnp.where(low, a, b) for a, b in zip(coefficients(low, table, BAND - 1), coefficients(low, table, 0))]
    stepped = row_step(coefs, edge, prim, source, g_in, g_out, None, masks(), blades(blade_ref, SECTOR))
    for v in ALL:
        next_ref[v] = stepped[v]


def early_kernel(table, blade_ref, q_ref, qp_ref, rad_ref, p1_ref, source_ref):
    low = lax.axis_index("rad") == 0
    mask = masks()
    blade = blades(blade_ref, SECTOR)

    def load(j):
        if j < 0:
            return [jnp.where(low, MIRROR[v] * q_ref[v, 0], rad_ref[v]) for v in ALL]
        if j == BAND:
            return [jnp.where(low, rad_ref[v], MIRROR[v] * q_ref[v, BAND - 1]) for v in ALL]
        return [q_ref[v, j] for v in ALL]

    def step(j, q, prim, g_in, g_out):
        source = [40.0 * q[v] - 10.0 * qp_ref[v, j] for v in ALL]
        for v in ALL:
            source_ref[v, j] = source[v]
        return row_step(coefficients(low, table, j), q, prim, source, g_in, g_out, None, mask, blade)

    def store(j, q):
        for v in ALL:
            p1_ref[v, j] = q[v]

    sweep(load, step, store)


def final_kernel(
    total_rows,
    circle,
    table,
    blade_ref,
    edges_ref,
    own_ref,
    rad_ref,
    p1_ref,
    source_ref,
    next_ref,
    other_ref,
    core_ref,
    flow_ref,
    send_ref,
    p1,
    nearby,
    ends,
    fields,
):
    odd = lax.axis_index("theta") % 2 == 1
    band = lax.axis_index("rad")
    low = band == 0
    mask = masks()
    blade = blades(blade_ref, SECTOR)
    for v in ALL:
        p1[v] = p1_ref[v]
        nearby[v] = next_ref[v]

    geo = Columns(band * BAND, total_rows, circle)
    near_inv_h = jnp.where(low, coefficients(low, table, BAND)[2], coefficients(low, table, -1)[2])

    for side in (0, 1):
        use_core = odd if side == 0 else jnp.logical_not(odd)
        at = 0 if side == 0 else SECTOR - 1
        sign = 1.0 if side == 0 else -1.0

        def pick(first, step, count):
            spans = [slice(first + step * v, first + step * v + count) for v in ALL]
            return [jnp.where(use_core, core_ref[span], other_ref[span]) for span in spans]

        def ordered(halo, halo_prim, own, own_prim):
            a, b = flux(halo, halo_prim, 3), flux(own, own_prim, 3)
            return face(halo, a, own, b) if side == 0 else face(own, b, halo, a)

        near, near_part, corner = pick(0, 32, 16), pick(16, 32, 16), pick(160, 1, 1)
        own = [edges_ref[v, side, 0:16] for v in ALL]
        own_prim, near_prim = primitives(own), primitives(near)
        shared = ordered(near, near_prim, own, own_prim)
        own_scale = (sign * geo.inv_h) * step_weight(own_prim, geo.inv_h)[1]
        near_scale = (-sign * geo.inv_h) * step_weight(near_prim, geo.inv_h)[1]
        own_next = [own_ref[v, side] + own_scale * shared[v] for v in ALL]
        near_next = [near_part[v] + near_scale * shared[v] for v in ALL]

        edge = [rad_ref[v, at : at + 1, :] for v in ALL]
        edge_prim = primitives(edge)
        corner_face = ordered(corner, primitives(corner), edge, edge_prim)
        corner_scale = (sign * near_inv_h) * step_weight(edge_prim, near_inv_h)[1]

        faces = ordered(near_next, primitives(near_next), own_next, primitives(own_next))
        for v in ALL:
            p1[v, :, at, :] = own_next[v]
            nearby[v, at : at + 1, :] = next_ref[v, at : at + 1, :] + corner_scale * corner_face[v]
            ends[v, :, at, :] = faces[v]

    def load(j):
        if j < 0:
            return [jnp.where(low, MIRROR[v] * p1[v, 0], nearby[v]) for v in ALL]
        if j == BAND:
            return [jnp.where(low, nearby[v], MIRROR[v] * p1[v, BAND - 1]) for v in ALL]
        return [p1[v, j] for v in ALL]

    def step(j, q, prim, g_in, g_out):
        source, end = [source_ref[v, j] for v in ALL], [ends[v, j] for v in ALL]
        return row_step(coefficients(low, table, j), q, prim, source, g_in, g_out, end, mask, blade)

    def store(j, q):
        for v in ALL:
            flow_ref[v, j] = q[v]
        ux, _, _, pressure, _ = primitives(q)
        fields[0, j] = pressure
        fields[1, j] = ux

    sweep(load, step, store)
    for f in (0, 1):
        turned = fields[f].reshape(BAND * SECTOR, AXIAL).T
        send_ref[pl.ds(f, AXIAL, stride=2), :] = turned


def write_kernel(flow_ref, out_ref, sem):
    copy = pltpu.make_async_copy(flow_ref, out_ref, sem)
    copy.start()
    copy.wait()


def mode_kernel(got_ref, basis_ref, keep_ref, give_ref, turned):
    chips = got_ref.shape[0] // 8
    core = lax.axis_index("theta") % 2
    left = lax.broadcasted_iota(jnp.int32, (BAND, 2 * chips), 1) < chips
    parts = []
    for n in range(8):
        cells = got_ref[pl.ds(n, chips, stride=8), :]
        turned[n] = jnp.concatenate([cells, cells], axis=0).T
        rows = [turned[n, pl.ds(m, BAND, stride=SECTOR), :] for m in range(SECTOR)]
        parts.append(
            jnp.concatenate([jnp.where(left, rows[m], rows[m + 1]) for m in range(0, SECTOR, 2)], axis=1)
        )
    product = jnp.dot(
        jnp.concatenate(parts, axis=0), basis_ref[core], precision=lax.Precision.HIGHEST, preferred_element_type=F32
    )
    half = 4 * BAND
    keep_ref[...] = jnp.where(core == 0, product[:half], product[half:])
    give_ref[...] = jnp.where(core == 0, product[half:], product[:half])


def sum_kernel(keep_ref, got_ref, out_ref):
    total = keep_ref[...] + got_ref[...]
    for e in (0, 1):
        for f in (0, 1):
            n = 2 * e + f
            out_ref[e, :, 2 * MODES * f : 2 * MODES * (f + 1)] = total[BAND * n : BAND * (n + 1)]


def mode_basis(sectors):
    circle = sectors * SECTOR
    sector = 2 * np.arange(sectors // 2)[None, None, :] + np.arange(2)[:, None, None]
    cell = (np.arange(SECTOR)[None, :, None] + SECTOR * sector).reshape(2, -1)
    phase = (cell[:, :, None] * np.arange(1, MODES + 1) % circle) * (2.0 * np.pi / circle)
    return (np.concatenate([np.cos(phase), -np.sin(phase)], axis=2) / np.sqrt(circle)).astype(np.float32)


def shaped(*shape):
    return jax.ShapeDtypeStruct(shape, F32)


def vmem():
    return pl.BlockSpec(memory_space=pltpu.VMEM)


def limit(mib):
    return pltpu.CompilerParams(vmem_limit_bytes=int(mib * 2**20))


def per_device(q_level, q_prev, blade_row):
    sectors = lax.axis_size("theta")
    bands = lax.axis_size("rad")
    circle = sectors * SECTOR
    core = [(t, t ^ 1) for t in range(sectors)]
    other = [(t, (((t + 1) ^ 1) - 1) % sectors) for t in range(sectors)]
    table = geometry_table(bands * BAND, circle)
    blade = blade_row.reshape(1, AXIAL)

    hbm = pl.BlockSpec(memory_space=pltpu.HBM)
    swap = [(0, 1), (1, 0)]

    def edges(*refs):
        edge_kernel(bands * BAND, circle, *refs)

    def pack(*refs):
        pack_kernel(table, *refs)

    def neighbour(*refs):
        next_kernel(table, *refs)

    def early(*refs):
        early_kernel(table, *refs)

    def final(*refs):
        final_kernel(bands * BAND, circle, table, *refs)

    near, q_level, q_prev = pl.pallas_call(
        load_kernel,
        out_shape=[shaped(5, SECTOR, AXIAL)] + [shaped(5, BAND, SECTOR, AXIAL)] * 2,
        in_specs=[hbm] * 2,
        out_specs=[vmem()] * 3,
        scratch_shapes=[pltpu.SemaphoreType.DMA((3,))],
        compiler_params=pltpu.CompilerParams(vmem_limit_bytes=LOAD_VMEM),
        cost_estimate=pl.CostEstimate(flops=0, bytes_accessed=3_000_000, transcendentals=0),
    )(q_level, q_prev)
    rad_in = lax.ppermute(near, "rad", swap)
    edge_columns = pl.pallas_call(
        edges,
        out_shape=shaped(5, 2, 32, AXIAL),
        in_specs=[vmem()] * 3,
        out_specs=vmem(),
        scratch_shapes=[pltpu.VMEM((5, 2, 32, AXIAL), F32), pltpu.VMEM((5, 2, 2, BAND, AXIAL), F32)],
        compiler_params=limit(4),
        cost_estimate=pl.CostEstimate(flops=5_000_000, bytes_accessed=2_000_000, transcendentals=50_000),
    )(blade, q_level, q_prev)
    own_columns, core_out, other_out = pl.pallas_call(
        pack,
        out_shape=[shaped(5, 2, BAND, AXIAL)] + [shaped(168, AXIAL)] * 2,
        in_specs=[vmem()] * 3,
        out_specs=[vmem()] * 3,
        compiler_params=limit(4),
    )(q_level, edge_columns, rad_in)
    core_in = lax.ppermute(core_out, "theta", core)
    other_in = lax.ppermute(other_out, "theta", other)
    next_out = pl.pallas_call(
        neighbour,
        out_shape=shaped(5, SECTOR, AXIAL),
        in_specs=[vmem()] * 4,
        out_specs=vmem(),
        compiler_params=limit(4),
    )(blade, q_level, q_prev, rad_in)
    next_in = lax.ppermute(next_out, "rad", swap)
    part, source = pl.pallas_call(
        early,
        out_shape=[shaped(5, BAND, SECTOR, AXIAL)] * 2,
        in_specs=[vmem()] * 4,
        out_specs=[vmem()] * 2,
        compiler_params=limit(8),
        cost_estimate=pl.CostEstimate(flops=10_000_000, bytes_accessed=3_500_000, transcendentals=100_000),
    )(blade, q_level, q_prev, rad_in)
    flow_state, send = pl.pallas_call(
        final,
        out_shape=[shaped(5, BAND, SECTOR, AXIAL), shaped(2 * AXIAL, BAND * SECTOR)],
        in_specs=[vmem()] * 9,
        out_specs=[vmem()] * 2,
        scratch_shapes=[
            pltpu.VMEM((5, BAND, SECTOR, AXIAL), F32),
            pltpu.VMEM((5, SECTOR, AXIAL), F32),
            pltpu.VMEM((5, BAND, SECTOR, AXIAL), F32),
            pltpu.VMEM((2, BAND, SECTOR, AXIAL), F32),
        ],
        compiler_params=limit(8),
    )(blade, edge_columns, own_columns, rad_in, part, source, next_in, other_in, core_in)
    chips = sectors // 2
    got = lax.all_to_all(
        send.reshape(chips, 8, 128),
        "theta",
        split_axis=0,
        concat_axis=0,
        tiled=True,
        axis_index_groups=[[2 * chip + c for chip in range(chips)] for c in (0, 1)],
    )
    keep, give = pl.pallas_call(
        mode_kernel,
        out_shape=[shaped(4 * BAND, 2 * MODES)] * 2,
        in_specs=[vmem()] * 2,
        out_specs=[vmem()] * 2,
        scratch_shapes=[pltpu.VMEM((8, BAND * SECTOR, 2 * chips), F32)],
        compiler_params=limit(4),
    )(got.reshape(8 * chips, 128), jnp.asarray(mode_basis(sectors)))
    given = lax.ppermute(give, "theta", core)
    flow_state = pl.pallas_call(
        write_kernel,
        out_shape=shaped(5, BAND, SECTOR, AXIAL),
        in_specs=[vmem()],
        out_specs=hbm,
        scratch_shapes=[pltpu.SemaphoreType.DMA],
        compiler_params=limit(2),
        cost_estimate=pl.CostEstimate(flops=0, bytes_accessed=1_400_000, transcendentals=0),
    )(flow_state)
    spectra = pl.pallas_call(
        sum_kernel,
        out_shape=shaped(2, BAND, 4 * MODES),
        in_specs=[vmem()] * 2,
        out_specs=vmem(),
        compiler_params=limit(2),
    )(keep, given)
    return flow_state, spectra


def solution(mesh):
    in_specs = (P(None, "rad", "theta", None), P(None, "rad", "theta", None), P())
    out_specs = (P(None, "rad", "theta", None), P("theta", "rad", None))
    return jax.shard_map(per_device, mesh=mesh, in_specs=in_specs, out_specs=out_specs, check_vma=False)
```

```python
import math

import jax
import jax.numpy as jnp
import numpy as np
from jax import lax
from jax.experimental import pallas as pl
from jax.experimental.pallas import tpu as pltpu
from jax.sharding import PartitionSpec as P

MODES = 64
GAMMA = 1.4
KAPPA = 2.0

BAND = 16
SECTOR = 8
AXIAL = 256
RAD_VMEM = 56_200_000
LOAD_VMEM = 55_000_000
F32 = jnp.float32
ALL = range(5)


def primitives(q):
    inverse = 1.0 / q[0]
    ux, ur, ut = q[1] * inverse, q[2] * inverse, q[3] * inverse
    pressure = (GAMMA - 1.0) * (q[4] - 0.5 * (q[1] * ux + q[2] * ur + q[3] * ut))
    sound = jnp.sqrt(GAMMA * pressure * inverse)
    return ux, ur, ut, pressure, sound


def flux(q, prim, d):
    u, pressure = prim[d - 1], prim[3]
    f = [q[d], q[1] * u, q[2] * u, q[3] * u, (q[4] + pressure) * u]
    f[d] = f[d] + pressure
    return f, jnp.abs(u) + prim[4]


def face(left_q, left_flux, right_q, right_flux):
    (fl, sl), (fr, sr) = left_flux, right_flux
    fastest = jnp.maximum(sl, sr)
    return [(fl[v] + fr[v]) - fastest * (right_q[v] - left_q[v]) for v in ALL]


HALF = AXIAL // 2


def axial_neighbour(x, lane, step, end):
    low, high = x[:, :HALF], x[:, HALF:]
    turned_low, turned_high = pltpu.roll(low, -step % HALF, 1), pltpu.roll(high, -step % HALF, 1)
    if step == 1:
        seam = lane == HALF - 1
        parts = [jnp.where(seam, turned_high, turned_low), jnp.where(seam, end, turned_high)]
    else:
        seam = lane == 0
        parts = [jnp.where(seam, end, turned_low), jnp.where(seam, turned_low, turned_high)]
    return jnp.concatenate(parts, axis=1)


def axial_difference(q, prim, lane):
    f, speed = flux(q, prim, 1)

    def following(x):
        return axial_neighbour(x, lane, 1, x[:, HALF:])

    qn = [following(x) for x in q]
    fn = [qn[1]] + [following(f[v]) for v in range(1, 5)]
    right = face(q, (f, speed), qn, (fn, following(speed)))
    return [x - axial_neighbour(x, lane, -1, 2.0 * f[v][:, :HALF]) for v, x in enumerate(right)]


def step_weight(prim, inv_h):
    ux, ur, ut, _, sound = prim
    rate = 4.0 * (jnp.abs(ux) + jnp.abs(ur)) + jnp.abs(ut) * (4.0 * inv_h) + sound * (8.0 + 4.0 * inv_h)
    return rate, 1.0 / (rate + 30.0)


def blade_force(q, spin_r, blade):
    bladed, rotor = blade
    return bladed * (q[3] - (rotor * spin_r) * q[0])


def advance(q, prim, source, axial, radial, swirl, inv_r, inv_h, spin_r, blade):
    ux, ur, ut, pressure, sound = prim
    twice_r = 2.0 * inv_r
    rate, weight = step_weight(prim, inv_h)
    gains = [None, None, twice_r * (q[3] * ut + pressure), -twice_r * (q[2] * ut), None]
    if blade is not None:
        force = blade_force(q, spin_r, blade)
        gains[3] = gains[3] - force
        gains[4] = -ut * force
    out = []
    for v in ALL:
        total = source[v] - axial[v] - radial[v] - swirl[v]
        if gains[v] is not None:
            total = total + gains[v]
        out.append((rate * q[v] + total) * weight)
    return out


def geometry_table(rows, circle):
    mean = circle / (2.0 * math.pi)
    row = np.arange(rows, dtype=np.float64)
    radius = mean * (0.8 + 0.4 * (row + 0.5) / rows)
    inner = mean * (0.8 + 0.4 * row / rows)
    outer = mean * (0.8 + 0.4 * (row + 1.0) / rows)
    spacing = radius * (2.0 * math.pi / circle)
    return np.stack([outer / radius, inner / radius, 1.0 / spacing, 1.0 / radius, radius / (1.2 * mean)])


def coefficients(low, table, j):
    last = table.shape[1] - 1
    at = [min(max(j + first, 0), last) for first in (0, BAND)]
    return [jnp.where(low, np.float32(row[at[0]]), np.float32(row[at[1]])) for row in table]


def edge_row(band, at_low, at_high):
    return jnp.where(band == 0, at_low, at_high)


MIRROR = (1.0, 1.0, -1.0, 1.0, 1.0)


def blades(blade_ref, rows):
    blade = blade_ref[...]
    bladed = jnp.broadcast_to(4.0 * (blade > 0).astype(F32), (rows, AXIAL))
    rotor = jnp.broadcast_to((blade == 1).astype(F32), (rows, AXIAL))
    return bladed, rotor


def rad_kernel(q_ref, near_ref, sem):
    copy = pltpu.make_async_copy(q_ref.at[:, edge_row(lax.axis_index("rad"), BAND - 1, 0)], near_ref, sem)
    copy.start()
    copy.wait()


def load_kernel(q_ref, qp_ref, q_out_ref, qp_out_ref, sems):
    copies = [
        pltpu.make_async_copy(q_ref, q_out_ref, sems.at[0]),
        pltpu.make_async_copy(qp_ref, qp_out_ref, sems.at[1]),
    ]
    for copy in copies:
        copy.start()
    for copy in copies:
        copy.wait()


class Columns:
    def __init__(self, first_row, total_rows, circle):
        rows = (lax.broadcasted_iota(jnp.int32, (BAND, AXIAL), 0) + first_row).astype(F32)
        mean = circle / (2.0 * math.pi)
        radius = mean * (0.8 + 0.4 * (rows + 0.5) / total_rows)
        self.inner = mean * (0.8 + 0.4 * rows / total_rows)
        self.outer = mean * (0.8 + 0.4 * (rows + 1.0) / total_rows)
        self.inv_r = 1.0 / radius
        self.inv_h = self.inv_r * mean
        self.spin_r = radius * (1.0 / (1.2 * mean))
        self.a_h = 0.25 * self.inv_h


def edge_kernel(total_rows, circle, q_ref, qp_ref, edges_ref, ce, taken):
    band = lax.axis_index("rad")
    low = band == 0
    geo = Columns(band * BAND, total_rows, circle)
    lane = lax.broadcasted_iota(jnp.int32, (BAND, HALF), 1)
    row = lax.broadcasted_iota(jnp.int32, (BAND, AXIAL), 0)
    below_scale = jnp.where((row == 0) & jnp.logical_not(low), 0.0, geo.inv_r * geo.inner)
    above_scale = jnp.where((row == BAND - 1) & low, 0.0, geo.inv_r * geo.outer)
    for side in (0, 1):
        at, inner = (0, 1) if side == 0 else (SECTOR - 1, SECTOR - 2)
        for v in ALL:
            ce[v, side, 8:24] = q_ref[v, :, at, :]
            taken[v, side, 0] = q_ref[v, :, inner, :]
            taken[v, side, 1] = qp_ref[v, :, at, :]
    for side in (0, 1):
        edge = [ce[v, side, 8:24] for v in ALL]
        second = [taken[v, side, 0] for v in ALL]
        source = [40.0 * edge[v] - 10.0 * taken[v, side, 1] for v in ALL]
        for v in ALL:
            ce[v, side, 7:8] = MIRROR[v] * edge[v][0:1]
            ce[v, side, 24:25] = MIRROR[v] * edge[v][BAND - 1 : BAND]
        below = [ce[v, side, 7:23] for v in ALL]
        above = [ce[v, side, 9:25] for v in ALL]
        prim = primitives(edge)
        f = flux(edge, prim, 2)
        g_in = face(below, flux(below, primitives(below), 2), edge, f)
        g_out = face(edge, f, above, flux(above, primitives(above), 2))
        f = flux(edge, prim, 3)
        second_flux = flux(second, primitives(second), 3)
        if side == 0:
            swirl = [geo.inv_h * x for x in face(edge, f, second, second_flux)]
        else:
            swirl = [-geo.inv_h * x for x in face(second, second_flux, edge, f)]
        part = advance(
            edge,
            prim,
            source,
            axial_difference(edge, prim, lane),
            [above_scale * g_out[v] - below_scale * g_in[v] for v in ALL],
            swirl,
            geo.inv_r,
            geo.inv_h,
            geo.spin_r,
            None,
        )
        for v in ALL:
            edges_ref[v, side, 0:16] = edge[v]
            edges_ref[v, side, 16:32] = part[v]


def pack_kernel(table, q_ref, edges_ref, rad_ref, own_ref, core_ref, other_ref):
    odd = lax.axis_index("theta") % 2 == 1
    band = lax.axis_index("rad")
    low = band == 0
    edge_at = edge_row(band, BAND - 1, 0)
    below_coefs, above_coefs = coefficients(low, table, 0), coefficients(low, table, BAND - 1)
    edge = [q_ref[v, edge_at] for v in ALL]
    near = [rad_ref[v] for v in ALL]
    edge_prim, near_prim = primitives(edge), primitives(near)
    (fe, se), (fn, sn) = flux(edge, edge_prim, 2), flux(near, near_prim, 2)
    fastest = jnp.where(low, np.float32(1.0), np.float32(-1.0)) * jnp.maximum(se, sn)
    _, weight = step_weight(edge_prim, jnp.where(low, above_coefs[2], below_coefs[2]))
    scale = jnp.where(low, -above_coefs[0], below_coefs[1]) * weight
    change = [scale * ((fe[v] + fn[v]) - fastest * (near[v] - edge[v])) for v in ALL]
    here = lax.broadcasted_iota(jnp.int32, (BAND, AXIAL), 0) == edge_at
    for v in ALL:
        for side in (0, 1):
            at = 0 if side == 0 else SECTOR - 1
            own_ref[v, side] = edges_ref[v, side, 16:32] + jnp.where(here, change[v][at : at + 1], 0.0)
        for ref, flip in ((core_ref, jnp.logical_not(odd)), (other_ref, odd)):
            at = 32 * v
            ref[at : at + 16] = jnp.where(flip, edges_ref[v, 1, 0:16], edges_ref[v, 0, 0:16])
            ref[at + 16 : at + 32] = jnp.where(flip, own_ref[v, 1], own_ref[v, 0])
            ref[160 + v : 161 + v] = jnp.where(flip, near[v][SECTOR - 1 : SECTOR], near[v][0:1])


def masks():
    return (
        lax.broadcasted_iota(jnp.int32, (SECTOR, HALF), 1),
        lax.broadcasted_iota(jnp.int32, (SECTOR, AXIAL), 0),
    )


def row_step(coefs, q, prim, source, g_in, g_out, ends, masks, blade):
    lane, sub = masks
    a_out, a_in, inv_h, inv_r, spin_r = coefs
    f, speed = flux(q, prim, 3)
    ahead = lambda x: pltpu.roll(x, SECTOR - 1, 0)
    qn = [ahead(x) for x in q]
    fn = [qn[3]] + [ahead(f[v]) for v in range(1, 5)]
    between = face(q, (f, speed), qn, (fn, ahead(speed)))
    swirl = []
    for v in ALL:
        end = 0.0 if ends is None else ends[v]
        right = jnp.where(sub == SECTOR - 1, end, between[v])
        left = jnp.where(sub == 0, end, pltpu.roll(between[v], 1, 0))
        swirl.append(inv_h * (right - left))
    radial = [a_out * g_out[v] - a_in * g_in[v] for v in ALL]
    return advance(q, prim, source, axial_difference(q, prim, lane), radial, swirl, inv_r, inv_h, spin_r, blade)


def sweep(load, step, store):
    below, q = load(-1), load(0)
    prim = primitives(q)
    g_in = face(below, flux(below, primitives(below), 2), q, flux(q, prim, 2))
    for j in range(BAND):
        above = load(j + 1)
        above_prim = primitives(above)
        g_out = face(q, flux(q, prim, 2), above, flux(above, above_prim, 2))
        store(j, step(j, q, prim, g_in, g_out))
        q, prim, g_in = above, above_prim, g_out


def next_kernel(table, blade_ref, q_ref, qp_ref, rad_ref, next_ref):
    band = lax.axis_index("rad")
    low = band == 0
    edge_at = edge_row(band, BAND - 1, 0)
    edge = [q_ref[v, edge_at] for v in ALL]
    inner = [q_ref[v, edge_row(band, BAND - 2, 1)] for v in ALL]
    near = [rad_ref[v] for v in ALL]
    prim = primitives(edge)
    f = flux(edge, prim, 2)
    below = [jnp.where(low, inner[v], near[v]) for v in ALL]
    above = [jnp.where(low, near[v], inner[v]) for v in ALL]
    g_in = face(below, flux(below, primitives(below), 2), edge, f)
    g_out = face(edge, f, above, flux(above, primitives(above), 2))
    source = [40.0 * edge[v] - 10.0 * qp_ref[v, edge_at] for v in ALL]
    coefs = [jnp.where(low, a, b) for a, b in zip(coefficients(low, table, BAND - 1), coefficients(low, table, 0))]
    stepped = row_step(coefs, edge, prim, source, g_in, g_out, None, masks(), blades(blade_ref, SECTOR))
    for v in ALL:
        next_ref[v] = stepped[v]


def early_kernel(table, blade_ref, q_ref, qp_ref, rad_ref, p1_ref, source_ref):
    low = lax.axis_index("rad") == 0
    mask = masks()
    blade = blades(blade_ref, SECTOR)

    def load(j):
        if j < 0:
            return [jnp.where(low, MIRROR[v] * q_ref[v, 0], rad_ref[v]) for v in ALL]
        if j == BAND:
            return [jnp.where(low, rad_ref[v], MIRROR[v] * q_ref[v, BAND - 1]) for v in ALL]
        return [q_ref[v, j] for v in ALL]

    def step(j, q, prim, g_in, g_out):
        source = [40.0 * q[v] - 10.0 * qp_ref[v, j] for v in ALL]
        for v in ALL:
            source_ref[v, j] = source[v]
        return row_step(coefficients(low, table, j), q, prim, source, g_in, g_out, None, mask, blade)

    def store(j, q):
        for v in ALL:
            p1_ref[v, j] = q[v]

    sweep(load, step, store)


def final_kernel(
    total_rows,
    circle,
    table,
    blade_ref,
    edges_ref,
    own_ref,
    rad_ref,
    p1_ref,
    source_ref,
    next_ref,
    other_ref,
    core_ref,
    flow_ref,
    send_ref,
    p1,
    nearby,
    ends,
    fields,
):
    odd = lax.axis_index("theta") % 2 == 1
    band = lax.axis_index("rad")
    low = band == 0
    mask = masks()
    blade = blades(blade_ref, SECTOR)
    for v in ALL:
        p1[v] = p1_ref[v]
        nearby[v] = next_ref[v]

    geo = Columns(band * BAND, total_rows, circle)
    column_blade = blades(blade_ref, BAND)
    near_inv_h = jnp.where(low, coefficients(low, table, BAND)[2], coefficients(low, table, -1)[2])

    for side in (0, 1):
        use_core = odd if side == 0 else jnp.logical_not(odd)
        at = 0 if side == 0 else SECTOR - 1
        sign = 1.0 if side == 0 else -1.0

        def pick(first, step, count):
            spans = [slice(first + step * v, first + step * v + count) for v in ALL]
            return [jnp.where(use_core, core_ref[span], other_ref[span]) for span in spans]

        def ordered(halo, halo_prim, own, own_prim):
            a, b = flux(halo, halo_prim, 3), flux(own, own_prim, 3)
            return face(halo, a, own, b) if side == 0 else face(own, b, halo, a)

        near, near_part, corner = pick(0, 32, 16), pick(16, 32, 16), pick(160, 1, 1)
        own = [edges_ref[v, side, 0:16] for v in ALL]
        own_prim, near_prim = primitives(own), primitives(near)
        shared = ordered(near, near_prim, own, own_prim)
        own_part = [own_ref[v, side] for v in ALL]
        own_next, near_next = [], []
        for q, prim, part, scale, out in (
            (own, own_prim, own_part, sign * geo.inv_h, own_next),
            (near, near_prim, near_part, -sign * geo.inv_h, near_next),
        ):
            force = blade_force(q, geo.spin_r, column_blade)
            change = [scale * x for x in shared]
            change[3] = change[3] - force
            change[4] = change[4] - prim[2] * force
            weight = step_weight(prim, geo.inv_h)[1]
            out.extend(part[v] + weight * change[v] for v in ALL)

        edge = [rad_ref[v, at : at + 1, :] for v in ALL]
        edge_prim = primitives(edge)
        corner_face = ordered(corner, primitives(corner), edge, edge_prim)
        corner_scale = (sign * near_inv_h) * step_weight(edge_prim, near_inv_h)[1]

        faces = ordered(near_next, primitives(near_next), own_next, primitives(own_next))
        for v in ALL:
            p1[v, :, at, :] = own_next[v]
            nearby[v, at : at + 1, :] = next_ref[v, at : at + 1, :] + corner_scale * corner_face[v]
            ends[v, :, at, :] = faces[v]

    def load(j):
        if j < 0:
            return [jnp.where(low, MIRROR[v] * p1[v, 0], nearby[v]) for v in ALL]
        if j == BAND:
            return [jnp.where(low, nearby[v], MIRROR[v] * p1[v, BAND - 1]) for v in ALL]
        return [p1[v, j] for v in ALL]

    def step(j, q, prim, g_in, g_out):
        source, end = [source_ref[v, j] for v in ALL], [ends[v, j] for v in ALL]
        return row_step(coefficients(low, table, j), q, prim, source, g_in, g_out, end, mask, blade)

    def store(j, q):
        for v in ALL:
            flow_ref[v, j] = q[v]
        ux, _, _, pressure, _ = primitives(q)
        fields[0, j] = pressure
        fields[1, j] = ux

    sweep(load, step, store)
    for f in (0, 1):
        turned = fields[f].reshape(BAND * SECTOR, AXIAL).T
        send_ref[pl.ds(f, AXIAL, stride=2), :] = turned


def write_kernel(flow_ref, out_ref, sem):
    copy = pltpu.make_async_copy(flow_ref, out_ref, sem)
    copy.start()
    copy.wait()


def mode_kernel(got_ref, basis_ref, keep_ref, give_ref, turned):
    chips = got_ref.shape[0] // 8
    core = lax.axis_index("theta") % 2
    left = lax.broadcasted_iota(jnp.int32, (BAND, 2 * chips), 1) < chips
    parts = []
    for n in range(8):
        cells = got_ref[pl.ds(n, chips, stride=8), :]
        turned[n] = jnp.concatenate([cells, cells], axis=0).T
        rows = [turned[n, pl.ds(m, BAND, stride=SECTOR), :] for m in range(SECTOR)]
        parts.append(
            jnp.concatenate([jnp.where(left, rows[m], rows[m + 1]) for m in range(0, SECTOR, 2)], axis=1)
        )
    product = jnp.dot(
        jnp.concatenate(parts, axis=0), basis_ref[core], precision=lax.Precision.HIGHEST, preferred_element_type=F32
    )
    half = 4 * BAND
    keep_ref[...] = jnp.where(core == 0, product[:half], product[half:])
    give_ref[...] = jnp.where(core == 0, product[half:], product[:half])


def sum_kernel(keep_ref, got_ref, out_ref):
    total = keep_ref[...] + got_ref[...]
    for e in (0, 1):
        for f in (0, 1):
            n = 2 * e + f
            out_ref[e, :, 2 * MODES * f : 2 * MODES * (f + 1)] = total[BAND * n : BAND * (n + 1)]


def mode_basis(sectors):
    circle = sectors * SECTOR
    sector = 2 * np.arange(sectors // 2)[None, None, :] + np.arange(2)[:, None, None]
    cell = (np.arange(SECTOR)[None, :, None] + SECTOR * sector).reshape(2, -1)
    phase = (cell[:, :, None] * np.arange(1, MODES + 1) % circle) * (2.0 * np.pi / circle)
    return (np.concatenate([np.cos(phase), -np.sin(phase)], axis=2) / np.sqrt(circle)).astype(np.float32)


def shaped(*shape):
    return jax.ShapeDtypeStruct(shape, F32)


def vmem():
    return pl.BlockSpec(memory_space=pltpu.VMEM)


def limit(mib):
    return pltpu.CompilerParams(vmem_limit_bytes=int(mib * 2**20))


def per_device(q_level, q_prev, blade_row):
    sectors = lax.axis_size("theta")
    bands = lax.axis_size("rad")
    circle = sectors * SECTOR
    core = [(t, t ^ 1) for t in range(sectors)]
    other = [(t, (((t + 1) ^ 1) - 1) % sectors) for t in range(sectors)]
    table = geometry_table(bands * BAND, circle)
    blade = blade_row.reshape(1, AXIAL)

    hbm = pl.BlockSpec(memory_space=pltpu.HBM)
    swap = [(0, 1), (1, 0)]

    def edges(*refs):
        edge_kernel(bands * BAND, circle, *refs)

    def pack(*refs):
        pack_kernel(table, *refs)

    def neighbour(*refs):
        next_kernel(table, *refs)

    def early(*refs):
        early_kernel(table, *refs)

    def final(*refs):
        final_kernel(bands * BAND, circle, table, *refs)

    near = pl.pallas_call(
        rad_kernel,
        out_shape=shaped(5, SECTOR, AXIAL),
        in_specs=[hbm],
        out_specs=vmem(),
        scratch_shapes=[pltpu.SemaphoreType.DMA],
        compiler_params=pltpu.CompilerParams(vmem_limit_bytes=RAD_VMEM),
    )(q_level)
    rad_in = lax.ppermute(near, "rad", swap)
    q_level, q_prev = pl.pallas_call(
        load_kernel,
        out_shape=[shaped(5, BAND, SECTOR, AXIAL)] * 2,
        in_specs=[hbm] * 2,
        out_specs=[vmem()] * 2,
        scratch_shapes=[pltpu.SemaphoreType.DMA((2,))],
        compiler_params=pltpu.CompilerParams(vmem_limit_bytes=LOAD_VMEM),
        cost_estimate=pl.CostEstimate(flops=0, bytes_accessed=3_000_000, transcendentals=0),
    )(q_level, q_prev)
    edge_columns = pl.pallas_call(
        edges,
        out_shape=shaped(5, 2, 32, AXIAL),
        in_specs=[vmem()] * 2,
        out_specs=vmem(),
        scratch_shapes=[pltpu.VMEM((5, 2, 32, AXIAL), F32), pltpu.VMEM((5, 2, 2, BAND, AXIAL), F32)],
        compiler_params=limit(4),
        cost_estimate=pl.CostEstimate(flops=5_000_000, bytes_accessed=2_000_000, transcendentals=50_000),
    )(q_level, q_prev)
    own_columns, core_out, other_out = pl.pallas_call(
        pack,
        out_shape=[shaped(5, 2, BAND, AXIAL)] + [shaped(168, AXIAL)] * 2,
        in_specs=[vmem()] * 3,
        out_specs=[vmem()] * 3,
        compiler_params=limit(4),
    )(q_level, edge_columns, rad_in)
    core_in = lax.ppermute(core_out, "theta", core)
    other_in = lax.ppermute(other_out, "theta", other)
    next_out = pl.pallas_call(
        neighbour,
        out_shape=shaped(5, SECTOR, AXIAL),
        in_specs=[vmem()] * 4,
        out_specs=vmem(),
        compiler_params=limit(4),
    )(blade, q_level, q_prev, rad_in)
    next_in = lax.ppermute(next_out, "rad", swap)
    part, source = pl.pallas_call(
        early,
        out_shape=[shaped(5, BAND, SECTOR, AXIAL)] * 2,
        in_specs=[vmem()] * 4,
        out_specs=[vmem()] * 2,
        compiler_params=limit(8),
        cost_estimate=pl.CostEstimate(flops=10_000_000, bytes_accessed=3_500_000, transcendentals=100_000),
    )(blade, q_level, q_prev, rad_in)
    flow_state, send = pl.pallas_call(
        final,
        out_shape=[shaped(5, BAND, SECTOR, AXIAL), shaped(2 * AXIAL, BAND * SECTOR)],
        in_specs=[vmem()] * 9,
        out_specs=[vmem()] * 2,
        scratch_shapes=[
            pltpu.VMEM((5, BAND, SECTOR, AXIAL), F32),
            pltpu.VMEM((5, SECTOR, AXIAL), F32),
            pltpu.VMEM((5, BAND, SECTOR, AXIAL), F32),
            pltpu.VMEM((2, BAND, SECTOR, AXIAL), F32),
        ],
        compiler_params=limit(8),
    )(blade, edge_columns, own_columns, rad_in, part, source, next_in, other_in, core_in)
    chips = sectors // 2
    got = lax.all_to_all(
        send.reshape(chips, 8, 128),
        "theta",
        split_axis=0,
        concat_axis=0,
        tiled=True,
        axis_index_groups=[[2 * chip + c for chip in range(chips)] for c in (0, 1)],
    )
    keep, give = pl.pallas_call(
        mode_kernel,
        out_shape=[shaped(4 * BAND, 2 * MODES)] * 2,
        in_specs=[vmem()] * 2,
        out_specs=[vmem()] * 2,
        scratch_shapes=[pltpu.VMEM((8, BAND * SECTOR, 2 * chips), F32)],
        compiler_params=limit(4),
    )(got.reshape(8 * chips, 128), jnp.asarray(mode_basis(sectors)))
    given = lax.ppermute(give, "theta", core)
    flow_state = pl.pallas_call(
        write_kernel,
        out_shape=shaped(5, BAND, SECTOR, AXIAL),
        in_specs=[vmem()],
        out_specs=hbm,
        scratch_shapes=[pltpu.SemaphoreType.DMA],
        compiler_params=limit(2),
        cost_estimate=pl.CostEstimate(flops=0, bytes_accessed=1_400_000, transcendentals=0),
    )(flow_state)
    spectra = pl.pallas_call(
        sum_kernel,
        out_shape=shaped(2, BAND, 4 * MODES),
        in_specs=[vmem()] * 2,
        out_specs=vmem(),
        compiler_params=limit(2),
    )(keep, given)
    return flow_state, spectra


def solution(mesh):
    in_specs = (P(None, "rad", "theta", None), P(None, "rad", "theta", None), P())
    out_specs = (P(None, "rad", "theta", None), P("theta", "rad", None))
    return jax.shard_map(per_device, mesh=mesh, in_specs=in_specs, out_specs=out_specs, check_vma=False)
```

```python
import math

import jax
import jax.numpy as jnp
import numpy as np
from jax import lax
from jax.experimental import pallas as pl
from jax.experimental.pallas import tpu as pltpu
from jax.sharding import PartitionSpec as P

MODES = 64
GAMMA = 1.4
KAPPA = 2.0

BAND = 16
SECTOR = 8
AXIAL = 256
RING = 16
LOAD_VMEM = 55_000_000
F32 = jnp.float32
ALL = range(5)


def primitives(q):
    inverse = 1.0 / q[0]
    ux, ur, ut = q[1] * inverse, q[2] * inverse, q[3] * inverse
    pressure = (GAMMA - 1.0) * (q[4] - 0.5 * (q[1] * ux + q[2] * ur + q[3] * ut))
    sound = jnp.sqrt(GAMMA * pressure * inverse)
    return ux, ur, ut, pressure, sound


def flux(q, prim, d):
    u, pressure = prim[d - 1], prim[3]
    f = [q[d], q[1] * u, q[2] * u, q[3] * u, (q[4] + pressure) * u]
    f[d] = f[d] + pressure
    return f, jnp.abs(u) + prim[4]


def face(left_q, left_flux, right_q, right_flux):
    (fl, sl), (fr, sr) = left_flux, right_flux
    fastest = jnp.maximum(sl, sr)
    return [(fl[v] + fr[v]) - fastest * (right_q[v] - left_q[v]) for v in ALL]


HALF = AXIAL // 2


def axial_neighbour(x, lane, step, end):
    low, high = x[:, :HALF], x[:, HALF:]
    turned_low, turned_high = pltpu.roll(low, -step % HALF, 1), pltpu.roll(high, -step % HALF, 1)
    if step == 1:
        seam = lane == HALF - 1
        parts = [jnp.where(seam, turned_high, turned_low), jnp.where(seam, end, turned_high)]
    else:
        seam = lane == 0
        parts = [jnp.where(seam, end, turned_low), jnp.where(seam, turned_low, turned_high)]
    return jnp.concatenate(parts, axis=1)


def axial_difference(q, prim, lane):
    f, speed = flux(q, prim, 1)

    def following(x):
        return axial_neighbour(x, lane, 1, x[:, HALF:])

    qn = [following(x) for x in q]
    fn = [qn[1]] + [following(f[v]) for v in range(1, 5)]
    right = face(q, (f, speed), qn, (fn, following(speed)))
    return [x - axial_neighbour(x, lane, -1, 2.0 * f[v][:, :HALF]) for v, x in enumerate(right)]


def step_weight(prim, inv_h):
    ux, ur, ut, _, sound = prim
    rate = 4.0 * (jnp.abs(ux) + jnp.abs(ur)) + jnp.abs(ut) * (4.0 * inv_h) + sound * (8.0 + 4.0 * inv_h)
    return rate, 1.0 / (rate + 30.0)


def blade_force(q, spin_r, blade):
    bladed, rotor = blade
    return bladed * (q[3] - (rotor * spin_r) * q[0])


def advance(q, prim, source, axial, radial, swirl, inv_r, inv_h, spin_r, blade):
    ux, ur, ut, pressure, sound = prim
    twice_r = 2.0 * inv_r
    rate, weight = step_weight(prim, inv_h)
    gains = [None, None, twice_r * (q[3] * ut + pressure), -twice_r * (q[2] * ut), None]
    if blade is not None:
        force = blade_force(q, spin_r, blade)
        gains[3] = gains[3] - force
        gains[4] = -ut * force
    out = []
    for v in ALL:
        total = source[v] - axial[v] - radial[v] - swirl[v]
        if gains[v] is not None:
            total = total + gains[v]
        out.append((rate * q[v] + total) * weight)
    return out


def geometry_table(rows, circle):
    mean = circle / (2.0 * math.pi)
    row = np.arange(rows, dtype=np.float64)
    radius = mean * (0.8 + 0.4 * (row + 0.5) / rows)
    inner = mean * (0.8 + 0.4 * row / rows)
    outer = mean * (0.8 + 0.4 * (row + 1.0) / rows)
    spacing = radius * (2.0 * math.pi / circle)
    return np.stack([outer / radius, inner / radius, 1.0 / spacing, 1.0 / radius, radius / (1.2 * mean)])


def coefficients(low, table, j):
    last = table.shape[1] - 1
    at = [min(max(j + first, 0), last) for first in (0, BAND)]
    return [jnp.where(low, np.float32(row[at[0]]), np.float32(row[at[1]])) for row in table]


def edge_row(band, at_low, at_high):
    return jnp.where(band == 0, at_low, at_high)


MIRROR = (1.0, 1.0, -1.0, 1.0, 1.0)


def blades(blade_ref, rows):
    blade = blade_ref[...]
    bladed = jnp.broadcast_to(4.0 * (blade > 0).astype(F32), (rows, AXIAL))
    rotor = jnp.broadcast_to((blade == 1).astype(F32), (rows, AXIAL))
    return bladed, rotor


def load_kernel(q_ref, qp_ref, near_ref, q_out_ref, qp_out_ref, sems):
    copies = [
        pltpu.make_async_copy(q_ref.at[:, edge_row(lax.axis_index("rad"), BAND - 1, 0)], near_ref, sems.at[0]),
        pltpu.make_async_copy(q_ref, q_out_ref, sems.at[1]),
        pltpu.make_async_copy(qp_ref, qp_out_ref, sems.at[2]),
    ]
    for copy in copies:
        copy.start()
    for copy in copies:
        copy.wait()


def is_late():
    return lax.axis_index("theta") % RING == RING - 1


class Columns:
    def __init__(self, first_row, total_rows, circle):
        rows = (lax.broadcasted_iota(jnp.int32, (BAND, AXIAL), 0) + first_row).astype(F32)
        mean = circle / (2.0 * math.pi)
        radius = mean * (0.8 + 0.4 * (rows + 0.5) / total_rows)
        self.inner = mean * (0.8 + 0.4 * rows / total_rows)
        self.outer = mean * (0.8 + 0.4 * (rows + 1.0) / total_rows)
        self.inv_r = 1.0 / radius
        self.inv_h = self.inv_r * mean
        self.spin_r = radius * (1.0 / (1.2 * mean))
        self.a_h = 0.25 * self.inv_h


def edge_kernel(total_rows, circle, q_ref, qp_ref, edges_ref, ce, taken):
    band = lax.axis_index("rad")
    low = band == 0
    geo = Columns(band * BAND, total_rows, circle)
    lane = lax.broadcasted_iota(jnp.int32, (BAND, HALF), 1)
    row = lax.broadcasted_iota(jnp.int32, (BAND, AXIAL), 0)
    below_scale = jnp.where((row == 0) & jnp.logical_not(low), 0.0, geo.inv_r * geo.inner)
    above_scale = jnp.where((row == BAND - 1) & low, 0.0, geo.inv_r * geo.outer)
    for side in (0, 1):
        at, inner = (0, 1) if side == 0 else (SECTOR - 1, SECTOR - 2)
        for v in ALL:
            ce[v, side, 8:24] = q_ref[v, :, at, :]
            taken[v, side, 0] = q_ref[v, :, inner, :]
            taken[v, side, 1] = qp_ref[v, :, at, :]
    for side in (0, 1):
        edge = [ce[v, side, 8:24] for v in ALL]
        second = [taken[v, side, 0] for v in ALL]
        source = [40.0 * edge[v] - 10.0 * taken[v, side, 1] for v in ALL]
        for v in ALL:
            ce[v, side, 7:8] = MIRROR[v] * edge[v][0:1]
            ce[v, side, 24:25] = MIRROR[v] * edge[v][BAND - 1 : BAND]
        below = [ce[v, side, 7:23] for v in ALL]
        above = [ce[v, side, 9:25] for v in ALL]
        prim = primitives(edge)
        f = flux(edge, prim, 2)
        g_in = face(below, flux(below, primitives(below), 2), edge, f)
        g_out = face(edge, f, above, flux(above, primitives(above), 2))
        f = flux(edge, prim, 3)
        second_flux = flux(second, primitives(second), 3)
        if side == 0:
            swirl = [geo.inv_h * x for x in face(edge, f, second, second_flux)]
        else:
            swirl = [-geo.inv_h * x for x in face(second, second_flux, edge, f)]
        part = advance(
            edge,
            prim,
            source,
            axial_difference(edge, prim, lane),
            [above_scale * g_out[v] - below_scale * g_in[v] for v in ALL],
            swirl,
            geo.inv_r,
            geo.inv_h,
            geo.spin_r,
            None,
        )
        for v in ALL:
            edges_ref[v, side, 0:16] = edge[v]
            edges_ref[v, side, 16:32] = part[v]


def closing(table, low, edge, near):
    coefs = [coefficients(low, table, j) for j in (0, BAND - 1)]
    edge_prim, near_prim = primitives(edge), primitives(near)
    (fe, se), (fn, sn) = flux(edge, edge_prim, 2), flux(near, near_prim, 2)
    fastest = jnp.where(low, np.float32(1.0), np.float32(-1.0)) * jnp.maximum(se, sn)
    _, weight = step_weight(edge_prim, jnp.where(low, coefs[1][2], coefs[0][2]))
    scale = jnp.where(low, -coefs[1][0], coefs[0][1]) * weight
    return [scale * ((fe[v] + fn[v]) - fastest * (near[v] - edge[v])) for v in ALL]


def closed_columns(table, q_ref, edges_ref, near, skip):
    band = lax.axis_index("rad")
    edge_at = edge_row(band, BAND - 1, 0)
    change = closing(table, band == 0, [q_ref[v, edge_at] for v in ALL], near)
    here = lax.broadcasted_iota(jnp.int32, (BAND, AXIAL), 0) == edge_at
    if skip is not None:
        here = here & jnp.logical_not(skip)
    return [
        [
            edges_ref[v, side, 16:32] + jnp.where(here, jnp.broadcast_to(change[v][at : at + 1], (BAND, AXIAL)), 0.0)
            for v in ALL
        ]
        for side, at in ((0, 0), (1, SECTOR - 1))
    ]


def put_message(ref, flip, edges_ref, closed, near):
    for v in ALL:
        at = 32 * v
        ref[at : at + 16] = jnp.where(flip, edges_ref[v, 1, 0:16], edges_ref[v, 0, 0:16])
        ref[at + 16 : at + 32] = jnp.where(flip, closed[1][v], closed[0][v])
        ref[160 + v : 161 + v] = jnp.where(flip, near[v][SECTOR - 1 : SECTOR], near[v][0:1])


def other_kernel(table, q_ref, edges_ref, rad_ref, other_ref):
    odd = lax.axis_index("theta") % 2 == 1
    near = [rad_ref[v] for v in ALL]
    closed = closed_columns(table, q_ref, edges_ref, near, is_late())
    put_message(other_ref, odd, edges_ref, closed, near)


def core_kernel(table, q_ref, edges_ref, first_ref, second_ref, own_ref, core_ref, rad_ref):
    odd = lax.axis_index("theta") % 2 == 1
    near = [jnp.where(is_late(), second_ref[v], first_ref[v]) for v in ALL]
    closed = closed_columns(table, q_ref, edges_ref, near, None)
    put_message(core_ref, jnp.logical_not(odd), edges_ref, closed, near)
    for v in ALL:
        rad_ref[v] = near[v]
        for side in (0, 1):
            own_ref[v, side] = closed[side][v]


def corner_kernel(other_ref, part_ref, corner_ref):
    del part_ref
    edge_at = edge_row(lax.axis_index("rad"), BAND - 1, 0)
    corner_ref[...] = jnp.zeros((8, AXIAL), F32)
    for v in ALL:
        corner_ref[v : v + 1] = other_ref[pl.ds(32 * v + edge_at, 1), :]


def masks():
    return (
        lax.broadcasted_iota(jnp.int32, (SECTOR, HALF), 1),
        lax.broadcasted_iota(jnp.int32, (SECTOR, AXIAL), 0),
    )


def row_step(coefs, q, prim, source, g_in, g_out, ends, masks, blade):
    lane, sub = masks
    a_out, a_in, inv_h, inv_r, spin_r = coefs
    f, speed = flux(q, prim, 3)
    ahead = lambda x: pltpu.roll(x, SECTOR - 1, 0)
    qn = [ahead(x) for x in q]
    fn = [qn[3]] + [ahead(f[v]) for v in range(1, 5)]
    between = face(q, (f, speed), qn, (fn, ahead(speed)))
    swirl = []
    for v in ALL:
        first, last = (0.0, 0.0) if ends is None else ends[v]
        right = jnp.where(sub == SECTOR - 1, last, between[v])
        left = jnp.where(sub == 0, first, pltpu.roll(between[v], 1, 0))
        swirl.append(inv_h * (right - left))
    radial = [a_out * g_out[v] - a_in * g_in[v] for v in ALL]
    return advance(q, prim, source, axial_difference(q, prim, lane), radial, swirl, inv_r, inv_h, spin_r, blade)


def column_rows(ref, v, j):
    return [ref[v, 2 * side + j // SECTOR, j % SECTOR : j % SECTOR + 1, :] for side in (0, 1)]


def sweep(load, step, store):
    below, q = load(-1), load(0)
    prim = primitives(q)
    g_in = face(below, flux(below, primitives(below), 2), q, flux(q, prim, 2))
    for j in range(BAND):
        above = load(j + 1)
        above_prim = primitives(above)
        g_out = face(q, flux(q, prim, 2), above, flux(above, above_prim, 2))
        store(j, step(j, q, prim, g_in, g_out))
        q, prim, g_in = above, above_prim, g_out


def next_kernel(table, blade_ref, q_ref, qp_ref, rad_ref, next_ref):
    band = lax.axis_index("rad")
    low = band == 0
    edge_at = edge_row(band, BAND - 1, 0)
    edge = [q_ref[v, edge_at] for v in ALL]
    inner = [q_ref[v, edge_row(band, BAND - 2, 1)] for v in ALL]
    near = [rad_ref[v] for v in ALL]
    prim = primitives(edge)
    f = flux(edge, prim, 2)
    below = [jnp.where(low, inner[v], near[v]) for v in ALL]
    above = [jnp.where(low, near[v], inner[v]) for v in ALL]
    g_in = face(below, flux(below, primitives(below), 2), edge, f)
    g_out = face(edge, f, above, flux(above, primitives(above), 2))
    source = [40.0 * edge[v] - 10.0 * qp_ref[v, edge_at] for v in ALL]
    coefs = [jnp.where(low, a, b) for a, b in zip(coefficients(low, table, BAND - 1), coefficients(low, table, 0))]
    stepped = row_step(coefs, edge, prim, source, g_in, g_out, None, masks(), blades(blade_ref, SECTOR))
    for v in ALL:
        next_ref[v] = stepped[v]


def early_kernel(table, blade_ref, q_ref, qp_ref, rad_ref, p1_ref, source_ref):
    low = lax.axis_index("rad") == 0
    mask = masks()
    blade = blades(blade_ref, SECTOR)

    def load(j):
        if j < 0:
            return [jnp.where(low, MIRROR[v] * q_ref[v, 0], rad_ref[v]) for v in ALL]
        if j == BAND:
            return [jnp.where(low, rad_ref[v], MIRROR[v] * q_ref[v, BAND - 1]) for v in ALL]
        return [q_ref[v, j] for v in ALL]

    def step(j, q, prim, g_in, g_out):
        source = [40.0 * q[v] - 10.0 * qp_ref[v, j] for v in ALL]
        for v in ALL:
            source_ref[v, j] = source[v]
        return row_step(coefficients(low, table, j), q, prim, source, g_in, g_out, None, mask, blade)

    def store(j, q):
        for v in ALL:
            p1_ref[v, j] = q[v]

    sweep(load, step, store)


def final_kernel(
    total_rows,
    circle,
    table,
    blade_ref,
    edges_ref,
    own_ref,
    rad_ref,
    p1_ref,
    source_ref,
    next_ref,
    other_ref,
    core_ref,
    corner_ref,
    flow_ref,
    send_ref,
    own_rows,
    nearby,
    ends,
    fields,
):
    odd = lax.axis_index("theta") % 2 == 1
    band = lax.axis_index("rad")
    low = band == 0
    mask = masks()
    blade = blades(blade_ref, SECTOR)
    for v in ALL:
        nearby[v] = next_ref[v]

    geo = Columns(band * BAND, total_rows, circle)
    column_blade = blades(blade_ref, BAND)
    near_inv_h = jnp.where(low, coefficients(low, table, BAND)[2], coefficients(low, table, -1)[2])

    for side in (0, 1):
        use_core = odd if side == 0 else jnp.logical_not(odd)
        at = 0 if side == 0 else SECTOR - 1
        sign = 1.0 if side == 0 else -1.0

        def pick(first, step, count):
            spans = [slice(first + step * v, first + step * v + count) for v in ALL]
            return [jnp.where(use_core, core_ref[span], other_ref[span]) for span in spans]

        def ordered(halo, halo_prim, own, own_prim):
            a, b = flux(halo, halo_prim, 3), flux(own, own_prim, 3)
            return face(halo, a, own, b) if side == 0 else face(own, b, halo, a)

        near, near_part, corner = pick(0, 32, 16), pick(16, 32, 16), pick(160, 1, 1)
        if side == 0:
            first = lax.axis_index("theta") % RING == 0
            corner = [jnp.where(first, corner_ref[v : v + 1], corner[v]) for v in ALL]
            edge_at = edge_row(band, BAND - 1, 0)
            cell = [jnp.where(low, near[v][BAND - 1 : BAND], near[v][0:1]) for v in ALL]
            change = closing(table, low, cell, corner)
            here = (lax.broadcasted_iota(jnp.int32, (BAND, AXIAL), 0) == edge_at) & first
            near_part = [
                near_part[v] + jnp.where(here, jnp.broadcast_to(change[v], (BAND, AXIAL)), 0.0) for v in ALL
            ]
        own = [edges_ref[v, side, 0:16] for v in ALL]
        own_prim, near_prim = primitives(own), primitives(near)
        shared = ordered(near, near_prim, own, own_prim)
        own_part = [own_ref[v, side] for v in ALL]
        own_next, near_next = [], []
        for q, prim, part, scale, out in (
            (own, own_prim, own_part, sign * geo.inv_h, own_next),
            (near, near_prim, near_part, -sign * geo.inv_h, near_next),
        ):
            force = blade_force(q, geo.spin_r, column_blade)
            change = [scale * x for x in shared]
            change[3] = change[3] - force
            change[4] = change[4] - prim[2] * force
            weight = step_weight(prim, geo.inv_h)[1]
            out.extend(part[v] + weight * change[v] for v in ALL)

        edge = [rad_ref[v, at : at + 1, :] for v in ALL]
        edge_prim = primitives(edge)
        corner_face = ordered(corner, primitives(corner), edge, edge_prim)
        corner_scale = (sign * near_inv_h) * step_weight(edge_prim, near_inv_h)[1]

        faces = ordered(near_next, primitives(near_next), own_next, primitives(own_next))
        for v in ALL:
            own_rows[v, 2 * side : 2 * side + 2] = own_next[v].reshape(2, SECTOR, AXIAL)
            nearby[v, at : at + 1, :] = next_ref[v, at : at + 1, :] + corner_scale * corner_face[v]
            ends[v, 2 * side : 2 * side + 2] = faces[v].reshape(2, SECTOR, AXIAL)

    sub = mask[1]

    def row(v, j):
        first, last = column_rows(own_rows, v, j)
        return jnp.where(sub == 0, first, jnp.where(sub == SECTOR - 1, last, p1_ref[v, j]))

    def load(j):
        if j < 0:
            return [jnp.where(low, MIRROR[v] * row(v, 0), nearby[v]) for v in ALL]
        if j == BAND:
            return [jnp.where(low, nearby[v], MIRROR[v] * row(v, BAND - 1)) for v in ALL]
        return [row(v, j) for v in ALL]

    def step(j, q, prim, g_in, g_out):
        source, end = [source_ref[v, j] for v in ALL], [column_rows(ends, v, j) for v in ALL]
        return row_step(coefficients(low, table, j), q, prim, source, g_in, g_out, end, mask, blade)

    def store(j, q):
        for v in ALL:
            flow_ref[v, j] = q[v]
        ux, _, _, pressure, _ = primitives(q)
        fields[0, j] = pressure
        fields[1, j] = ux

    sweep(load, step, store)
    for f in (0, 1):
        turned = fields[f].reshape(BAND * SECTOR, AXIAL).T
        send_ref[pl.ds(f, AXIAL, stride=2), :] = turned


def write_kernel(flow_ref, out_ref, sem):
    copy = pltpu.make_async_copy(flow_ref, out_ref, sem)
    copy.start()
    copy.wait()


def mode_kernel(got_ref, basis_ref, keep_ref, give_ref, turned):
    chips = got_ref.shape[0] // 8
    core = lax.axis_index("theta") % 2
    left = lax.broadcasted_iota(jnp.int32, (BAND, 2 * chips), 1) < chips
    parts = []
    for n in range(8):
        cells = got_ref[pl.ds(n, chips, stride=8), :]
        turned[n] = jnp.concatenate([cells, cells], axis=0).T
        rows = [turned[n, pl.ds(m, BAND, stride=SECTOR), :] for m in range(SECTOR)]
        parts.append(
            jnp.concatenate([jnp.where(left, rows[m], rows[m + 1]) for m in range(0, SECTOR, 2)], axis=1)
        )
    product = jnp.dot(
        jnp.concatenate(parts, axis=0), basis_ref[core], precision=lax.Precision.HIGHEST, preferred_element_type=F32
    )
    half = 4 * BAND
    keep_ref[...] = jnp.where(core == 0, product[:half], product[half:])
    give_ref[...] = jnp.where(core == 0, product[half:], product[:half])


def sum_kernel(keep_ref, got_ref, out_ref):
    total = keep_ref[...] + got_ref[...]
    for e in (0, 1):
        for f in (0, 1):
            n = 2 * e + f
            out_ref[e, :, 2 * MODES * f : 2 * MODES * (f + 1)] = total[BAND * n : BAND * (n + 1)]


def mode_basis(sectors):
    circle = sectors * SECTOR
    sector = 2 * np.arange(sectors // 2)[None, None, :] + np.arange(2)[:, None, None]
    cell = (np.arange(SECTOR)[None, :, None] + SECTOR * sector).reshape(2, -1)
    phase = (cell[:, :, None] * np.arange(1, MODES + 1) % circle) * (2.0 * np.pi / circle)
    return (np.concatenate([np.cos(phase), -np.sin(phase)], axis=2) / np.sqrt(circle)).astype(np.float32)


def shaped(*shape):
    return jax.ShapeDtypeStruct(shape, F32)


def vmem():
    return pl.BlockSpec(memory_space=pltpu.VMEM)


def limit(mib):
    return pltpu.CompilerParams(vmem_limit_bytes=int(mib * 2**20))


def per_device(q_level, q_prev, blade_row):
    sectors = lax.axis_size("theta")
    bands = lax.axis_size("rad")
    circle = sectors * SECTOR
    core = [(t, t ^ 1) for t in range(sectors)]
    other = [(t, (((t + 1) ^ 1) - 1) % sectors) for t in range(sectors)]
    table = geometry_table(bands * BAND, circle)
    blade = blade_row.reshape(1, AXIAL)

    hbm = pl.BlockSpec(memory_space=pltpu.HBM)
    swap = [(0, 1), (1, 0)]

    def edges(*refs):
        edge_kernel(bands * BAND, circle, *refs)

    def for_other(*refs):
        other_kernel(table, *refs)

    def for_core(*refs):
        core_kernel(table, *refs)

    def neighbour(*refs):
        next_kernel(table, *refs)

    def early(*refs):
        early_kernel(table, *refs)

    def final(*refs):
        final_kernel(bands * BAND, circle, table, *refs)

    def rad_swap(x, chosen):
        pairs = [(bands * t + b, bands * t + 1 - b) for t in range(sectors) if chosen(t % RING) for b in range(bands)]
        return lax.ppermute(x, ("theta", "rad"), pairs)

    near, q_level, q_prev = pl.pallas_call(
        load_kernel,
        out_shape=[shaped(5, SECTOR, AXIAL)] + [shaped(5, BAND, SECTOR, AXIAL)] * 2,
        in_specs=[hbm] * 2,
        out_specs=[vmem()] * 3,
        scratch_shapes=[pltpu.SemaphoreType.DMA((3,))],
        compiler_params=pltpu.CompilerParams(vmem_limit_bytes=LOAD_VMEM),
        cost_estimate=pl.CostEstimate(flops=0, bytes_accessed=3_000_000, transcendentals=0),
    )(q_level, q_prev)
    first_in = rad_swap(near, lambda place: place != RING - 1)
    second_in = rad_swap(near, lambda place: place == RING - 1)
    edge_columns = pl.pallas_call(
        edges,
        out_shape=shaped(5, 2, 32, AXIAL),
        in_specs=[vmem()] * 2,
        out_specs=vmem(),
        scratch_shapes=[pltpu.VMEM((5, 2, 32, AXIAL), F32), pltpu.VMEM((5, 2, 2, BAND, AXIAL), F32)],
        compiler_params=limit(4),
        cost_estimate=pl.CostEstimate(flops=5_000_000, bytes_accessed=2_000_000, transcendentals=50_000),
    )(q_level, q_prev)
    other_out = pl.pallas_call(
        for_other,
        out_shape=shaped(168, AXIAL),
        in_specs=[vmem()] * 3,
        out_specs=vmem(),
        compiler_params=limit(4),
    )(q_level, edge_columns, first_in)
    other_in = lax.ppermute(other_out, "theta", other)
    own_columns, core_out, rad_in = pl.pallas_call(
        for_core,
        out_shape=[shaped(5, 2, BAND, AXIAL), shaped(168, AXIAL), shaped(5, SECTOR, AXIAL)],
        in_specs=[vmem()] * 4,
        out_specs=[vmem()] * 3,
        compiler_params=limit(4),
    )(q_level, edge_columns, first_in, second_in)
    core_in = lax.ppermute(core_out, "theta", core)
    next_out = pl.pallas_call(
        neighbour,
        out_shape=shaped(5, SECTOR, AXIAL),
        in_specs=[vmem()] * 4,
        out_specs=vmem(),
        compiler_params=limit(4),
    )(blade, q_level, q_prev, rad_in)
    next_in = lax.ppermute(next_out, "rad", swap)
    part, source = pl.pallas_call(
        early,
        out_shape=[shaped(5, BAND, SECTOR, AXIAL)] * 2,
        in_specs=[vmem()] * 4,
        out_specs=[vmem()] * 2,
        compiler_params=limit(8),
        cost_estimate=pl.CostEstimate(flops=10_000_000, bytes_accessed=3_500_000, transcendentals=100_000),
    )(blade, q_level, q_prev, rad_in)
    corner = pl.pallas_call(
        corner_kernel,
        out_shape=shaped(8, AXIAL),
        in_specs=[vmem()] * 2,
        out_specs=vmem(),
        compiler_params=limit(4),
    )(other_in, part)
    corner_in = rad_swap(corner, lambda place: place == 0)
    flow_state, send = pl.pallas_call(
        final,
        out_shape=[shaped(5, BAND, SECTOR, AXIAL), shaped(2 * AXIAL, BAND * SECTOR)],
        in_specs=[vmem()] * 10,
        out_specs=[vmem()] * 2,
        scratch_shapes=[
            pltpu.VMEM((5, 4, SECTOR, AXIAL), F32),
            pltpu.VMEM((5, SECTOR, AXIAL), F32),
            pltpu.VMEM((5, 4, SECTOR, AXIAL), F32),
            pltpu.VMEM((2, BAND, SECTOR, AXIAL), F32),
        ],
        compiler_params=limit(8),
    )(blade, edge_columns, own_columns, rad_in, part, source, next_in, other_in, core_in, corner_in)
    chips = sectors // 2
    got = lax.all_to_all(
        send.reshape(chips, 8, 128),
        "theta",
        split_axis=0,
        concat_axis=0,
        tiled=True,
        axis_index_groups=[[2 * chip + c for chip in range(chips)] for c in (0, 1)],
    )
    keep, give = pl.pallas_call(
        mode_kernel,
        out_shape=[shaped(4 * BAND, 2 * MODES)] * 2,
        in_specs=[vmem()] * 2,
        out_specs=[vmem()] * 2,
        scratch_shapes=[pltpu.VMEM((8, BAND * SECTOR, 2 * chips), F32)],
        compiler_params=limit(4),
    )(got.reshape(8 * chips, 128), jnp.asarray(mode_basis(sectors)))
    given = lax.ppermute(give, "theta", core)
    flow_state = pl.pallas_call(
        write_kernel,
        out_shape=shaped(5, BAND, SECTOR, AXIAL),
        in_specs=[vmem()],
        out_specs=hbm,
        scratch_shapes=[pltpu.SemaphoreType.DMA],
        compiler_params=limit(2),
        cost_estimate=pl.CostEstimate(flops=0, bytes_accessed=1_400_000, transcendentals=0),
    )(flow_state)
    spectra = pl.pallas_call(
        sum_kernel,
        out_shape=shaped(2, BAND, 4 * MODES),
        in_specs=[vmem()] * 2,
        out_specs=vmem(),
        compiler_params=limit(2),
    )(keep, given)
    return flow_state, spectra


def solution(mesh):
    in_specs = (P(None, "rad", "theta", None), P(None, "rad", "theta", None), P())
    out_specs = (P(None, "rad", "theta", None), P("theta", "rad", None))
    return jax.shard_map(per_device, mesh=mesh, in_specs=in_specs, out_specs=out_specs, check_vma=False)
```

```python
import math

import jax
import jax.numpy as jnp
import numpy as np
from jax import lax
from jax.experimental import pallas as pl
from jax.experimental.pallas import tpu as pltpu
from jax.sharding import PartitionSpec as P

MODES = 64
GAMMA = 1.4
KAPPA = 2.0

BAND = 16
SECTOR = 8
AXIAL = 256
RAD_VMEM = 56_200_000
LOAD_VMEM = 55_000_000
F32 = jnp.float32
ALL = range(5)


def primitives(q):
    inverse = 1.0 / q[0]
    ux, ur, ut = q[1] * inverse, q[2] * inverse, q[3] * inverse
    pressure = (GAMMA - 1.0) * (q[4] - 0.5 * (q[1] * ux + q[2] * ur + q[3] * ut))
    sound = jnp.sqrt(GAMMA * pressure * inverse)
    return ux, ur, ut, pressure, sound


def flux(q, prim, d):
    u, pressure = prim[d - 1], prim[3]
    f = [q[d], q[1] * u, q[2] * u, q[3] * u, (q[4] + pressure) * u]
    f[d] = f[d] + pressure
    return f, jnp.abs(u) + prim[4]


def face(left_q, left_flux, right_q, right_flux):
    (fl, sl), (fr, sr) = left_flux, right_flux
    fastest = jnp.maximum(sl, sr)
    return [(fl[v] + fr[v]) - fastest * (right_q[v] - left_q[v]) for v in ALL]


HALF = AXIAL // 2


def axial_neighbour(x, lane, step, end):
    low, high = x[:, :HALF], x[:, HALF:]
    turned_low, turned_high = pltpu.roll(low, -step % HALF, 1), pltpu.roll(high, -step % HALF, 1)
    if step == 1:
        seam = lane == HALF - 1
        parts = [jnp.where(seam, turned_high, turned_low), jnp.where(seam, end, turned_high)]
    else:
        seam = lane == 0
        parts = [jnp.where(seam, end, turned_low), jnp.where(seam, turned_low, turned_high)]
    return jnp.concatenate(parts, axis=1)


def axial_difference(q, prim, lane):
    f, speed = flux(q, prim, 1)

    def following(x):
        return axial_neighbour(x, lane, 1, x[:, HALF:])

    qn = [following(x) for x in q]
    fn = [qn[1]] + [following(f[v]) for v in range(1, 5)]
    right = face(q, (f, speed), qn, (fn, following(speed)))
    return [x - axial_neighbour(x, lane, -1, 2.0 * f[v][:, :HALF]) for v, x in enumerate(right)]


def step_weight(prim, inv_h):
    ux, ur, ut, _, sound = prim
    rate = 4.0 * (jnp.abs(ux) + jnp.abs(ur)) + jnp.abs(ut) * (4.0 * inv_h) + sound * (8.0 + 4.0 * inv_h)
    return rate, 1.0 / (rate + 30.0)


def blade_force(q, spin_r, blade):
    bladed, rotor = blade
    return bladed * (q[3] - (rotor * spin_r) * q[0])


def advance(q, prim, source, axial, radial, swirl, inv_r, inv_h, spin_r, blade):
    ux, ur, ut, pressure, sound = prim
    twice_r = 2.0 * inv_r
    rate, weight = step_weight(prim, inv_h)
    gains = [None, None, twice_r * (q[3] * ut + pressure), -twice_r * (q[2] * ut), None]
    if blade is not None:
        force = blade_force(q, spin_r, blade)
        gains[3] = gains[3] - force
        gains[4] = -ut * force
    out = []
    for v in ALL:
        total = source[v] - axial[v] - radial[v] - swirl[v]
        if gains[v] is not None:
            total = total + gains[v]
        out.append((rate * q[v] + total) * weight)
    return out


def geometry_table(rows, circle):
    mean = circle / (2.0 * math.pi)
    row = np.arange(rows, dtype=np.float64)
    radius = mean * (0.8 + 0.4 * (row + 0.5) / rows)
    inner = mean * (0.8 + 0.4 * row / rows)
    outer = mean * (0.8 + 0.4 * (row + 1.0) / rows)
    spacing = radius * (2.0 * math.pi / circle)
    return np.stack([outer / radius, inner / radius, 1.0 / spacing, 1.0 / radius, radius / (1.2 * mean)])


def coefficients(low, table, j):
    last = table.shape[1] - 1
    at = [min(max(j + first, 0), last) for first in (0, BAND)]
    return [jnp.where(low, np.float32(row[at[0]]), np.float32(row[at[1]])) for row in table]


def edge_row(band, at_low, at_high):
    return jnp.where(band == 0, at_low, at_high)


MIRROR = (1.0, 1.0, -1.0, 1.0, 1.0)


def blades(blade_ref, rows):
    blade = blade_ref[...]
    bladed = jnp.broadcast_to(4.0 * (blade > 0).astype(F32), (rows, AXIAL))
    rotor = jnp.broadcast_to((blade == 1).astype(F32), (rows, AXIAL))
    return bladed, rotor


def rad_kernel(q_ref, near_ref, sem):
    copy = pltpu.make_async_copy(q_ref.at[:, edge_row(lax.axis_index("rad"), BAND - 1, 0)], near_ref, sem)
    copy.start()
    copy.wait()


def load_kernel(q_ref, qp_ref, q_out_ref, qp_out_ref, sems):
    copies = [
        pltpu.make_async_copy(q_ref, q_out_ref, sems.at[0]),
        pltpu.make_async_copy(qp_ref, qp_out_ref, sems.at[1]),
    ]
    for copy in copies:
        copy.start()
    for copy in copies:
        copy.wait()


class Columns:
    def __init__(self, first_row, total_rows, circle):
        rows = (lax.broadcasted_iota(jnp.int32, (BAND, AXIAL), 0) + first_row).astype(F32)
        mean = circle / (2.0 * math.pi)
        radius = mean * (0.8 + 0.4 * (rows + 0.5) / total_rows)
        self.inner = mean * (0.8 + 0.4 * rows / total_rows)
        self.outer = mean * (0.8 + 0.4 * (rows + 1.0) / total_rows)
        self.inv_r = 1.0 / radius
        self.inv_h = self.inv_r * mean
        self.spin_r = radius * (1.0 / (1.2 * mean))
        self.a_h = 0.25 * self.inv_h


def edge_kernel(total_rows, circle, q_ref, qp_ref, edges_ref, ce, taken):
    band = lax.axis_index("rad")
    low = band == 0
    geo = Columns(band * BAND, total_rows, circle)
    lane = lax.broadcasted_iota(jnp.int32, (BAND, HALF), 1)
    row = lax.broadcasted_iota(jnp.int32, (BAND, AXIAL), 0)
    below_scale = jnp.where((row == 0) & jnp.logical_not(low), 0.0, geo.inv_r * geo.inner)
    above_scale = jnp.where((row == BAND - 1) & low, 0.0, geo.inv_r * geo.outer)
    for side in (0, 1):
        at, inner = (0, 1) if side == 0 else (SECTOR - 1, SECTOR - 2)
        for v in ALL:
            ce[v, side, 8:24] = q_ref[v, :, at, :]
            taken[v, side, 0] = q_ref[v, :, inner, :]
            taken[v, side, 1] = qp_ref[v, :, at, :]
    for side in (0, 1):
        edge = [ce[v, side, 8:24] for v in ALL]
        second = [taken[v, side, 0] for v in ALL]
        source = [40.0 * edge[v] - 10.0 * taken[v, side, 1] for v in ALL]
        for v in ALL:
            ce[v, side, 7:8] = MIRROR[v] * edge[v][0:1]
            ce[v, side, 24:25] = MIRROR[v] * edge[v][BAND - 1 : BAND]
        below = [ce[v, side, 7:23] for v in ALL]
        above = [ce[v, side, 9:25] for v in ALL]
        prim = primitives(edge)
        f = flux(edge, prim, 2)
        g_in = face(below, flux(below, primitives(below), 2), edge, f)
        g_out = face(edge, f, above, flux(above, primitives(above), 2))
        f = flux(edge, prim, 3)
        second_flux = flux(second, primitives(second), 3)
        if side == 0:
            swirl = [geo.inv_h * x for x in face(edge, f, second, second_flux)]
        else:
            swirl = [-geo.inv_h * x for x in face(second, second_flux, edge, f)]
        part = advance(
            edge,
            prim,
            source,
            axial_difference(edge, prim, lane),
            [above_scale * g_out[v] - below_scale * g_in[v] for v in ALL],
            swirl,
            geo.inv_r,
            geo.inv_h,
            geo.spin_r,
            None,
        )
        for v in ALL:
            edges_ref[v, side, 0:16] = edge[v]
            edges_ref[v, side, 16:32] = part[v]


def pack_kernel(table, q_ref, edges_ref, rad_ref, own_ref, core_ref, other_ref):
    odd = lax.axis_index("theta") % 2 == 1
    band = lax.axis_index("rad")
    low = band == 0
    edge_at = edge_row(band, BAND - 1, 0)
    below_coefs, above_coefs = coefficients(low, table, 0), coefficients(low, table, BAND - 1)
    edge = [q_ref[v, edge_at] for v in ALL]
    near = [rad_ref[v] for v in ALL]
    edge_prim, near_prim = primitives(edge), primitives(near)
    (fe, se), (fn, sn) = flux(edge, edge_prim, 2), flux(near, near_prim, 2)
    fastest = jnp.where(low, np.float32(1.0), np.float32(-1.0)) * jnp.maximum(se, sn)
    _, weight = step_weight(edge_prim, jnp.where(low, above_coefs[2], below_coefs[2]))
    scale = jnp.where(low, -above_coefs[0], below_coefs[1]) * weight
    change = [scale * ((fe[v] + fn[v]) - fastest * (near[v] - edge[v])) for v in ALL]
    here = lax.broadcasted_iota(jnp.int32, (BAND, AXIAL), 0) == edge_at
    for v in ALL:
        for side in (0, 1):
            at = 0 if side == 0 else SECTOR - 1
            own_ref[v, side] = edges_ref[v, side, 16:32] + jnp.where(here, change[v][at : at + 1], 0.0)
        for ref, flip in ((core_ref, jnp.logical_not(odd)), (other_ref, odd)):
            at = 32 * v
            ref[at : at + 16] = jnp.where(flip, edges_ref[v, 1, 0:16], edges_ref[v, 0, 0:16])
            ref[at + 16 : at + 32] = jnp.where(flip, own_ref[v, 1], own_ref[v, 0])
            ref[160 + v : 161 + v] = jnp.where(flip, near[v][SECTOR - 1 : SECTOR], near[v][0:1])


def masks():
    return (
        lax.broadcasted_iota(jnp.int32, (SECTOR, HALF), 1),
        lax.broadcasted_iota(jnp.int32, (SECTOR, AXIAL), 0),
    )


def row_step(coefs, q, prim, source, g_in, g_out, ends, masks, blade):
    lane, sub = masks
    a_out, a_in, inv_h, inv_r, spin_r = coefs
    f, speed = flux(q, prim, 3)
    ahead = lambda x: pltpu.roll(x, SECTOR - 1, 0)
    qn = [ahead(x) for x in q]
    fn = [qn[3]] + [ahead(f[v]) for v in range(1, 5)]
    between = face(q, (f, speed), qn, (fn, ahead(speed)))
    swirl = []
    for v in ALL:
        first, last = (0.0, 0.0) if ends is None else ends[v]
        right = jnp.where(sub == SECTOR - 1, last, between[v])
        left = jnp.where(sub == 0, first, pltpu.roll(between[v], 1, 0))
        swirl.append(inv_h * (right - left))
    radial = [a_out * g_out[v] - a_in * g_in[v] for v in ALL]
    return advance(q, prim, source, axial_difference(q, prim, lane), radial, swirl, inv_r, inv_h, spin_r, blade)


def column_rows(ref, v, j):
    return [ref[v, 2 * side + j // SECTOR, j % SECTOR : j % SECTOR + 1, :] for side in (0, 1)]


def sweep(load, step, store):
    below, q = load(-1), load(0)
    prim = primitives(q)
    g_in = face(below, flux(below, primitives(below), 2), q, flux(q, prim, 2))
    for j in range(BAND):
        above = load(j + 1)
        above_prim = primitives(above)
        g_out = face(q, flux(q, prim, 2), above, flux(above, above_prim, 2))
        store(j, step(j, q, prim, g_in, g_out))
        q, prim, g_in = above, above_prim, g_out


def next_kernel(table, blade_ref, q_ref, qp_ref, rad_ref, next_ref):
    band = lax.axis_index("rad")
    low = band == 0
    edge_at = edge_row(band, BAND - 1, 0)
    edge = [q_ref[v, edge_at] for v in ALL]
    inner = [q_ref[v, edge_row(band, BAND - 2, 1)] for v in ALL]
    near = [rad_ref[v] for v in ALL]
    prim = primitives(edge)
    f = flux(edge, prim, 2)
    below = [jnp.where(low, inner[v], near[v]) for v in ALL]
    above = [jnp.where(low, near[v], inner[v]) for v in ALL]
    g_in = face(below, flux(below, primitives(below), 2), edge, f)
    g_out = face(edge, f, above, flux(above, primitives(above), 2))
    source = [40.0 * edge[v] - 10.0 * qp_ref[v, edge_at] for v in ALL]
    coefs = [jnp.where(low, a, b) for a, b in zip(coefficients(low, table, BAND - 1), coefficients(low, table, 0))]
    stepped = row_step(coefs, edge, prim, source, g_in, g_out, None, masks(), blades(blade_ref, SECTOR))
    for v in ALL:
        next_ref[v] = stepped[v]


def early_kernel(table, blade_ref, q_ref, qp_ref, rad_ref, p1_ref, source_ref):
    low = lax.axis_index("rad") == 0
    mask = masks()
    blade = blades(blade_ref, SECTOR)

    def load(j):
        if j < 0:
            return [jnp.where(low, MIRROR[v] * q_ref[v, 0], rad_ref[v]) for v in ALL]
        if j == BAND:
            return [jnp.where(low, rad_ref[v], MIRROR[v] * q_ref[v, BAND - 1]) for v in ALL]
        return [q_ref[v, j] for v in ALL]

    def step(j, q, prim, g_in, g_out):
        source = [40.0 * q[v] - 10.0 * qp_ref[v, j] for v in ALL]
        for v in ALL:
            source_ref[v, j] = source[v]
        return row_step(coefficients(low, table, j), q, prim, source, g_in, g_out, None, mask, blade)

    def store(j, q):
        for v in ALL:
            p1_ref[v, j] = q[v]

    sweep(load, step, store)


def final_kernel(
    total_rows,
    circle,
    table,
    blade_ref,
    edges_ref,
    own_ref,
    rad_ref,
    p1_ref,
    source_ref,
    next_ref,
    other_ref,
    core_ref,
    flow_ref,
    send_ref,
    own_rows,
    nearby,
    ends,
    fields,
):
    odd = lax.axis_index("theta") % 2 == 1
    band = lax.axis_index("rad")
    low = band == 0
    mask = masks()
    blade = blades(blade_ref, SECTOR)
    for v in ALL:
        nearby[v] = next_ref[v]

    geo = Columns(band * BAND, total_rows, circle)
    column_blade = blades(blade_ref, BAND)
    near_inv_h = jnp.where(low, coefficients(low, table, BAND)[2], coefficients(low, table, -1)[2])

    for side in (0, 1):
        use_core = odd if side == 0 else jnp.logical_not(odd)
        at = 0 if side == 0 else SECTOR - 1
        sign = 1.0 if side == 0 else -1.0

        def pick(first, step, count):
            spans = [slice(first + step * v, first + step * v + count) for v in ALL]
            return [jnp.where(use_core, core_ref[span], other_ref[span]) for span in spans]

        def ordered(halo, halo_prim, own, own_prim):
            a, b = flux(halo, halo_prim, 3), flux(own, own_prim, 3)
            return face(halo, a, own, b) if side == 0 else face(own, b, halo, a)

        near, near_part, corner = pick(0, 32, 16), pick(16, 32, 16), pick(160, 1, 1)
        own = [edges_ref[v, side, 0:16] for v in ALL]
        own_prim, near_prim = primitives(own), primitives(near)
        shared = ordered(near, near_prim, own, own_prim)
        own_part = [own_ref[v, side] for v in ALL]
        own_next, near_next = [], []
        for q, prim, part, scale, out in (
            (own, own_prim, own_part, sign * geo.inv_h, own_next),
            (near, near_prim, near_part, -sign * geo.inv_h, near_next),
        ):
            force = blade_force(q, geo.spin_r, column_blade)
            change = [scale * x for x in shared]
            change[3] = change[3] - force
            change[4] = change[4] - prim[2] * force
            weight = step_weight(prim, geo.inv_h)[1]
            out.extend(part[v] + weight * change[v] for v in ALL)

        edge = [rad_ref[v, at : at + 1, :] for v in ALL]
        edge_prim = primitives(edge)
        corner_face = ordered(corner, primitives(corner), edge, edge_prim)
        corner_scale = (sign * near_inv_h) * step_weight(edge_prim, near_inv_h)[1]

        faces = ordered(near_next, primitives(near_next), own_next, primitives(own_next))
        for v in ALL:
            own_rows[v, 2 * side : 2 * side + 2] = own_next[v].reshape(2, SECTOR, AXIAL)
            nearby[v, at : at + 1, :] = next_ref[v, at : at + 1, :] + corner_scale * corner_face[v]
            ends[v, 2 * side : 2 * side + 2] = faces[v].reshape(2, SECTOR, AXIAL)

    sub = mask[1]

    def row(v, j):
        first, last = column_rows(own_rows, v, j)
        return jnp.where(sub == 0, first, jnp.where(sub == SECTOR - 1, last, p1_ref[v, j]))

    def load(j):
        if j < 0:
            return [jnp.where(low, MIRROR[v] * row(v, 0), nearby[v]) for v in ALL]
        if j == BAND:
            return [jnp.where(low, nearby[v], MIRROR[v] * row(v, BAND - 1)) for v in ALL]
        return [row(v, j) for v in ALL]

    def step(j, q, prim, g_in, g_out):
        source, end = [source_ref[v, j] for v in ALL], [column_rows(ends, v, j) for v in ALL]
        return row_step(coefficients(low, table, j), q, prim, source, g_in, g_out, end, mask, blade)

    def store(j, q):
        for v in ALL:
            flow_ref[v, j] = q[v]
        ux, _, _, pressure, _ = primitives(q)
        fields[0, j] = pressure
        fields[1, j] = ux

    sweep(load, step, store)
    for f in (0, 1):
        turned = fields[f].reshape(BAND * SECTOR, AXIAL).T
        send_ref[pl.ds(f, AXIAL, stride=2), :] = turned


def write_kernel(flow_ref, out_ref, sem):
    copy = pltpu.make_async_copy(flow_ref, out_ref, sem)
    copy.start()
    copy.wait()


def mode_kernel(got_ref, basis_ref, keep_ref, give_ref, turned):
    chips = got_ref.shape[0] // 8
    core = lax.axis_index("theta") % 2
    left = lax.broadcasted_iota(jnp.int32, (BAND, 2 * chips), 1) < chips
    parts = []
    for n in range(8):
        cells = got_ref[pl.ds(n, chips, stride=8), :]
        turned[n] = jnp.concatenate([cells, cells], axis=0).T
        rows = [turned[n, pl.ds(m, BAND, stride=SECTOR), :] for m in range(SECTOR)]
        parts.append(
            jnp.concatenate([jnp.where(left, rows[m], rows[m + 1]) for m in range(0, SECTOR, 2)], axis=1)
        )
    product = jnp.dot(
        jnp.concatenate(parts, axis=0), basis_ref[core], precision=lax.Precision.HIGHEST, preferred_element_type=F32
    )
    half = 4 * BAND
    keep_ref[...] = jnp.where(core == 0, product[:half], product[half:])
    give_ref[...] = jnp.where(core == 0, product[half:], product[:half])


def sum_kernel(keep_ref, got_ref, out_ref):
    total = keep_ref[...] + got_ref[...]
    for e in (0, 1):
        for f in (0, 1):
            n = 2 * e + f
            out_ref[e, :, 2 * MODES * f : 2 * MODES * (f + 1)] = total[BAND * n : BAND * (n + 1)]


def mode_basis(sectors):
    circle = sectors * SECTOR
    sector = 2 * np.arange(sectors // 2)[None, None, :] + np.arange(2)[:, None, None]
    cell = (np.arange(SECTOR)[None, :, None] + SECTOR * sector).reshape(2, -1)
    phase = (cell[:, :, None] * np.arange(1, MODES + 1) % circle) * (2.0 * np.pi / circle)
    return (np.concatenate([np.cos(phase), -np.sin(phase)], axis=2) / np.sqrt(circle)).astype(np.float32)


def shaped(*shape):
    return jax.ShapeDtypeStruct(shape, F32)


def vmem():
    return pl.BlockSpec(memory_space=pltpu.VMEM)


def limit(mib):
    return pltpu.CompilerParams(vmem_limit_bytes=int(mib * 2**20))


def per_device(q_level, q_prev, blade_row):
    sectors = lax.axis_size("theta")
    bands = lax.axis_size("rad")
    circle = sectors * SECTOR
    core = [(t, t ^ 1) for t in range(sectors)]
    other = [(t, (((t + 1) ^ 1) - 1) % sectors) for t in range(sectors)]
    table = geometry_table(bands * BAND, circle)
    blade = blade_row.reshape(1, AXIAL)

    hbm = pl.BlockSpec(memory_space=pltpu.HBM)
    swap = [(0, 1), (1, 0)]

    def edges(*refs):
        edge_kernel(bands * BAND, circle, *refs)

    def pack(*refs):
        pack_kernel(table, *refs)

    def neighbour(*refs):
        next_kernel(table, *refs)

    def early(*refs):
        early_kernel(table, *refs)

    def final(*refs):
        final_kernel(bands * BAND, circle, table, *refs)

    near = pl.pallas_call(
        rad_kernel,
        out_shape=shaped(5, SECTOR, AXIAL),
        in_specs=[hbm],
        out_specs=vmem(),
        scratch_shapes=[pltpu.SemaphoreType.DMA],
        compiler_params=pltpu.CompilerParams(vmem_limit_bytes=RAD_VMEM),
    )(q_level)
    rad_in = lax.ppermute(near, "rad", swap)
    q_level, q_prev = pl.pallas_call(
        load_kernel,
        out_shape=[shaped(5, BAND, SECTOR, AXIAL)] * 2,
        in_specs=[hbm] * 2,
        out_specs=[vmem()] * 2,
        scratch_shapes=[pltpu.SemaphoreType.DMA((2,))],
        compiler_params=pltpu.CompilerParams(vmem_limit_bytes=LOAD_VMEM),
        cost_estimate=pl.CostEstimate(flops=0, bytes_accessed=3_000_000, transcendentals=0),
    )(q_level, q_prev)
    edge_columns = pl.pallas_call(
        edges,
        out_shape=shaped(5, 2, 32, AXIAL),
        in_specs=[vmem()] * 2,
        out_specs=vmem(),
        scratch_shapes=[pltpu.VMEM((5, 2, 32, AXIAL), F32), pltpu.VMEM((5, 2, 2, BAND, AXIAL), F32)],
        compiler_params=limit(4),
        cost_estimate=pl.CostEstimate(flops=5_000_000, bytes_accessed=2_000_000, transcendentals=50_000),
    )(q_level, q_prev)
    own_columns, core_out, other_out = pl.pallas_call(
        pack,
        out_shape=[shaped(5, 2, BAND, AXIAL)] + [shaped(168, AXIAL)] * 2,
        in_specs=[vmem()] * 3,
        out_specs=[vmem()] * 3,
        compiler_params=limit(4),
    )(q_level, edge_columns, rad_in)
    core_in = lax.ppermute(core_out, "theta", core)
    other_in = lax.ppermute(other_out, "theta", other)
    next_out = pl.pallas_call(
        neighbour,
        out_shape=shaped(5, SECTOR, AXIAL),
        in_specs=[vmem()] * 4,
        out_specs=vmem(),
        compiler_params=limit(4),
    )(blade, q_level, q_prev, rad_in)
    next_in = lax.ppermute(next_out, "rad", swap)
    part, source = pl.pallas_call(
        early,
        out_shape=[shaped(5, BAND, SECTOR, AXIAL)] * 2,
        in_specs=[vmem()] * 4,
        out_specs=[vmem()] * 2,
        compiler_params=limit(8),
        cost_estimate=pl.CostEstimate(flops=10_000_000, bytes_accessed=3_500_000, transcendentals=100_000),
    )(blade, q_level, q_prev, rad_in)
    flow_state, send = pl.pallas_call(
        final,
        out_shape=[shaped(5, BAND, SECTOR, AXIAL), shaped(2 * AXIAL, BAND * SECTOR)],
        in_specs=[vmem()] * 9,
        out_specs=[vmem()] * 2,
        scratch_shapes=[
            pltpu.VMEM((5, 4, SECTOR, AXIAL), F32),
            pltpu.VMEM((5, SECTOR, AXIAL), F32),
            pltpu.VMEM((5, 4, SECTOR, AXIAL), F32),
            pltpu.VMEM((2, BAND, SECTOR, AXIAL), F32),
        ],
        compiler_params=limit(8),
    )(blade, edge_columns, own_columns, rad_in, part, source, next_in, other_in, core_in)
    chips = sectors // 2
    got = lax.all_to_all(
        send.reshape(chips, 8, 128),
        "theta",
        split_axis=0,
        concat_axis=0,
        tiled=True,
        axis_index_groups=[[2 * chip + c for chip in range(chips)] for c in (0, 1)],
    )
    keep, give = pl.pallas_call(
        mode_kernel,
        out_shape=[shaped(4 * BAND, 2 * MODES)] * 2,
        in_specs=[vmem()] * 2,
        out_specs=[vmem()] * 2,
        scratch_shapes=[pltpu.VMEM((8, BAND * SECTOR, 2 * chips), F32)],
        compiler_params=limit(4),
    )(got.reshape(8 * chips, 128), jnp.asarray(mode_basis(sectors)))
    given = lax.ppermute(give, "theta", core)
    flow_state = pl.pallas_call(
        write_kernel,
        out_shape=shaped(5, BAND, SECTOR, AXIAL),
        in_specs=[vmem()],
        out_specs=hbm,
        scratch_shapes=[pltpu.SemaphoreType.DMA],
        compiler_params=limit(2),
        cost_estimate=pl.CostEstimate(flops=0, bytes_accessed=1_400_000, transcendentals=0),
    )(flow_state)
    spectra = pl.pallas_call(
        sum_kernel,
        out_shape=shaped(2, BAND, 4 * MODES),
        in_specs=[vmem()] * 2,
        out_specs=vmem(),
        compiler_params=limit(2),
    )(keep, given)
    return flow_state, spectra


def solution(mesh):
    in_specs = (P(None, "rad", "theta", None), P(None, "rad", "theta", None), P())
    out_specs = (P(None, "rad", "theta", None), P("theta", "rad", None))
    return jax.shard_map(per_device, mesh=mesh, in_specs=in_specs, out_specs=out_specs, check_vma=False)
```

```python
import math

import jax
import jax.numpy as jnp
import numpy as np
from jax import lax
from jax.experimental import pallas as pl
from jax.experimental.pallas import tpu as pltpu
from jax.sharding import PartitionSpec as P

MODES = 64
GAMMA = 1.4
KAPPA = 2.0

BAND = 16
HALF_BAND = BAND // 2
SECTOR = 8
AXIAL = 256
RAD_VMEM = 56_200_000
LOAD_VMEM = 55_000_000
F32 = jnp.float32
ALL = range(5)


def primitives(q):
    inverse = 1.0 / q[0]
    ux, ur, ut = q[1] * inverse, q[2] * inverse, q[3] * inverse
    pressure = (GAMMA - 1.0) * (q[4] - 0.5 * (q[1] * ux + q[2] * ur + q[3] * ut))
    sound = jnp.sqrt(GAMMA * pressure * inverse)
    return ux, ur, ut, pressure, sound


def flux(q, prim, d):
    u, pressure = prim[d - 1], prim[3]
    f = [q[d], q[1] * u, q[2] * u, q[3] * u, (q[4] + pressure) * u]
    f[d] = f[d] + pressure
    return f, jnp.abs(u) + prim[4]


def face(left_q, left_flux, right_q, right_flux):
    (fl, sl), (fr, sr) = left_flux, right_flux
    fastest = jnp.maximum(sl, sr)
    return [(fl[v] + fr[v]) - fastest * (right_q[v] - left_q[v]) for v in ALL]


HALF = AXIAL // 2


def axial_neighbour(x, lane, step, end):
    low, high = x[:, :HALF], x[:, HALF:]
    turned_low, turned_high = pltpu.roll(low, -step % HALF, 1), pltpu.roll(high, -step % HALF, 1)
    if step == 1:
        seam = lane == HALF - 1
        parts = [jnp.where(seam, turned_high, turned_low), jnp.where(seam, end, turned_high)]
    else:
        seam = lane == 0
        parts = [jnp.where(seam, end, turned_low), jnp.where(seam, turned_low, turned_high)]
    return jnp.concatenate(parts, axis=1)


def axial_difference(q, prim, lane):
    f, speed = flux(q, prim, 1)

    def following(x):
        return axial_neighbour(x, lane, 1, x[:, HALF:])

    qn = [following(x) for x in q]
    fn = [qn[1]] + [following(f[v]) for v in range(1, 5)]
    right = face(q, (f, speed), qn, (fn, following(speed)))
    return [x - axial_neighbour(x, lane, -1, 2.0 * f[v][:, :HALF]) for v, x in enumerate(right)]


def step_weight(prim, inv_h):
    ux, ur, ut, _, sound = prim
    rate = 4.0 * (jnp.abs(ux) + jnp.abs(ur)) + jnp.abs(ut) * (4.0 * inv_h) + sound * (8.0 + 4.0 * inv_h)
    return rate, 1.0 / (rate + 30.0)


def blade_force(q, spin_r, blade):
    bladed, rotor = blade
    return bladed * (q[3] - (rotor * spin_r) * q[0])


def advance(q, prim, source, axial, radial, swirl, inv_r, inv_h, spin_r, blade):
    ux, ur, ut, pressure, sound = prim
    twice_r = 2.0 * inv_r
    rate, weight = step_weight(prim, inv_h)
    gains = [None, None, twice_r * (q[3] * ut + pressure), -twice_r * (q[2] * ut), None]
    if blade is not None:
        force = blade_force(q, spin_r, blade)
        gains[3] = gains[3] - force
        gains[4] = -ut * force
    out = []
    for v in ALL:
        total = source[v] - axial[v] - radial[v] - swirl[v]
        if gains[v] is not None:
            total = total + gains[v]
        out.append((rate * q[v] + total) * weight)
    return out


def geometry_table(rows, circle):
    mean = circle / (2.0 * math.pi)
    row = np.arange(rows, dtype=np.float64)
    radius = mean * (0.8 + 0.4 * (row + 0.5) / rows)
    inner = mean * (0.8 + 0.4 * row / rows)
    outer = mean * (0.8 + 0.4 * (row + 1.0) / rows)
    spacing = radius * (2.0 * math.pi / circle)
    return np.stack([outer / radius, inner / radius, 1.0 / spacing, 1.0 / radius, radius / (1.2 * mean)])


def coefficients(low, table, j):
    last = table.shape[1] - 1
    at = [min(max(j + first, 0), last) for first in (0, BAND)]
    return [jnp.where(low, np.float32(row[at[0]]), np.float32(row[at[1]])) for row in table]


def edge_row(band, at_low, at_high):
    return jnp.where(band == 0, at_low, at_high)


MIRROR = (1.0, 1.0, -1.0, 1.0, 1.0)


def blades(blade_ref, rows):
    blade = blade_ref[...]
    bladed = jnp.broadcast_to(4.0 * (blade > 0).astype(F32), (rows, AXIAL))
    rotor = jnp.broadcast_to((blade == 1).astype(F32), (rows, AXIAL))
    return bladed, rotor


def rad_kernel(q_ref, near_ref, sem):
    copy = pltpu.make_async_copy(q_ref.at[:, edge_row(lax.axis_index("rad"), BAND - 1, 0)], near_ref, sem)
    copy.start()
    copy.wait()


def load_kernel(q_ref, qp_ref, q_out_ref, qp_out_ref, sems):
    copies = [
        pltpu.make_async_copy(q_ref, q_out_ref, sems.at[0]),
        pltpu.make_async_copy(qp_ref, qp_out_ref, sems.at[1]),
    ]
    for copy in copies:
        copy.start()
    for copy in copies:
        copy.wait()


class Columns:
    def __init__(self, first_row, total_rows, circle):
        rows = (lax.broadcasted_iota(jnp.int32, (BAND, AXIAL), 0) + first_row).astype(F32)
        mean = circle / (2.0 * math.pi)
        radius = mean * (0.8 + 0.4 * (rows + 0.5) / total_rows)
        self.inner = mean * (0.8 + 0.4 * rows / total_rows)
        self.outer = mean * (0.8 + 0.4 * (rows + 1.0) / total_rows)
        self.inv_r = 1.0 / radius
        self.inv_h = self.inv_r * mean
        self.spin_r = radius * (1.0 / (1.2 * mean))
        self.a_h = 0.25 * self.inv_h


def edge_kernel(total_rows, circle, q_ref, qp_ref, edges_ref, ce, taken):
    band = lax.axis_index("rad")
    low = band == 0
    geo = Columns(band * BAND, total_rows, circle)
    lane = lax.broadcasted_iota(jnp.int32, (BAND, HALF), 1)
    row = lax.broadcasted_iota(jnp.int32, (BAND, AXIAL), 0)
    below_scale = jnp.where((row == 0) & jnp.logical_not(low), 0.0, geo.inv_r * geo.inner)
    above_scale = jnp.where((row == BAND - 1) & low, 0.0, geo.inv_r * geo.outer)
    for side in (0, 1):
        at, inner = (0, 1) if side == 0 else (SECTOR - 1, SECTOR - 2)
        for v in ALL:
            ce[v, side, 8:24] = q_ref[v, :, at, :]
            taken[v, side, 0] = q_ref[v, :, inner, :]
            taken[v, side, 1] = qp_ref[v, :, at, :]
    for side in (0, 1):
        edge = [ce[v, side, 8:24] for v in ALL]
        second = [taken[v, side, 0] for v in ALL]
        source = [40.0 * edge[v] - 10.0 * taken[v, side, 1] for v in ALL]
        for v in ALL:
            ce[v, side, 7:8] = MIRROR[v] * edge[v][0:1]
            ce[v, side, 24:25] = MIRROR[v] * edge[v][BAND - 1 : BAND]
        below = [ce[v, side, 7:23] for v in ALL]
        above = [ce[v, side, 9:25] for v in ALL]
        prim = primitives(edge)
        f = flux(edge, prim, 2)
        g_in = face(below, flux(below, primitives(below), 2), edge, f)
        g_out = face(edge, f, above, flux(above, primitives(above), 2))
        f = flux(edge, prim, 3)
        second_flux = flux(second, primitives(second), 3)
        if side == 0:
            swirl = [geo.inv_h * x for x in face(edge, f, second, second_flux)]
        else:
            swirl = [-geo.inv_h * x for x in face(second, second_flux, edge, f)]
        part = advance(
            edge,
            prim,
            source,
            axial_difference(edge, prim, lane),
            [above_scale * g_out[v] - below_scale * g_in[v] for v in ALL],
            swirl,
            geo.inv_r,
            geo.inv_h,
            geo.spin_r,
            None,
        )
        for v in ALL:
            edges_ref[v, side, 0:16] = edge[v]
            edges_ref[v, side, 16:32] = part[v]


def pack_kernel(table, q_ref, edges_ref, rad_ref, own_ref, core_ref, other_ref):
    odd = lax.axis_index("theta") % 2 == 1
    band = lax.axis_index("rad")
    low = band == 0
    edge_at = edge_row(band, BAND - 1, 0)
    below_coefs, above_coefs = coefficients(low, table, 0), coefficients(low, table, BAND - 1)
    edge = [q_ref[v, edge_at] for v in ALL]
    near = [rad_ref[v] for v in ALL]
    edge_prim, near_prim = primitives(edge), primitives(near)
    (fe, se), (fn, sn) = flux(edge, edge_prim, 2), flux(near, near_prim, 2)
    fastest = jnp.where(low, np.float32(1.0), np.float32(-1.0)) * jnp.maximum(se, sn)
    _, weight = step_weight(edge_prim, jnp.where(low, above_coefs[2], below_coefs[2]))
    scale = jnp.where(low, -above_coefs[0], below_coefs[1]) * weight
    change = [scale * ((fe[v] + fn[v]) - fastest * (near[v] - edge[v])) for v in ALL]
    here = lax.broadcasted_iota(jnp.int32, (BAND, AXIAL), 0) == edge_at
    for v in ALL:
        for side in (0, 1):
            at = 0 if side == 0 else SECTOR - 1
            own_ref[v, side] = edges_ref[v, side, 16:32] + jnp.where(here, change[v][at : at + 1], 0.0)
        for ref, flip in ((core_ref, jnp.logical_not(odd)), (other_ref, odd)):
            at = 32 * v
            ref[at : at + 16] = jnp.where(flip, edges_ref[v, 1, 0:16], edges_ref[v, 0, 0:16])
            ref[at + 16 : at + 32] = jnp.where(flip, own_ref[v, 1], own_ref[v, 0])
            ref[160 + v : 161 + v] = jnp.where(flip, near[v][SECTOR - 1 : SECTOR], near[v][0:1])


def masks():
    return (
        lax.broadcasted_iota(jnp.int32, (SECTOR, HALF), 1),
        lax.broadcasted_iota(jnp.int32, (SECTOR, AXIAL), 0),
    )


def row_step(coefs, q, prim, source, g_in, g_out, ends, masks, blade):
    lane, sub = masks
    a_out, a_in, inv_h, inv_r, spin_r = coefs
    f, speed = flux(q, prim, 3)
    ahead = lambda x: pltpu.roll(x, SECTOR - 1, 0)
    qn = [ahead(x) for x in q]
    fn = [qn[3]] + [ahead(f[v]) for v in range(1, 5)]
    between = face(q, (f, speed), qn, (fn, ahead(speed)))
    swirl = []
    for v in ALL:
        first, last = (0.0, 0.0) if ends is None else ends[v]
        right = jnp.where(sub == SECTOR - 1, last, between[v])
        left = jnp.where(sub == 0, first, pltpu.roll(between[v], 1, 0))
        swirl.append(inv_h * (right - left))
    radial = [a_out * g_out[v] - a_in * g_in[v] for v in ALL]
    return advance(q, prim, source, axial_difference(q, prim, lane), radial, swirl, inv_r, inv_h, spin_r, blade)


def column_rows(ref, v, j):
    return [ref[v, 2 * side + j // SECTOR, j % SECTOR : j % SECTOR + 1, :] for side in (0, 1)]


def sweep(load, step, store):
    below, q = load(-1), load(0)
    prim = primitives(q)
    g_in = face(below, flux(below, primitives(below), 2), q, flux(q, prim, 2))
    for j in range(BAND):
        above = load(j + 1)
        above_prim = primitives(above)
        g_out = face(q, flux(q, prim, 2), above, flux(above, above_prim, 2))
        store(j, step(j, q, prim, g_in, g_out))
        q, prim, g_in = above, above_prim, g_out


def next_kernel(table, blade_ref, q_ref, qp_ref, rad_ref, next_ref):
    band = lax.axis_index("rad")
    low = band == 0
    edge_at = edge_row(band, BAND - 1, 0)
    edge = [q_ref[v, edge_at] for v in ALL]
    inner = [q_ref[v, edge_row(band, BAND - 2, 1)] for v in ALL]
    near = [rad_ref[v] for v in ALL]
    prim = primitives(edge)
    f = flux(edge, prim, 2)
    below = [jnp.where(low, inner[v], near[v]) for v in ALL]
    above = [jnp.where(low, near[v], inner[v]) for v in ALL]
    g_in = face(below, flux(below, primitives(below), 2), edge, f)
    g_out = face(edge, f, above, flux(above, primitives(above), 2))
    source = [40.0 * edge[v] - 10.0 * qp_ref[v, edge_at] for v in ALL]
    coefs = [jnp.where(low, a, b) for a, b in zip(coefficients(low, table, BAND - 1), coefficients(low, table, 0))]
    stepped = row_step(coefs, edge, prim, source, g_in, g_out, None, masks(), blades(blade_ref, SECTOR))
    for v in ALL:
        next_ref[v] = stepped[v]


def early_kernel(table, blade_ref, q_ref, qp_ref, rad_ref, p1_ref, source_ref):
    low = lax.axis_index("rad") == 0
    mask = masks()
    blade = blades(blade_ref, SECTOR)

    def load(j):
        if j < 0:
            return [jnp.where(low, MIRROR[v] * q_ref[v, 0], rad_ref[v]) for v in ALL]
        if j == BAND:
            return [jnp.where(low, rad_ref[v], MIRROR[v] * q_ref[v, BAND - 1]) for v in ALL]
        return [q_ref[v, j] for v in ALL]

    def step(j, q, prim, g_in, g_out):
        source = [40.0 * q[v] - 10.0 * qp_ref[v, j] for v in ALL]
        for v in ALL:
            source_ref[v, j] = source[v]
        return row_step(coefficients(low, table, j), q, prim, source, g_in, g_out, None, mask, blade)

    def store(j, q):
        for v in ALL:
            p1_ref[v, j] = q[v]

    sweep(load, step, store)


def final_kernel(
    total_rows,
    circle,
    table,
    blade_ref,
    edges_ref,
    own_ref,
    rad_ref,
    p1_ref,
    source_ref,
    next_ref,
    other_ref,
    core_ref,
    flow_ref,
    send_ref,
    own_rows,
    nearby,
    ends,
    fields,
):
    odd = lax.axis_index("theta") % 2 == 1
    band = lax.axis_index("rad")
    low = band == 0
    mask = masks()
    blade = blades(blade_ref, SECTOR)
    for v in ALL:
        nearby[v] = next_ref[v]

    geo = Columns(band * BAND, total_rows, circle)
    column_blade = blades(blade_ref, BAND)
    near_inv_h = jnp.where(low, coefficients(low, table, BAND)[2], coefficients(low, table, -1)[2])

    for side in (0, 1):
        use_core = odd if side == 0 else jnp.logical_not(odd)
        at = 0 if side == 0 else SECTOR - 1
        sign = 1.0 if side == 0 else -1.0

        def pick(first, step, count):
            spans = [slice(first + step * v, first + step * v + count) for v in ALL]
            return [jnp.where(use_core, core_ref[span], other_ref[span]) for span in spans]

        def ordered(halo, halo_prim, own, own_prim):
            a, b = flux(halo, halo_prim, 3), flux(own, own_prim, 3)
            return face(halo, a, own, b) if side == 0 else face(own, b, halo, a)

        near, near_part, corner = pick(0, 32, 16), pick(16, 32, 16), pick(160, 1, 1)
        own = [edges_ref[v, side, 0:16] for v in ALL]
        own_prim, near_prim = primitives(own), primitives(near)
        shared = ordered(near, near_prim, own, own_prim)
        own_part = [own_ref[v, side] for v in ALL]
        own_next, near_next = [], []
        for q, prim, part, scale, out in (
            (own, own_prim, own_part, sign * geo.inv_h, own_next),
            (near, near_prim, near_part, -sign * geo.inv_h, near_next),
        ):
            force = blade_force(q, geo.spin_r, column_blade)
            change = [scale * x for x in shared]
            change[3] = change[3] - force
            change[4] = change[4] - prim[2] * force
            weight = step_weight(prim, geo.inv_h)[1]
            out.extend(part[v] + weight * change[v] for v in ALL)

        edge = [rad_ref[v, at : at + 1, :] for v in ALL]
        edge_prim = primitives(edge)
        corner_face = ordered(corner, primitives(corner), edge, edge_prim)
        corner_scale = (sign * near_inv_h) * step_weight(edge_prim, near_inv_h)[1]

        faces = ordered(near_next, primitives(near_next), own_next, primitives(own_next))
        for v in ALL:
            own_rows[v, 2 * side : 2 * side + 2] = own_next[v].reshape(2, SECTOR, AXIAL)
            nearby[v, at : at + 1, :] = next_ref[v, at : at + 1, :] + corner_scale * corner_face[v]
            ends[v, 2 * side : 2 * side + 2] = faces[v].reshape(2, SECTOR, AXIAL)

    sub = mask[1]

    def row(v, j):
        first, last = column_rows(own_rows, v, j)
        return jnp.where(sub == 0, first, jnp.where(sub == SECTOR - 1, last, p1_ref[v, j]))

    def load(j):
        if j < 0:
            return [jnp.where(low, MIRROR[v] * row(v, 0), nearby[v]) for v in ALL]
        if j == BAND:
            return [jnp.where(low, nearby[v], MIRROR[v] * row(v, BAND - 1)) for v in ALL]
        return [row(v, j) for v in ALL]

    def step(j, q, prim, g_in, g_out):
        source, end = [source_ref[v, j] for v in ALL], [column_rows(ends, v, j) for v in ALL]
        return row_step(coefficients(low, table, j), q, prim, source, g_in, g_out, end, mask, blade)

    def store(j, q):
        for v in ALL:
            flow_ref[v, j] = q[v]
        ux, _, _, pressure, _ = primitives(q)
        fields[j // HALF_BAND, 0, j % HALF_BAND] = pressure
        fields[j // HALF_BAND, 1, j % HALF_BAND] = ux
        if j % HALF_BAND == HALF_BAND - 1:
            half = j // HALF_BAND
            send_ref[pl.ds(half, AXIAL, stride=2), :] = fields[half].reshape(BAND * SECTOR, AXIAL).T

    sweep(load, step, store)


def write_kernel(flow_ref, out_ref, sem):
    copy = pltpu.make_async_copy(flow_ref, out_ref, sem)
    copy.start()
    copy.wait()


def mode_kernel(mine, got_ref, basis_ref, out_ref, turned):
    chips = got_ref.shape[0] // 8
    core = lax.axis_index("theta") % 2
    first = 4 * (core if mine else 1 - core)
    left = lax.broadcasted_iota(jnp.int32, (BAND, 2 * chips), 1) < chips
    parts = []
    for n in range(4):
        cells = got_ref[pl.ds(first + n, chips, stride=8), :]
        turned[n] = jnp.concatenate([cells, cells], axis=0).T
        rows = [turned[n, pl.ds(m, BAND, stride=SECTOR), :] for m in range(SECTOR)]
        parts.append(
            jnp.concatenate([jnp.where(left, rows[m], rows[m + 1]) for m in range(0, SECTOR, 2)], axis=1)
        )
    out_ref[...] = jnp.dot(
        jnp.concatenate(parts, axis=0), basis_ref[core], precision=lax.Precision.HIGHEST, preferred_element_type=F32
    )


def sum_kernel(keep_ref, got_ref, out_ref):
    total = keep_ref[...] + got_ref[...]
    for e in (0, 1):
        for half in (0, 1):
            for f in (0, 1):
                at = (2 * e + half) * BAND + f * HALF_BAND
                rows = slice(half * HALF_BAND, (half + 1) * HALF_BAND)
                out_ref[e, rows, 2 * MODES * f : 2 * MODES * (f + 1)] = total[at : at + HALF_BAND]


def mode_basis(sectors):
    circle = sectors * SECTOR
    sector = 2 * np.arange(sectors // 2)[None, None, :] + np.arange(2)[:, None, None]
    cell = (np.arange(SECTOR)[None, :, None] + SECTOR * sector).reshape(2, -1)
    phase = (cell[:, :, None] * np.arange(1, MODES + 1) % circle) * (2.0 * np.pi / circle)
    return (np.concatenate([np.cos(phase), -np.sin(phase)], axis=2) / np.sqrt(circle)).astype(np.float32)


def shaped(*shape):
    return jax.ShapeDtypeStruct(shape, F32)


def vmem():
    return pl.BlockSpec(memory_space=pltpu.VMEM)


def limit(mib):
    return pltpu.CompilerParams(vmem_limit_bytes=int(mib * 2**20))


def per_device(q_level, q_prev, blade_row):
    sectors = lax.axis_size("theta")
    bands = lax.axis_size("rad")
    circle = sectors * SECTOR
    core = [(t, t ^ 1) for t in range(sectors)]
    other = [(t, (((t + 1) ^ 1) - 1) % sectors) for t in range(sectors)]
    table = geometry_table(bands * BAND, circle)
    blade = blade_row.reshape(1, AXIAL)

    hbm = pl.BlockSpec(memory_space=pltpu.HBM)
    swap = [(0, 1), (1, 0)]

    def edges(*refs):
        edge_kernel(bands * BAND, circle, *refs)

    def pack(*refs):
        pack_kernel(table, *refs)

    def neighbour(*refs):
        next_kernel(table, *refs)

    def early(*refs):
        early_kernel(table, *refs)

    def final(*refs):
        final_kernel(bands * BAND, circle, table, *refs)

    near = pl.pallas_call(
        rad_kernel,
        out_shape=shaped(5, SECTOR, AXIAL),
        in_specs=[hbm],
        out_specs=vmem(),
        scratch_shapes=[pltpu.SemaphoreType.DMA],
        compiler_params=pltpu.CompilerParams(vmem_limit_bytes=RAD_VMEM),
    )(q_level)
    rad_in = lax.ppermute(near, "rad", swap)
    q_level, q_prev = pl.pallas_call(
        load_kernel,
        out_shape=[shaped(5, BAND, SECTOR, AXIAL)] * 2,
        in_specs=[hbm] * 2,
        out_specs=[vmem()] * 2,
        scratch_shapes=[pltpu.SemaphoreType.DMA((2,))],
        compiler_params=pltpu.CompilerParams(vmem_limit_bytes=LOAD_VMEM),
        cost_estimate=pl.CostEstimate(flops=0, bytes_accessed=3_000_000, transcendentals=0),
    )(q_level, q_prev)
    edge_columns = pl.pallas_call(
        edges,
        out_shape=shaped(5, 2, 32, AXIAL),
        in_specs=[vmem()] * 2,
        out_specs=vmem(),
        scratch_shapes=[pltpu.VMEM((5, 2, 32, AXIAL), F32), pltpu.VMEM((5, 2, 2, BAND, AXIAL), F32)],
        compiler_params=limit(4),
        cost_estimate=pl.CostEstimate(flops=5_000_000, bytes_accessed=2_000_000, transcendentals=50_000),
    )(q_level, q_prev)
    own_columns, core_out, other_out = pl.pallas_call(
        pack,
        out_shape=[shaped(5, 2, BAND, AXIAL)] + [shaped(168, AXIAL)] * 2,
        in_specs=[vmem()] * 3,
        out_specs=[vmem()] * 3,
        compiler_params=limit(4),
    )(q_level, edge_columns, rad_in)
    core_in = lax.ppermute(core_out, "theta", core)
    other_in = lax.ppermute(other_out, "theta", other)
    next_out = pl.pallas_call(
        neighbour,
        out_shape=shaped(5, SECTOR, AXIAL),
        in_specs=[vmem()] * 4,
        out_specs=vmem(),
        compiler_params=limit(4),
    )(blade, q_level, q_prev, rad_in)
    next_in = lax.ppermute(next_out, "rad", swap)
    part, source = pl.pallas_call(
        early,
        out_shape=[shaped(5, BAND, SECTOR, AXIAL)] * 2,
        in_specs=[vmem()] * 4,
        out_specs=[vmem()] * 2,
        compiler_params=limit(8),
        cost_estimate=pl.CostEstimate(flops=10_000_000, bytes_accessed=3_500_000, transcendentals=100_000),
    )(blade, q_level, q_prev, rad_in)
    flow_state, send = pl.pallas_call(
        final,
        out_shape=[shaped(5, BAND, SECTOR, AXIAL), shaped(2 * AXIAL, BAND * SECTOR)],
        in_specs=[vmem()] * 9,
        out_specs=[vmem()] * 2,
        scratch_shapes=[
            pltpu.VMEM((5, 4, SECTOR, AXIAL), F32),
            pltpu.VMEM((5, SECTOR, AXIAL), F32),
            pltpu.VMEM((5, 4, SECTOR, AXIAL), F32),
            pltpu.VMEM((2, 2, HALF_BAND, SECTOR, AXIAL), F32),
        ],
        compiler_params=limit(8),
    )(blade, edge_columns, own_columns, rad_in, part, source, next_in, other_in, core_in)
    chips = sectors // 2
    got = lax.all_to_all(
        send.reshape(chips, 8, 128),
        "theta",
        split_axis=0,
        concat_axis=0,
        tiled=True,
        axis_index_groups=[[2 * chip + c for chip in range(chips)] for c in (0, 1)],
    )
    got = got.reshape(8 * chips, 128)
    basis = jnp.asarray(mode_basis(sectors))

    def modes(mine):
        def kernel(*refs):
            mode_kernel(mine, *refs)

        return pl.pallas_call(
            kernel,
            out_shape=shaped(4 * BAND, 2 * MODES),
            in_specs=[vmem()] * 2,
            out_specs=vmem(),
            scratch_shapes=[pltpu.VMEM((4, BAND * SECTOR, 2 * chips), F32)],
            compiler_params=limit(4),
            cost_estimate=pl.CostEstimate(flops=20_000_000, bytes_accessed=800_000, transcendentals=0),
        )(got, basis)

    given = lax.ppermute(modes(False), "theta", core)
    keep = modes(True)
    flow_state = pl.pallas_call(
        write_kernel,
        out_shape=shaped(5, BAND, SECTOR, AXIAL),
        in_specs=[vmem()],
        out_specs=hbm,
        scratch_shapes=[pltpu.SemaphoreType.DMA],
        compiler_params=limit(2),
        cost_estimate=pl.CostEstimate(flops=0, bytes_accessed=1_400_000, transcendentals=0),
    )(flow_state)
    spectra = pl.pallas_call(
        sum_kernel,
        out_shape=shaped(2, BAND, 4 * MODES),
        in_specs=[vmem()] * 2,
        out_specs=vmem(),
        compiler_params=limit(2),
    )(keep, given)
    return flow_state, spectra


def solution(mesh):
    in_specs = (P(None, "rad", "theta", None), P(None, "rad", "theta", None), P())
    out_specs = (P(None, "rad", "theta", None), P("theta", "rad", None))
    return jax.shard_map(per_device, mesh=mesh, in_specs=in_specs, out_specs=out_specs, check_vma=False)
```

```python
import math

import jax
import jax.numpy as jnp
import numpy as np
from jax import lax
from jax.experimental import pallas as pl
from jax.experimental.pallas import tpu as pltpu
from jax.sharding import PartitionSpec as P

MODES = 64
GAMMA = 1.4
KAPPA = 2.0

BAND = 16
HALF_BAND = BAND // 2
SECTOR = 8
AXIAL = 256
RAD_VMEM = 56_200_000
LOAD_VMEM = 55_000_000
F32 = jnp.float32
ALL = range(5)


def primitives(q):
    inverse = 1.0 / q[0]
    ux, ur, ut = q[1] * inverse, q[2] * inverse, q[3] * inverse
    pressure = (GAMMA - 1.0) * (q[4] - 0.5 * (q[1] * ux + q[2] * ur + q[3] * ut))
    sound = jnp.sqrt(GAMMA * pressure * inverse)
    return ux, ur, ut, pressure, sound


def flux(q, prim, d):
    u, pressure = prim[d - 1], prim[3]
    f = [q[d], q[1] * u, q[2] * u, q[3] * u, (q[4] + pressure) * u]
    f[d] = f[d] + pressure
    return f, jnp.abs(u) + prim[4]


def face(left_q, left_flux, right_q, right_flux):
    (fl, sl), (fr, sr) = left_flux, right_flux
    fastest = jnp.maximum(sl, sr)
    return [(fl[v] + fr[v]) - fastest * (right_q[v] - left_q[v]) for v in ALL]


HALF = AXIAL // 2


def axial_neighbour(x, lane, step, end):
    low, high = x[:, :HALF], x[:, HALF:]
    turned_low, turned_high = pltpu.roll(low, -step % HALF, 1), pltpu.roll(high, -step % HALF, 1)
    if step == 1:
        seam = lane == HALF - 1
        parts = [jnp.where(seam, turned_high, turned_low), jnp.where(seam, end, turned_high)]
    else:
        seam = lane == 0
        parts = [jnp.where(seam, end, turned_low), jnp.where(seam, turned_low, turned_high)]
    return jnp.concatenate(parts, axis=1)


def axial_difference(q, prim, lane):
    f, speed = flux(q, prim, 1)

    def following(x):
        return axial_neighbour(x, lane, 1, x[:, HALF:])

    qn = [following(x) for x in q]
    fn = [qn[1]] + [following(f[v]) for v in range(1, 5)]
    right = face(q, (f, speed), qn, (fn, following(speed)))
    return [x - axial_neighbour(x, lane, -1, 2.0 * f[v][:, :HALF]) for v, x in enumerate(right)]


def step_weight(prim, inv_h):
    ux, ur, ut, _, sound = prim
    rate = 4.0 * (jnp.abs(ux) + jnp.abs(ur)) + jnp.abs(ut) * (4.0 * inv_h) + sound * (8.0 + 4.0 * inv_h)
    return rate, 1.0 / (rate + 30.0)


def blade_force(q, spin_r, blade):
    bladed, rotor = blade
    return bladed * (q[3] - (rotor * spin_r) * q[0])


def advance(q, prim, source, axial, radial, swirl, inv_r, inv_h, spin_r, blade):
    ux, ur, ut, pressure, sound = prim
    twice_r = 2.0 * inv_r
    rate, weight = step_weight(prim, inv_h)
    gains = [None, None, twice_r * (q[3] * ut + pressure), -twice_r * (q[2] * ut), None]
    if blade is not None:
        force = blade_force(q, spin_r, blade)
        gains[3] = gains[3] - force
        gains[4] = -ut * force
    out = []
    for v in ALL:
        total = source[v] - axial[v] - radial[v] - swirl[v]
        if gains[v] is not None:
            total = total + gains[v]
        out.append((rate * q[v] + total) * weight)
    return out


def geometry_table(rows, circle):
    mean = circle / (2.0 * math.pi)
    row = np.arange(rows, dtype=np.float64)
    radius = mean * (0.8 + 0.4 * (row + 0.5) / rows)
    inner = mean * (0.8 + 0.4 * row / rows)
    outer = mean * (0.8 + 0.4 * (row + 1.0) / rows)
    spacing = radius * (2.0 * math.pi / circle)
    return np.stack([outer / radius, inner / radius, 1.0 / spacing, 1.0 / radius, radius / (1.2 * mean)])


def coefficients(low, table, j):
    last = table.shape[1] - 1
    at = [min(max(j + first, 0), last) for first in (0, BAND)]
    return [jnp.where(low, np.float32(row[at[0]]), np.float32(row[at[1]])) for row in table]


def edge_row(band, at_low, at_high):
    return jnp.where(band == 0, at_low, at_high)


MIRROR = (1.0, 1.0, -1.0, 1.0, 1.0)


def blades(blade_ref, rows):
    blade = blade_ref[...]
    bladed = jnp.broadcast_to(4.0 * (blade > 0).astype(F32), (rows, AXIAL))
    rotor = jnp.broadcast_to((blade == 1).astype(F32), (rows, AXIAL))
    return bladed, rotor


def rad_kernel(q_ref, near_ref, sem):
    copy = pltpu.make_async_copy(q_ref.at[:, edge_row(lax.axis_index("rad"), BAND - 1, 0)], near_ref, sem)
    copy.start()
    copy.wait()


def load_kernel(q_ref, qp_ref, q_out_ref, qp_out_ref, sems):
    copies = [
        pltpu.make_async_copy(q_ref, q_out_ref, sems.at[0]),
        pltpu.make_async_copy(qp_ref, qp_out_ref, sems.at[1]),
    ]
    for copy in copies:
        copy.start()
    for copy in copies:
        copy.wait()


class Columns:
    def __init__(self, first_row, total_rows, circle):
        rows = (lax.broadcasted_iota(jnp.int32, (BAND, AXIAL), 0) + first_row).astype(F32)
        mean = circle / (2.0 * math.pi)
        radius = mean * (0.8 + 0.4 * (rows + 0.5) / total_rows)
        self.inner = mean * (0.8 + 0.4 * rows / total_rows)
        self.outer = mean * (0.8 + 0.4 * (rows + 1.0) / total_rows)
        self.inv_r = 1.0 / radius
        self.inv_h = self.inv_r * mean
        self.spin_r = radius * (1.0 / (1.2 * mean))
        self.a_h = 0.25 * self.inv_h


def edge_kernel(total_rows, circle, q_ref, qp_ref, edges_ref, ce, taken):
    band = lax.axis_index("rad")
    low = band == 0
    geo = Columns(band * BAND, total_rows, circle)
    lane = lax.broadcasted_iota(jnp.int32, (BAND, HALF), 1)
    row = lax.broadcasted_iota(jnp.int32, (BAND, AXIAL), 0)
    below_scale = jnp.where((row == 0) & jnp.logical_not(low), 0.0, geo.inv_r * geo.inner)
    above_scale = jnp.where((row == BAND - 1) & low, 0.0, geo.inv_r * geo.outer)
    for side in (0, 1):
        at, inner = (0, 1) if side == 0 else (SECTOR - 1, SECTOR - 2)
        for v in ALL:
            ce[v, side, 8:24] = q_ref[v, :, at, :]
            taken[v, side, 0] = q_ref[v, :, inner, :]
            taken[v, side, 1] = qp_ref[v, :, at, :]
    for side in (0, 1):
        edge = [ce[v, side, 8:24] for v in ALL]
        second = [taken[v, side, 0] for v in ALL]
        source = [40.0 * edge[v] - 10.0 * taken[v, side, 1] for v in ALL]
        for v in ALL:
            ce[v, side, 7:8] = MIRROR[v] * edge[v][0:1]
            ce[v, side, 24:25] = MIRROR[v] * edge[v][BAND - 1 : BAND]
        below = [ce[v, side, 7:23] for v in ALL]
        above = [ce[v, side, 9:25] for v in ALL]
        prim = primitives(edge)
        f = flux(edge, prim, 2)
        g_in = face(below, flux(below, primitives(below), 2), edge, f)
        g_out = face(edge, f, above, flux(above, primitives(above), 2))
        f = flux(edge, prim, 3)
        second_flux = flux(second, primitives(second), 3)
        if side == 0:
            swirl = [geo.inv_h * x for x in face(edge, f, second, second_flux)]
        else:
            swirl = [-geo.inv_h * x for x in face(second, second_flux, edge, f)]
        part = advance(
            edge,
            prim,
            source,
            axial_difference(edge, prim, lane),
            [above_scale * g_out[v] - below_scale * g_in[v] for v in ALL],
            swirl,
            geo.inv_r,
            geo.inv_h,
            geo.spin_r,
            None,
        )
        for v in ALL:
            edges_ref[v, side, 0:16] = edge[v]
            edges_ref[v, side, 16:32] = part[v]


def pack_kernel(table, q_ref, edges_ref, rad_ref, own_ref, core_ref, other_ref):
    odd = lax.axis_index("theta") % 2 == 1
    band = lax.axis_index("rad")
    low = band == 0
    edge_at = edge_row(band, BAND - 1, 0)
    below_coefs, above_coefs = coefficients(low, table, 0), coefficients(low, table, BAND - 1)
    edge = [q_ref[v, edge_at] for v in ALL]
    near = [rad_ref[v] for v in ALL]
    edge_prim, near_prim = primitives(edge), primitives(near)
    (fe, se), (fn, sn) = flux(edge, edge_prim, 2), flux(near, near_prim, 2)
    fastest = jnp.where(low, np.float32(1.0), np.float32(-1.0)) * jnp.maximum(se, sn)
    _, weight = step_weight(edge_prim, jnp.where(low, above_coefs[2], below_coefs[2]))
    scale = jnp.where(low, -above_coefs[0], below_coefs[1]) * weight
    change = [scale * ((fe[v] + fn[v]) - fastest * (near[v] - edge[v])) for v in ALL]
    here = lax.broadcasted_iota(jnp.int32, (BAND, AXIAL), 0) == edge_at
    for v in ALL:
        for side in (0, 1):
            at = 0 if side == 0 else SECTOR - 1
            own_ref[v, side] = edges_ref[v, side, 16:32] + jnp.where(here, change[v][at : at + 1], 0.0)
        for ref, flip in ((core_ref, jnp.logical_not(odd)), (other_ref, odd)):
            at = 32 * v
            ref[at : at + 16] = jnp.where(flip, edges_ref[v, 1, 0:16], edges_ref[v, 0, 0:16])
            ref[at + 16 : at + 32] = jnp.where(flip, own_ref[v, 1], own_ref[v, 0])
            ref[160 + v : 161 + v] = jnp.where(flip, near[v][SECTOR - 1 : SECTOR], near[v][0:1])


def masks():
    return (
        lax.broadcasted_iota(jnp.int32, (SECTOR, HALF), 1),
        lax.broadcasted_iota(jnp.int32, (SECTOR, AXIAL), 0),
    )


def row_step(coefs, q, prim, source, g_in, g_out, ends, masks, blade):
    lane, sub = masks
    a_out, a_in, inv_h, inv_r, spin_r = coefs
    f, speed = flux(q, prim, 3)
    ahead = lambda x: pltpu.roll(x, SECTOR - 1, 0)
    qn = [ahead(x) for x in q]
    fn = [qn[3]] + [ahead(f[v]) for v in range(1, 5)]
    between = face(q, (f, speed), qn, (fn, ahead(speed)))
    swirl = []
    for v in ALL:
        first, last = (0.0, 0.0) if ends is None else ends[v]
        right = jnp.where(sub == SECTOR - 1, last, between[v])
        left = jnp.where(sub == 0, first, pltpu.roll(between[v], 1, 0))
        swirl.append(inv_h * (right - left))
    radial = [a_out * g_out[v] - a_in * g_in[v] for v in ALL]
    return advance(q, prim, source, axial_difference(q, prim, lane), radial, swirl, inv_r, inv_h, spin_r, blade)


def column_rows(ref, v, j):
    return [ref[v, 2 * side + j // SECTOR, j % SECTOR : j % SECTOR + 1, :] for side in (0, 1)]


def sweep(load, step, store):
    below, q = load(-1), load(0)
    prim = primitives(q)
    g_in = face(below, flux(below, primitives(below), 2), q, flux(q, prim, 2))
    for j in range(BAND):
        above = load(j + 1)
        above_prim = primitives(above)
        g_out = face(q, flux(q, prim, 2), above, flux(above, above_prim, 2))
        store(j, step(j, q, prim, g_in, g_out))
        q, prim, g_in = above, above_prim, g_out


def next_kernel(table, blade_ref, q_ref, qp_ref, rad_ref, next_ref):
    band = lax.axis_index("rad")
    low = band == 0
    edge_at = edge_row(band, BAND - 1, 0)
    edge = [q_ref[v, edge_at] for v in ALL]
    inner = [q_ref[v, edge_row(band, BAND - 2, 1)] for v in ALL]
    near = [rad_ref[v] for v in ALL]
    prim = primitives(edge)
    f = flux(edge, prim, 2)
    below = [jnp.where(low, inner[v], near[v]) for v in ALL]
    above = [jnp.where(low, near[v], inner[v]) for v in ALL]
    g_in = face(below, flux(below, primitives(below), 2), edge, f)
    g_out = face(edge, f, above, flux(above, primitives(above), 2))
    source = [40.0 * edge[v] - 10.0 * qp_ref[v, edge_at] for v in ALL]
    coefs = [jnp.where(low, a, b) for a, b in zip(coefficients(low, table, BAND - 1), coefficients(low, table, 0))]
    stepped = row_step(coefs, edge, prim, source, g_in, g_out, None, masks(), blades(blade_ref, SECTOR))
    for v in ALL:
        next_ref[v] = stepped[v]


def early_kernel(table, blade_ref, q_ref, qp_ref, rad_ref, p1_ref, source_ref):
    low = lax.axis_index("rad") == 0
    mask = masks()
    blade = blades(blade_ref, SECTOR)

    def load(j):
        if j < 0:
            return [jnp.where(low, MIRROR[v] * q_ref[v, 0], rad_ref[v]) for v in ALL]
        if j == BAND:
            return [jnp.where(low, rad_ref[v], MIRROR[v] * q_ref[v, BAND - 1]) for v in ALL]
        return [q_ref[v, j] for v in ALL]

    def step(j, q, prim, g_in, g_out):
        source = [40.0 * q[v] - 10.0 * qp_ref[v, j] for v in ALL]
        for v in ALL:
            source_ref[v, j] = source[v]
        return row_step(coefficients(low, table, j), q, prim, source, g_in, g_out, None, mask, blade)

    def store(j, q):
        for v in ALL:
            p1_ref[v, j] = q[v]

    sweep(load, step, store)


def final_kernel(
    total_rows,
    circle,
    table,
    blade_ref,
    edges_ref,
    own_ref,
    rad_ref,
    p1_ref,
    source_ref,
    next_ref,
    other_ref,
    core_ref,
    flow_ref,
    send_ref,
    own_rows,
    nearby,
    ends,
    fields,
):
    odd = lax.axis_index("theta") % 2 == 1
    band = lax.axis_index("rad")
    low = band == 0
    mask = masks()
    blade = blades(blade_ref, SECTOR)
    for v in ALL:
        nearby[v] = next_ref[v]

    geo = Columns(band * BAND, total_rows, circle)
    column_blade = blades(blade_ref, BAND)
    near_inv_h = jnp.where(low, coefficients(low, table, BAND)[2], coefficients(low, table, -1)[2])

    for side in (0, 1):
        use_core = odd if side == 0 else jnp.logical_not(odd)
        at = 0 if side == 0 else SECTOR - 1
        sign = 1.0 if side == 0 else -1.0

        def pick(first, step, count):
            spans = [slice(first + step * v, first + step * v + count) for v in ALL]
            return [jnp.where(use_core, core_ref[span], other_ref[span]) for span in spans]

        def ordered(halo, halo_prim, own, own_prim):
            a, b = flux(halo, halo_prim, 3), flux(own, own_prim, 3)
            return face(halo, a, own, b) if side == 0 else face(own, b, halo, a)

        near, near_part, corner = pick(0, 32, 16), pick(16, 32, 16), pick(160, 1, 1)
        own = [edges_ref[v, side, 0:16] for v in ALL]
        own_prim, near_prim = primitives(own), primitives(near)
        shared = ordered(near, near_prim, own, own_prim)
        own_part = [own_ref[v, side] for v in ALL]
        own_next, near_next = [], []
        for q, prim, part, scale, out in (
            (own, own_prim, own_part, sign * geo.inv_h, own_next),
            (near, near_prim, near_part, -sign * geo.inv_h, near_next),
        ):
            force = blade_force(q, geo.spin_r, column_blade)
            change = [scale * x for x in shared]
            change[3] = change[3] - force
            change[4] = change[4] - prim[2] * force
            weight = step_weight(prim, geo.inv_h)[1]
            out.extend(part[v] + weight * change[v] for v in ALL)

        edge = [rad_ref[v, at : at + 1, :] for v in ALL]
        edge_prim = primitives(edge)
        corner_face = ordered(corner, primitives(corner), edge, edge_prim)
        corner_scale = (sign * near_inv_h) * step_weight(edge_prim, near_inv_h)[1]

        faces = ordered(near_next, primitives(near_next), own_next, primitives(own_next))
        for v in ALL:
            own_rows[v, 2 * side : 2 * side + 2] = own_next[v].reshape(2, SECTOR, AXIAL)
            nearby[v, at : at + 1, :] = next_ref[v, at : at + 1, :] + corner_scale * corner_face[v]
            ends[v, 2 * side : 2 * side + 2] = faces[v].reshape(2, SECTOR, AXIAL)

    sub = mask[1]

    def row(v, j):
        first, last = column_rows(own_rows, v, j)
        return jnp.where(sub == 0, first, jnp.where(sub == SECTOR - 1, last, p1_ref[v, j]))

    def load(j):
        if j < 0:
            return [jnp.where(low, MIRROR[v] * row(v, 0), nearby[v]) for v in ALL]
        if j == BAND:
            return [jnp.where(low, nearby[v], MIRROR[v] * row(v, BAND - 1)) for v in ALL]
        return [row(v, j) for v in ALL]

    def step(j, q, prim, g_in, g_out):
        source, end = [source_ref[v, j] for v in ALL], [column_rows(ends, v, j) for v in ALL]
        return row_step(coefficients(low, table, j), q, prim, source, g_in, g_out, end, mask, blade)

    def store(j, q):
        for v in ALL:
            flow_ref[v, j] = q[v]
        ux, _, _, pressure, _ = primitives(q)
        fields[j // HALF_BAND, 0, j % HALF_BAND] = pressure
        fields[j // HALF_BAND, 1, j % HALF_BAND] = ux
        if j % HALF_BAND == HALF_BAND - 1:
            half = j // HALF_BAND
            send_ref[pl.ds(half, AXIAL, stride=2), :] = fields[half].reshape(BAND * SECTOR, AXIAL).T

    sweep(load, step, store)


def mode_kernel(mine, got_ref, basis_ref, out_ref, turned):
    chips = got_ref.shape[0] // 8
    core = lax.axis_index("theta") % 2
    first = 4 * (core if mine else 1 - core)
    left = lax.broadcasted_iota(jnp.int32, (BAND, 2 * chips), 1) < chips
    parts = []
    for n in range(4):
        cells = got_ref[pl.ds(first + n, chips, stride=8), :]
        turned[n] = jnp.concatenate([cells, cells], axis=0).T
        rows = [turned[n, pl.ds(m, BAND, stride=SECTOR), :] for m in range(SECTOR)]
        parts.append(
            jnp.concatenate([jnp.where(left, rows[m], rows[m + 1]) for m in range(0, SECTOR, 2)], axis=1)
        )
    out_ref[...] = jnp.dot(
        jnp.concatenate(parts, axis=0), basis_ref[core], precision=lax.Precision.HIGHEST, preferred_element_type=F32
    )


def keep_kernel(got_ref, basis_ref, flow_ref, out_ref, flow_out_ref, turned, sem):
    copy = pltpu.make_async_copy(flow_ref, flow_out_ref, sem)
    copy.start()
    mode_kernel(True, got_ref, basis_ref, out_ref, turned)
    copy.wait()


def sum_kernel(keep_ref, got_ref, out_ref):
    total = keep_ref[...] + got_ref[...]
    for e in (0, 1):
        for half in (0, 1):
            for f in (0, 1):
                at = (2 * e + half) * BAND + f * HALF_BAND
                rows = slice(half * HALF_BAND, (half + 1) * HALF_BAND)
                out_ref[e, rows, 2 * MODES * f : 2 * MODES * (f + 1)] = total[at : at + HALF_BAND]


def mode_basis(sectors):
    circle = sectors * SECTOR
    sector = 2 * np.arange(sectors // 2)[None, None, :] + np.arange(2)[:, None, None]
    cell = (np.arange(SECTOR)[None, :, None] + SECTOR * sector).reshape(2, -1)
    phase = (cell[:, :, None] * np.arange(1, MODES + 1) % circle) * (2.0 * np.pi / circle)
    return (np.concatenate([np.cos(phase), -np.sin(phase)], axis=2) / np.sqrt(circle)).astype(np.float32)


def shaped(*shape):
    return jax.ShapeDtypeStruct(shape, F32)


def vmem():
    return pl.BlockSpec(memory_space=pltpu.VMEM)


def limit(mib):
    return pltpu.CompilerParams(vmem_limit_bytes=int(mib * 2**20))


def per_device(q_level, q_prev, blade_row):
    sectors = lax.axis_size("theta")
    bands = lax.axis_size("rad")
    circle = sectors * SECTOR
    core = [(t, t ^ 1) for t in range(sectors)]
    other = [(t, (((t + 1) ^ 1) - 1) % sectors) for t in range(sectors)]
    table = geometry_table(bands * BAND, circle)
    blade = blade_row.reshape(1, AXIAL)

    hbm = pl.BlockSpec(memory_space=pltpu.HBM)
    swap = [(0, 1), (1, 0)]

    def edges(*refs):
        edge_kernel(bands * BAND, circle, *refs)

    def pack(*refs):
        pack_kernel(table, *refs)

    def neighbour(*refs):
        next_kernel(table, *refs)

    def early(*refs):
        early_kernel(table, *refs)

    def final(*refs):
        final_kernel(bands * BAND, circle, table, *refs)

    near = pl.pallas_call(
        rad_kernel,
        out_shape=shaped(5, SECTOR, AXIAL),
        in_specs=[hbm],
        out_specs=vmem(),
        scratch_shapes=[pltpu.SemaphoreType.DMA],
        compiler_params=pltpu.CompilerParams(vmem_limit_bytes=RAD_VMEM),
    )(q_level)
    rad_in = lax.ppermute(near, "rad", swap)
    q_level, q_prev = pl.pallas_call(
        load_kernel,
        out_shape=[shaped(5, BAND, SECTOR, AXIAL)] * 2,
        in_specs=[hbm] * 2,
        out_specs=[vmem()] * 2,
        scratch_shapes=[pltpu.SemaphoreType.DMA((2,))],
        compiler_params=pltpu.CompilerParams(vmem_limit_bytes=LOAD_VMEM),
        cost_estimate=pl.CostEstimate(flops=0, bytes_accessed=3_000_000, transcendentals=0),
    )(q_level, q_prev)
    edge_columns = pl.pallas_call(
        edges,
        out_shape=shaped(5, 2, 32, AXIAL),
        in_specs=[vmem()] * 2,
        out_specs=vmem(),
        scratch_shapes=[pltpu.VMEM((5, 2, 32, AXIAL), F32), pltpu.VMEM((5, 2, 2, BAND, AXIAL), F32)],
        compiler_params=limit(4),
        cost_estimate=pl.CostEstimate(flops=5_000_000, bytes_accessed=2_000_000, transcendentals=50_000),
    )(q_level, q_prev)
    own_columns, core_out, other_out = pl.pallas_call(
        pack,
        out_shape=[shaped(5, 2, BAND, AXIAL)] + [shaped(168, AXIAL)] * 2,
        in_specs=[vmem()] * 3,
        out_specs=[vmem()] * 3,
        compiler_params=limit(4),
    )(q_level, edge_columns, rad_in)
    core_in = lax.ppermute(core_out, "theta", core)
    other_in = lax.ppermute(other_out, "theta", other)
    next_out = pl.pallas_call(
        neighbour,
        out_shape=shaped(5, SECTOR, AXIAL),
        in_specs=[vmem()] * 4,
        out_specs=vmem(),
        compiler_params=limit(4),
    )(blade, q_level, q_prev, rad_in)
    next_in = lax.ppermute(next_out, "rad", swap)
    part, source = pl.pallas_call(
        early,
        out_shape=[shaped(5, BAND, SECTOR, AXIAL)] * 2,
        in_specs=[vmem()] * 4,
        out_specs=[vmem()] * 2,
        compiler_params=limit(8),
        cost_estimate=pl.CostEstimate(flops=10_000_000, bytes_accessed=3_500_000, transcendentals=100_000),
    )(blade, q_level, q_prev, rad_in)
    flow_state, send = pl.pallas_call(
        final,
        out_shape=[shaped(5, BAND, SECTOR, AXIAL), shaped(2 * AXIAL, BAND * SECTOR)],
        in_specs=[vmem()] * 9,
        out_specs=[vmem()] * 2,
        scratch_shapes=[
            pltpu.VMEM((5, 4, SECTOR, AXIAL), F32),
            pltpu.VMEM((5, SECTOR, AXIAL), F32),
            pltpu.VMEM((5, 4, SECTOR, AXIAL), F32),
            pltpu.VMEM((2, 2, HALF_BAND, SECTOR, AXIAL), F32),
        ],
        compiler_params=limit(8),
    )(blade, edge_columns, own_columns, rad_in, part, source, next_in, other_in, core_in)
    chips = sectors // 2
    got = lax.all_to_all(
        send.reshape(chips, 8, 128),
        "theta",
        split_axis=0,
        concat_axis=0,
        tiled=True,
        axis_index_groups=[[2 * chip + c for chip in range(chips)] for c in (0, 1)],
    )
    got = got.reshape(8 * chips, 128)
    basis = jnp.asarray(mode_basis(sectors))

    def give_kernel(*refs):
        mode_kernel(False, *refs)

    turned = pltpu.VMEM((4, BAND * SECTOR, 2 * chips), F32)
    give = pl.pallas_call(
        give_kernel,
        out_shape=shaped(4 * BAND, 2 * MODES),
        in_specs=[vmem()] * 2,
        out_specs=vmem(),
        scratch_shapes=[turned],
        compiler_params=limit(4),
    )(got, basis)
    given = lax.ppermute(give, "theta", core)
    keep, flow_state = pl.pallas_call(
        keep_kernel,
        out_shape=[shaped(4 * BAND, 2 * MODES), shaped(5, BAND, SECTOR, AXIAL)],
        in_specs=[vmem()] * 3,
        out_specs=[vmem(), hbm],
        scratch_shapes=[turned, pltpu.SemaphoreType.DMA],
        compiler_params=limit(4),
        cost_estimate=pl.CostEstimate(flops=20_000_000, bytes_accessed=2_000_000, transcendentals=0),
    )(got, basis, flow_state)
    spectra = pl.pallas_call(
        sum_kernel,
        out_shape=shaped(2, BAND, 4 * MODES),
        in_specs=[vmem()] * 2,
        out_specs=vmem(),
        compiler_params=limit(2),
    )(keep, given)
    return flow_state, spectra


def solution(mesh):
    in_specs = (P(None, "rad", "theta", None), P(None, "rad", "theta", None), P())
    out_specs = (P(None, "rad", "theta", None), P("theta", "rad", None))
    return jax.shard_map(per_device, mesh=mesh, in_specs=in_specs, out_specs=out_specs, check_vma=False)
```
